32 devices in a mesh: dp: 8 (over z, x), fsdp: 4 (over y, core).
Axes of the slice: x: 2, y: 2, z: 4, core: 2. Of those that a mesh axis runs over, the one named last changes fastest.
Arguments:
- tokens: bfloat16 [4096, 768], P(('dp', 'fsdp')), may hold values from -6 to 6
- encoded: bfloat16 [131072, 768], P(('dp', 'fsdp')), may hold values from -6 to 6
- segment_ids: int32 [32, 128], P(('dp', 'fsdp')), may hold values from 0 to 3, never falling along the last dimension, each value on 1 to 64 neighbouring positions
- passage_group: int32 [32, 4], P(('dp', 'fsdp')), may hold values from 0 to 3, each once within a row
- cotangent: bfloat16 [4096, 768], P(('dp', 'fsdp')), may hold values from -6 to 6
- self_gain: bfloat16 [768], P(('dp', 'fsdp')), may hold values from 0.5 to 1.5
- cross_gain: bfloat16 [768], P(('dp', 'fsdp')), may hold values from 0.5 to 1.5
- ffn_gain: bfloat16 [768], P(('dp', 'fsdp')), may hold values from 0.5 to 1.5
- self_query: bfloat16 [768, 768], P(('dp', 'fsdp')), may hold values from -0.21875 to 0.21875
- self_key: bfloat16 [768, 768], P(('dp', 'fsdp')), may hold values from -0.21875 to 0.21875
- self_value: bfloat16 [768, 768], P(('dp', 'fsdp')), may hold values from -0.21875 to 0.21875
- self_out: bfloat16 [768, 768], P(('dp', 'fsdp')), may hold values from -0.625 to 0.625
- cross_query: bfloat16 [768, 768], P(('dp', 'fsdp')), may hold values from -0.21875 to 0.21875
- cross_key: bfloat16 [768, 768], P(('dp', 'fsdp')), may hold values from -0.21875 to 0.21875
- cross_value: bfloat16 [768, 768], P(('dp', 'fsdp')), may hold values from -0.21875 to 0.21875
- cross_out: bfloat16 [768, 768], P(('dp', 'fsdp')), may hold values from -6 to 6
- ffn_in: bfloat16 [768, 3072], P(('dp', 'fsdp')), may hold values from -0.21875 to 0.21875
- ffn_out: bfloat16 [3072, 768], P(('dp', 'fsdp')), may hold values from -0.21875 to 0.21875
Outputs:
- block_out: bfloat16 [4096, 768], P(('dp', 'fsdp'))
- tokens_grad: float32 [4096, 768], P(('dp', 'fsdp'))
- encoded_grad: float32 [131072, 768], P(('dp', 'fsdp'))
- self_gain_grad: float32 [768], P(('dp', 'fsdp'))
- cross_gain_grad: float32 [768], P(('dp', 'fsdp'))
- ffn_gain_grad: float32 [768], P(('dp', 'fsdp'))
- self_query_grad: float32 [768, 768], P(('dp', 'fsdp'))
- self_key_grad: float32 [768, 768], P(('dp', 'fsdp'))
- self_value_grad: float32 [768, 768], P(('dp', 'fsdp'))
- self_out_grad: float32 [768, 768], P(('dp', 'fsdp'))
- cross_query_grad: float32 [768, 768], P(('dp', 'fsdp'))
- cross_key_grad: float32 [768, 768], P(('dp', 'fsdp'))
- cross_value_grad: float32 [768, 768], P(('dp', 'fsdp'))
- cross_out_grad: float32 [768, 768], P(('dp', 'fsdp'))
- ffn_in_grad: float32 [768, 3072], P(('dp', 'fsdp'))
- ffn_out_grad: float32 [3072, 768], P(('dp', 'fsdp'))
The draws below stay inside these ranges and needn't reach their ends.
Inputs may be any that keep to these rules, and one draw needn't show every extreme that they name: `segment_ids`: within a packed row the query numbers never fall; every one of the 4 queries has 1 to 64 tokens. `passage_group`: each packed row's entries are a permutation of 0 to 3: every query reads a passage block of its own.
All inputs are finite; a program needn't handle non-finite values.
Results may differ from the reference program's by a relative error of at most 0.02.
Values may be sent and summed in bfloat16 or wider, within the bound.
No kernel may reach another device: no remote copies, remote signals or barrier semaphores. Data moves between devices by JAX's collectives and lax.ppermute only.
A program may use at most 192 MiB of HBM per device.

```python
import math
import jax
import jax.numpy as jnp
import numpy as np
from jax import lax

D = 768
HEADS = 12
HEAD = 64
FF = 3072
ROW = 128
SEGS = 4
PASSAGES = 4
PASS_LEN = 256
SEG_MOST = 64
ENC_DEV = 4096
ROWS = 32
TOKENS = 4096
ENC_ALL = 131072


def raised(drawn, stream_key, source, target, shards_of, factor):
    owner, partner = [(jnp.arange(drawn.shape[position]) // (drawn.shape[position] // shards_of)).reshape([-1 if axis == position else 1 for axis in range(drawn.ndim)]) for position in (source, target)]
    chosen = jax.random.permutation(stream_key, shards_of)[partner]
    strong = (owner == chosen) | (owner == (partner + shards_of // 2) % shards_of)
    return jnp.where(strong, factor * drawn, drawn)


def block_scale(rng, extent, cuts, low, largest):
    gain = 1.0
    for axis_at, shards_of in cuts:
        steps = jax.random.uniform(jax.random.fold_in(jax.random.fold_in(rng, 6), axis_at), (shards_of,), jnp.float32, low / len(cuts), largest / len(cuts))
        gain = gain * jnp.repeat(jnp.exp(steps), extent[axis_at] // shards_of).reshape((-1,) + (1,) * (len(extent) - 1 - axis_at))
    return gain


def split_up(number_of, total, reach, skew):
    loads = [(1 << 20) // math.isqrt(grade ** skew) + 1 for grade in range(2, number_of + 1)]
    surplus, counts = total - reach - (number_of - 1), [1] * (number_of - 1)
    while surplus > 0:
        free = [i for i in range(number_of - 1) if counts[i] < reach]
        mass, remaining = sum([loads[i] for i in free]), surplus
        for i in free:
            more = min(reach - counts[i], max(1, remaining * loads[i] // mass), surplus)
            counts[i] = counts[i] + more
            surplus = surplus - more
    return np.array([reach] + counts)


def uneven_parts(own_key, number_of, total, bound, slope):
    if number_of == 2:
        one = jax.random.randint(own_key, (), max(1, total - bound), min(bound, total - 1) + 1)
        return jnp.stack([one, total - one])
    sizes = jnp.asarray(split_up(number_of, total, bound, slope), jnp.int32)
    pairs = (number_of - 1) // 2
    giver, sink = sizes[1:1 + 2 * pairs:2], sizes[2:2 + 2 * pairs:2]
    room = jnp.minimum(giver - 1, bound - sink)
    moved = jax.random.randint(jax.random.fold_in(own_key, 1), (pairs,), 0, 1 << 20) % (room + 1)
    sizes = sizes.at[1:1 + 2 * pairs:2].set(giver - moved).at[2:2 + 2 * pairs:2].set(sink + moved)
    return sizes[jax.random.permutation(jax.random.fold_in(own_key, 2), number_of)]


def gaussian(own_key, shape, width, bound, cuts=(), held_as=jnp.bfloat16):
    level = block_scale(own_key, shape, cuts, -0.22, 0.18) if cuts else 1.0
    values = jax.random.normal(own_key, shape, jnp.float32) * width * level
    return jnp.minimum(jnp.maximum(values, -bound), bound).astype(held_as)


def noise_with(rng, extent, width, reach, cuts, heavy, dtype=jnp.bfloat16):
    drawn = width * jax.random.normal(rng, extent, jnp.float32)
    if cuts:
        drawn = drawn * block_scale(rng, extent, cuts, -0.22, 0.18)
    return jnp.clip(raised(drawn, jax.random.fold_in(rng, 3), *heavy), -reach, reach).astype(dtype)


def setup_inputs(seed: int = 0) -> dict:
    seeds = jax.random.split(jax.random.key(seed), 19)
    tokens = noise_with(seeds[0], (TOKENS, D), 1.0, 6.0, ((0, 32),), (0, 1, 32, 2.75))
    encoded = gaussian(seeds[1], (ENC_ALL, D), 1.0, 6.0, ((0, 32),))
    segment_ids = jax.vmap(lambda own: jnp.searchsorted(jnp.cumsum(uneven_parts(own, SEGS, ROW, SEG_MOST, 1)), jnp.arange(ROW), side="right"))(jax.random.split(seeds[2], ROWS)).reshape((ROWS, ROW)).astype(jnp.int32)
    passage_group = jax.vmap(lambda own: jax.random.permutation(own, SEGS))(jax.random.split(seeds[3], ROWS)).reshape((ROWS, SEGS)).astype(jnp.int32)
    cotangent = gaussian(seeds[4], (TOKENS, D), 1.0, 6.0, ((0, 32),))
    self_gain = jnp.clip(1.0 + 0.1 * jax.random.normal(seeds[5], (D,), jnp.float32), 0.5, 1.5).astype(jnp.bfloat16)
    cross_gain = jnp.clip(1.0 + 0.1 * jax.random.normal(seeds[6], (D,), jnp.float32), 0.5, 1.5).astype(jnp.bfloat16)
    ffn_gain = jnp.clip(1.0 + 0.1 * jax.random.normal(seeds[7], (D,), jnp.float32), 0.5, 1.5).astype(jnp.bfloat16)
    self_query = gaussian(seeds[8], (D, D), D ** -0.5, 0.21875, ((0, 32),))
    self_key = gaussian(seeds[9], (D, D), D ** -0.5, 0.21875, ((0, 32),))
    self_value = gaussian(seeds[10], (D, D), D ** -0.5, 0.21875, ((0, 32),))
    self_out = gaussian(seeds[11], (D, D), (D * SEGS * 4 // ROW) ** -0.5, 0.625, ((0, 32),))
    cross_query = gaussian(seeds[12], (D, D), D ** -0.5, 0.21875, ((0, 32),))
    cross_key = gaussian(seeds[13], (D, D), D ** -0.5, 0.21875, ((0, 32),))
    cross_value = gaussian(seeds[14], (D, D), D ** -0.5, 0.21875, ((0, 32),))
    cross_out = gaussian(seeds[15], (D, D), (max(D // (PASSAGES * PASS_LEN // 2), 1)) ** -0.5, 6.0, ((0, 32),))
    ffn_in = gaussian(seeds[16], (D, FF), D ** -0.5, 0.21875, ((0, 32),))
    ffn_out = gaussian(seeds[17], (FF, D), (FF // 4) ** -0.5, 0.21875, ((0, 32),))
    return {"tokens": tokens, "encoded": encoded, "segment_ids": segment_ids, "passage_group": passage_group, "cotangent": cotangent, "self_gain": self_gain, "cross_gain": cross_gain, "ffn_gain": ffn_gain, "self_query": self_query, "self_key": self_key, "self_value": self_value, "self_out": self_out, "cross_query": cross_query, "cross_key": cross_key, "cross_value": cross_value, "cross_out": cross_out, "ffn_in": ffn_in, "ffn_out": ffn_out}


@jax.custom_vjp
def low(v):
    return lax.optimization_barrier(v.astype(jnp.bfloat16)).astype(jnp.float32)

@jax.custom_vjp
def low_back(v):
    return v

def low_keep(v):
    return (low(v), None)

def low_pass(kept, grad):
    return (grad,)

def back_keep(v):
    return (v, None)

def back_low(kept, grad):
    return (low(grad),)
low.defvjp(low_keep, low_pass)
low_back.defvjp(back_keep, back_low)
epsilon = 1e-06
score_scale = 0.125
masked_score = -1e+30
highest = lax.Precision.HIGHEST

def product(left_side, right_side):
    return jnp.dot(left_side, right_side, preferred_element_type=jnp.float32, precision=highest)

def rms_norm(values, gain_row):
    return values * lax.rsqrt(lax.optimization_barrier(jnp.mean(values * values, axis=-1, keepdims=True)) + epsilon) * gain_row

def attention(queries, key_rows, value_rows, allowed):
    query_heads = queries.reshape(queries.shape[0], HEADS, HEAD)
    key_heads = key_rows.reshape(key_rows.shape[0], HEADS, HEAD)
    value_heads = value_rows.reshape(value_rows.shape[0], HEADS, HEAD)
    scaled = low_back(jnp.einsum('qhd,khd->hqk', query_heads, key_heads, precision=highest) * score_scale)
    masked = jnp.where(allowed[None], scaled, masked_score)
    probabilities = low(jax.nn.softmax(masked, axis=-1))
    context = jnp.einsum('hqk,khd->qhd', probabilities, value_heads, precision=highest)
    return low(low_back(context.reshape(queries.shape[0], D)))

def block_row(hidden_in, encoder_rows, segments, groups_row, params):
    gain_self, gain_cross, gain_ffn, weight_query, weight_key, weight_value, weight_out, cross_query, cross_key, cross_value, cross_out, weight_in, weight_down = params
    positions = jnp.arange(ROW)
    self_allowed = (segments[:, None] == segments[None, :]) & (positions[None, :] <= positions[:, None])
    token_group = lax.optimization_barrier(jnp.sum(jnp.where(segments[:, None] == jnp.arange(SEGS)[None, :], groups_row[None, :], 0), axis=1))
    key_group = jnp.arange(ENC_DEV) // (PASSAGES * PASS_LEN)
    cross_allowed = token_group[:, None] == key_group[None, :]
    normed_one = low(rms_norm(hidden_in, gain_self))
    queries_one = low(low_back(product(normed_one, weight_query)))
    keys_one = low(low_back(product(normed_one, weight_key)))
    values_one = low(low_back(product(normed_one, weight_value)))
    after_self = hidden_in + low_back(product(attention(queries_one, keys_one, values_one, self_allowed), weight_out))
    normed_two = low(rms_norm(after_self, gain_cross))
    queries_two = low(low_back(product(normed_two, cross_query)))
    keys_two = low(low_back(product(encoder_rows, cross_key)))
    values_two = low(low_back(product(encoder_rows, cross_value)))
    after_cross = after_self + low_back(product(attention(queries_two, keys_two, values_two, cross_allowed), cross_out))
    normed_three = low(rms_norm(after_cross, gain_ffn))
    pre_act = low_back(product(normed_three, weight_in))
    activated = low(low_back(jax.nn.gelu(pre_act)))
    return after_cross + low_back(product(activated, weight_down))

def reference(tokens, encoded, segment_ids, passage_group, cotangent, self_gain, cross_gain, ffn_gain, self_query, self_key, self_value, self_out, cross_query, cross_key, cross_value, cross_out, ffn_in, ffn_out):
    params = tuple((p.astype(jnp.float32) for p in (self_gain, cross_gain, ffn_gain, self_query, self_key, self_value, self_out, cross_query, cross_key, cross_value, cross_out, ffn_in, ffn_out)))
    hidden_all = tokens.astype(jnp.float32).reshape(ROWS, ROW, D)
    encoder_all = encoded.astype(jnp.float32).reshape(ROWS, ENC_DEV, D)

    def whole(hidden_rows, encoder_rows, weights):

        def one_row(pieces):
            return block_row(pieces[0], pieces[1], pieces[2], pieces[3], weights)
        return lax.map(jax.checkpoint(one_row), (hidden_rows, encoder_rows, segment_ids, passage_group))
    result, pull_back = jax.vjp(whole, hidden_all, encoder_all, params)
    grad_hidden, grad_encoder, grads = pull_back(cotangent.astype(jnp.float32).reshape(ROWS, ROW, D))
    return (result.reshape(TOKENS, D).astype(jnp.bfloat16), grad_hidden.reshape(TOKENS, D), grad_encoder.reshape(ENC_ALL, D), grads[0], grads[1], grads[2], grads[3], grads[4], grads[5], grads[6], grads[7], grads[8], grads[9], grads[10], grads[11], grads[12])
```

```python
import functools

import jax
import jax.numpy as jnp
from jax import lax
from jax.sharding import PartitionSpec as P

HEAD = 64
SEGS = 4
PASSAGES = 4
PASS_LEN = 256


score_scale = 0.125
epsilon = 1e-06
masked_score = -1e30


def rms_norm(values, gain_row):
    return (
        values * lax.rsqrt(jnp.mean(values * values, axis=-1, keepdims=True) + epsilon) * gain_row
    )


def product(left_side, right_side):
    return jnp.dot(left_side, right_side, preferred_element_type=jnp.float32)


def product_left(left_side, right_side):
    return jnp.einsum("ti,td->id", left_side, right_side, preferred_element_type=jnp.float32)


def product_right(left_side, right_side):
    return jnp.einsum("td,id->ti", left_side, right_side, preferred_element_type=jnp.float32)


def split_heads(matrix):
    return matrix.reshape(matrix.shape[0], -1, HEAD)


def block_scores(query_block, key_heads, allowed):
    scores = (
        jnp.einsum("qhd,khd->hqk", query_block, key_heads, preferred_element_type=jnp.float32)
        * score_scale
    )
    return jnp.where(allowed[None], scores, masked_score)


def attend_forward(queries, key_rows, value_rows, allow_rule):
    row_count = queries.shape[0]
    block_rows = min(512, row_count)
    query_heads = split_heads(queries)
    key_heads = split_heads(key_rows)
    value_heads = split_heads(value_rows)
    scores = block_scores(query_heads, key_heads, allow_rule(0, block_rows))
    largest = jnp.max(scores, axis=-1, keepdims=True)
    weights = jnp.exp(scores - largest)
    totals = jnp.sum(weights, axis=-1, keepdims=True)
    probabilities = (weights / totals).astype(jnp.bfloat16)
    context = jnp.einsum(
        "hqk,khd->qhd", probabilities, value_heads, preferred_element_type=jnp.float32
    )
    contexts = context.reshape(block_rows, -1).astype(jnp.bfloat16)
    log_totals = [largest + jnp.log(totals)]
    return (contexts, log_totals)


def attend_backward(queries, key_rows, value_rows, log_totals, grad_context, allow_rule):
    row_count = queries.shape[0]
    block_rows = min(512, row_count)
    query_heads = split_heads(queries)
    key_heads = split_heads(key_rows)
    value_heads = split_heads(value_rows)
    key_grad = jnp.zeros(key_heads.shape, jnp.float32)
    value_grad = jnp.zeros(value_heads.shape, jnp.float32)
    query_grads = []
    for block_number, begin_row in enumerate(range(0, row_count, block_rows)):
        scores = block_scores(query_heads, key_heads, allow_rule(begin_row, block_rows))
        probabilities = jnp.exp(scores - log_totals[block_number])
        grad_block = split_heads(grad_context)
        value_grad = jnp.einsum(
            "hqk,qhd->khd",
            probabilities.astype(jnp.bfloat16),
            grad_block,
            preferred_element_type=jnp.float32,
        )
        prob_grad = jnp.einsum(
            "qhd,khd->hqk", grad_block, value_heads, preferred_element_type=jnp.float32
        )
        inner_sum = jnp.sum(probabilities * prob_grad, axis=-1, keepdims=True)
        score_grad = (probabilities * (prob_grad - inner_sum)).astype(jnp.bfloat16)
        query_grad = jnp.einsum(
            "hqk,khd->qhd", score_grad, key_heads, preferred_element_type=jnp.float32
        )
        query_grads.append(query_grad.reshape(block_rows, -1) * score_scale)
        key_grad = (
            jnp.einsum("hqk,qhd->khd", score_grad, query_heads, preferred_element_type=jnp.float32)
            * score_scale
        )
    return (
        query_grads[0].astype(jnp.bfloat16),
        key_grad.reshape(key_rows.shape[0], -1).astype(jnp.bfloat16),
        value_grad.reshape(value_rows.shape[0], -1).astype(jnp.bfloat16),
    )


def norm_backward(values, gain_row, grad_normed):
    unused_value, pull_back = jax.vjp(rms_norm, values, gain_row)
    grad_values, grad_gain = pull_back(grad_normed)
    return (grad_values, grad_gain)


AXES = ("dp", "fsdp")


def swap_with(piece, mask, devices):
    pairs = [(index, index ^ mask) for index in range(devices)]
    return lax.ppermute(piece, AXES, pairs)


def bit_of(me, bit):
    return (me >> bit) & 1


def pair_up(mine, theirs, my_bit, axis):
    low = jnp.where(my_bit == 0, mine, theirs)
    high = jnp.where(my_bit == 0, theirs, mine)
    return jnp.stack([low, high], axis=axis)


def gather_bits(block, order, bits, me, devices):
    held = block
    done = []
    for bit in order:
        theirs = swap_with(held, 1 << bit, devices)
        place = sum(1 for other in done if other > bit)
        held = pair_up(held, theirs, bit_of(me, bit), place)
        done.append(bit)
    return held.reshape(-1, block.shape[-1])


def scatter_bits(partial, order, bits, me, devices):
    rows = partial.shape[0] >> len(bits)
    held = partial.reshape((2,) * len(bits) + (rows, partial.shape[-1]))
    left = sorted(bits, reverse=True)
    for bit in order:
        place = left.index(bit)
        mine = lax.dynamic_index_in_dim(held, bit_of(me, bit), place, keepdims=False)
        other = lax.dynamic_index_in_dim(held, 1 - bit_of(me, bit), place, keepdims=False)
        theirs = swap_with(other.astype(jnp.bfloat16), 1 << bit, devices)
        held = mine.astype(jnp.float32) + theirs.astype(jnp.float32)
        left.remove(bit)
    return held


def per_device(
    fsdp,
    devices,
    tokens,
    encoded,
    segment_ids,
    passage_group,
    cotangent,
    self_gain,
    cross_gain,
    ffn_gain,
    self_query,
    self_key,
    self_value,
    self_out,
    cross_query,
    cross_key,
    cross_value,
    cross_out,
    ffn_in,
    ffn_out,
):
    me = lax.axis_index("dp") * fsdp + lax.axis_index("fsdp")
    core = bit_of(me, 0)
    chip_bits = list(range(1, devices.bit_length() - 1))
    line_bits = [bit for bit in reversed(chip_bits) if bit > 2]
    forward_orders = (line_bits + [2, 1], line_bits + [1, 2])
    backward_orders = ([2, 1] + line_bits[::-1], [1, 2] + line_bits[::-1])

    def my_columns(matrix, owner):
        half = matrix.shape[-1] // 2
        return lax.dynamic_slice_in_dim(matrix, owner * half, half, axis=matrix.ndim - 1)

    def gather_group(first, second, extra):
        pieces = [first, second]
        counts = len(first)
        send = jnp.concatenate([my_columns(s, 1 - core) for s in first + second] + extra, axis=1)
        keep = jnp.concatenate([my_columns(s, core) for s in first + second] + extra, axis=1)
        theirs = swap_with(send, 1, devices)
        block = pair_up(keep, theirs, core, 0).reshape(-1, keep.shape[1])
        cut = counts * (first[0].shape[1] // 2)
        parts = [block[:, cut:], block[:, :cut]]
        wholes = []
        for part, order in zip(parts, forward_orders):
            mine = gather_bits(part, order, chip_bits, me, devices)
            sibling = swap_with(mine[:, : cut], 1, devices)
            pair = (jnp.where(core == 0, mine[:, :cut], sibling), jnp.where(core == 0, sibling, mine[:, :cut]))
            half = cut // counts
            wholes.append(
                [
                    jnp.concatenate([side[:, n * half : (n + 1) * half] for side in pair], axis=1)
                    for n in range(counts)
                ]
                + [mine[:, cut:]]
            )
        return wholes[1][:-1], wholes[0][:-1], wholes[0][-1]

    gains = jnp.stack([self_gain, cross_gain, ffn_gain], axis=1)
    gains = jnp.pad(gains, ((0, 0), (0, 125)))
    (weight_query, weight_key), (weight_value, weight_out), gain_block = gather_group(
        [self_query, self_key], [self_value, self_out], [gains]
    )
    (weight_cq, weight_ck), (weight_cv, weight_co), unused_block = gather_group(
        [cross_query, cross_key], [cross_value, cross_out], []
    )
    gain_self, gain_cross, gain_ffn = gain_block[:, 0], gain_block[:, 1], gain_block[:, 2]
    model = ffn_out.shape[1]
    rows_in = ffn_in.shape[0]
    ffn_shard = jnp.concatenate(
        [ffn_in[:, n * model : (n + 1) * model] for n in range(ffn_in.shape[1] // model)] + [ffn_out],
        axis=0,
    )
    ffn_all = lax.all_gather(ffn_shard, AXES, axis=0)
    blocks_in = ffn_in.shape[1] // model
    weight_in = jnp.concatenate(
        [ffn_all[:, n * rows_in : (n + 1) * rows_in].reshape(-1, model) for n in range(blocks_in)], axis=1
    )
    weight_down = ffn_all[:, blocks_in * rows_in :].reshape(-1, model)

    def core_terms(left, right):
        mine = product_left(left, my_columns(right, core)).astype(jnp.bfloat16)
        other = product_left(left, my_columns(right, 1 - core)).astype(jnp.bfloat16)
        return mine, other

    def core_sum(mine, other):
        theirs = swap_with(other, 1, devices)
        return mine.astype(jnp.float32) + theirs.astype(jnp.float32)

    def reduce_groups(group_first, group_second):
        answers = []
        for group, order in zip((group_first, group_second), backward_orders):
            mine = jnp.concatenate([pair[0] for pair in group], axis=1)
            other = jnp.concatenate([pair[1] for pair in group], axis=1)
            total = core_sum(mine, other)
            total = scatter_bits(total, order, chip_bits, me, devices)
            half_rows = total.shape[0] // 2
            keep = lax.dynamic_slice_in_dim(total, core * half_rows, half_rows, axis=0)
            send = lax.dynamic_slice_in_dim(total, (1 - core) * half_rows, half_rows, axis=0)
            theirs = swap_with(send, 1, devices)
            low = jnp.where(core == 0, keep, theirs)
            high = jnp.where(core == 0, theirs, keep)
            at = 0
            found = []
            for pair in group:
                width = pair[0].shape[1]
                found.append(jnp.concatenate([low[:, at : at + width], high[:, at : at + width]], axis=1))
                at += width
            answers.append(found)
        return answers

    segments = segment_ids[0]
    groups_row = passage_group[0]
    row_count = tokens.shape[0]
    encoder_count = encoded.shape[0]
    positions = lax.iota(jnp.int32, row_count)
    token_group = jnp.sum(
        jnp.where(segments[:, None] == lax.iota(jnp.int32, SEGS)[None, :], groups_row[None, :], 0),
        axis=1,
    )
    key_group = lax.iota(jnp.int32, encoder_count) // (PASSAGES * PASS_LEN)

    def self_rule(begin_row, block_rows):
        return (segments[:, None] == segments[None, :]) & (positions[None, :] <= positions[:, None])

    def cross_rule(begin_row, block_rows):
        return token_group[begin_row : begin_row + block_rows, None] == key_group[None, :]

    hidden_in = tokens.astype(jnp.float32)
    normed_one = rms_norm(hidden_in, gain_self.astype(jnp.float32)).astype(jnp.bfloat16)
    queries_one = product(normed_one, weight_query).astype(jnp.bfloat16)
    keys_one = product(normed_one, weight_key).astype(jnp.bfloat16)
    values_one = product(normed_one, weight_value).astype(jnp.bfloat16)
    context_one, log_one = attend_forward(queries_one, keys_one, values_one, self_rule)
    after_self = hidden_in + product(context_one, weight_out)
    normed_two = rms_norm(after_self, gain_cross.astype(jnp.float32)).astype(jnp.bfloat16)
    queries_two = product(normed_two, weight_cq).astype(jnp.bfloat16)
    keys_two = product(encoded, weight_ck).astype(jnp.bfloat16)
    values_two = product(encoded, weight_cv).astype(jnp.bfloat16)
    context_two, log_two = attend_forward(queries_two, keys_two, values_two, cross_rule)
    after_cross = after_self + product(context_two, weight_co)
    normed_three = rms_norm(after_cross, gain_ffn.astype(jnp.float32)).astype(jnp.bfloat16)
    pre_act = product(normed_three, weight_in)
    activated = jax.nn.gelu(pre_act).astype(jnp.bfloat16)
    block_out = (after_cross + product(activated, weight_down)).astype(jnp.bfloat16)
    terms_down = core_terms(activated, cotangent)
    grad_act = product_right(cotangent, weight_down).astype(jnp.bfloat16)
    unused_act, gelu_back = jax.vjp(jax.nn.gelu, pre_act)
    grad_pre = gelu_back(grad_act.astype(jnp.float32))[0].astype(jnp.bfloat16)
    terms_in = core_terms(normed_three, grad_pre)
    grad_normed_three = product_right(grad_pre, weight_in)
    grad_residual, grad_gain_three = norm_backward(
        after_cross, gain_ffn.astype(jnp.float32), grad_normed_three
    )
    grad_after_cross = cotangent.astype(jnp.float32) + grad_residual
    half_in = terms_in[0].shape[1] // 2
    down_chips = [
        term.reshape(devices // 2, 2, -1, term.shape[1]).swapaxes(0, 1).reshape(2, -1, term.shape[1])
        for term in terms_down
    ]
    ((sum_in_first,), (sum_in_second,)) = reduce_groups(
        [(terms_in[0][:, :half_in], terms_in[1][:, :half_in])],
        [(terms_in[0][:, half_in:], terms_in[1][:, half_in:])],
    )
    quarter = half_in
    summed_in = jnp.concatenate(
        [sum_in_first[:, :quarter], sum_in_second[:, :quarter], sum_in_first[:, quarter:], sum_in_second[:, quarter:]],
        axis=1,
    )
    down_parts = []
    for side, order in zip((0, 1), backward_orders):
        total = core_sum(down_chips[0][side], down_chips[1][side])
        down_parts.append(scatter_bits(total, order, chip_bits, me, devices))
    down_keep = jnp.where(core == 0, down_parts[0], down_parts[1])
    down_send = jnp.where(core == 0, down_parts[1], down_parts[0])
    down_theirs = swap_with(down_send, 1, devices)
    summed_down = jnp.concatenate(
        [jnp.where(core == 0, down_keep, down_theirs), jnp.where(core == 0, down_theirs, down_keep)], axis=1
    )
    branch_two = grad_after_cross.astype(jnp.bfloat16)
    terms_co = core_terms(context_two, branch_two)
    grad_context_two = product_right(branch_two, weight_co).astype(jnp.bfloat16)
    grad_queries_two, grad_keys_two, grad_values_two = attend_backward(
        queries_two, keys_two, values_two, log_two, grad_context_two, cross_rule
    )
    terms_cq = core_terms(normed_two, grad_queries_two)
    terms_ck = core_terms(encoded, grad_keys_two)
    terms_cv = core_terms(encoded, grad_values_two)
    grad_normed_two = product_right(grad_queries_two, weight_cq)
    encoded_grad = product_right(grad_keys_two, weight_ck) + product_right(
        grad_values_two, weight_cv
    )
    grad_residual, grad_gain_two = norm_backward(
        after_self, gain_cross.astype(jnp.float32), grad_normed_two
    )
    grad_after_self = grad_after_cross + grad_residual
    (summed_cq, summed_co), (summed_ck, summed_cv) = reduce_groups([terms_cq, terms_co], [terms_ck, terms_cv])
    branch_one = grad_after_self.astype(jnp.bfloat16)
    terms_out = core_terms(context_one, branch_one)
    grad_context_one = product_right(branch_one, weight_out).astype(jnp.bfloat16)
    grad_queries_one, grad_keys_one, grad_values_one = attend_backward(
        queries_one, keys_one, values_one, log_one, grad_context_one, self_rule
    )
    terms_query = core_terms(normed_one, grad_queries_one)
    terms_key = core_terms(normed_one, grad_keys_one)
    terms_value = core_terms(normed_one, grad_values_one)
    grad_normed_one = (
        product_right(grad_queries_one, weight_query)
        + product_right(grad_keys_one, weight_key)
        + product_right(grad_values_one, weight_value)
    )
    grad_residual, grad_gain_one = norm_backward(
        hidden_in, gain_self.astype(jnp.float32), grad_normed_one
    )
    tokens_grad = grad_after_self + grad_residual
    grad_gains = jnp.pad(jnp.stack([grad_gain_one, grad_gain_two, grad_gain_three], axis=1), ((0, 0), (0, 125)))
    grad_gains = grad_gains.astype(jnp.bfloat16)
    (summed_query, summed_key, summed_gains), (summed_value, summed_out) = reduce_groups(
        [terms_query, terms_key, (grad_gains, grad_gains)], [terms_value, terms_out]
    )
    own_gains = jnp.where(core == 0, summed_gains[:, :128], summed_gains[:, 128:])
    return (
        block_out,
        tokens_grad,
        encoded_grad,
        own_gains[:, 0],
        own_gains[:, 1],
        own_gains[:, 2],
        summed_query,
        summed_key,
        summed_value,
        summed_out,
        summed_cq,
        summed_ck,
        summed_cv,
        summed_co,
        summed_in,
        summed_down,
    )


def solution(mesh):
    return jax.shard_map(
        functools.partial(per_device, mesh.shape["fsdp"], mesh.size),
        mesh=mesh,
        in_specs=(
            P(("dp", "fsdp"), None),
            P(("dp", "fsdp"), None),
            P(("dp", "fsdp"), None),
            P(("dp", "fsdp"), None),
            P(("dp", "fsdp"), None),
            P(("dp", "fsdp")),
            P(("dp", "fsdp")),
            P(("dp", "fsdp")),
            P(("dp", "fsdp"), None),
            P(("dp", "fsdp"), None),
            P(("dp", "fsdp"), None),
            P(("dp", "fsdp"), None),
            P(("dp", "fsdp"), None),
            P(("dp", "fsdp"), None),
            P(("dp", "fsdp"), None),
            P(("dp", "fsdp"), None),
            P(("dp", "fsdp"), None),
            P(("dp", "fsdp"), None),
        ),
        out_specs=(
            P(("dp", "fsdp"), None),
            P(("dp", "fsdp"), None),
            P(("dp", "fsdp"), None),
            P(("dp", "fsdp")),
            P(("dp", "fsdp")),
            P(("dp", "fsdp")),
            P(("dp", "fsdp"), None),
            P(("dp", "fsdp"), None),
            P(("dp", "fsdp"), None),
            P(("dp", "fsdp"), None),
            P(("dp", "fsdp"), None),
            P(("dp", "fsdp"), None),
            P(("dp", "fsdp"), None),
            P(("dp", "fsdp"), None),
            P(("dp", "fsdp"), None),
            P(("dp", "fsdp"), None),
        ),
        check_vma=False,
    )
```

```python
import functools

import jax
import jax.numpy as jnp
from jax import lax
from jax.experimental import pallas as pl
from jax.experimental.pallas import tpu as pltpu
from jax.sharding import PartitionSpec as P

HEAD = 64
CHUNK = 16
PAIR = 2 * HEAD
epsilon = 1e-06
masked_score = -1e30
VMEM_BYTES = 60 << 20


def contract(left, right, left_dim, right_dim):
    return lax.dot_general(
        left, right, (((left_dim,), (right_dim,)), ((), ())), preferred_element_type=jnp.float32
    )


def low(values):
    return values.astype(jnp.bfloat16)


def normalize(values, gain_row):
    return values * lax.rsqrt(jnp.mean(values * values, axis=-1, keepdims=True) + epsilon) * gain_row


def norm_backward(values, gain_row, grad):
    scale = lax.rsqrt(jnp.mean(values * values, axis=-1, keepdims=True) + epsilon)
    grad_gain = jnp.sum(grad * values * scale, axis=0, keepdims=True)
    weighted = gain_row * grad
    inner = jnp.mean(weighted * values, axis=-1, keepdims=True)
    return scale * weighted - values * (scale * scale * scale) * inner, grad_gain


def pair_rows(block):
    lane = lax.broadcasted_iota(jnp.int32, block.shape, 1)
    zero = jnp.zeros_like(block)
    return jnp.concatenate(
        [jnp.where(lane < HEAD, block, zero), jnp.where(lane >= HEAD, block, zero)], axis=0
    )


def pair_lanes(both):
    rows = both.shape[0] // 2
    lane = lax.broadcasted_iota(jnp.int32, (rows, both.shape[1]), 1)
    return jnp.where(lane < HEAD, both[:rows], both[rows:])


def weight_copies(core, sources, kept, sems):
    half = kept.shape[-1]
    copies = []
    for number in range(kept.shape[0]):
        for side, source in enumerate(sources[number // 2]):
            place = core if side == 0 else 1 - core
            copies.append(
                pltpu.make_async_copy(
                    source.at[:, (number % 2) * half : (number % 2 + 1) * half],
                    kept.at[number, place],
                    sems.at[2 * number + side],
                )
            )
    return copies


def times(left, kept, number):
    return jnp.concatenate([contract(left, kept[number, side], 1, 0) for side in range(2)], axis=1)


def times_back(left, kept, number):
    half = kept.shape[-1]
    return contract(left[:, :half], kept[number, 0], 1, 1) + contract(left[:, half:], kept[number, 1], 1, 1)


def grad_into(left, right, held, number):
    half = held.shape[-1]
    for side in range(2):
        held[number, side] = low(contract(left, right[:, side * half : (side + 1) * half], 0, 0))


def grad_copies(core, targets, held, number, sems):
    half = held.shape[-1]
    copies = []
    for side, target in enumerate(targets[number // 2]):
        place = core if side == 0 else 1 - core
        copies.append(
            pltpu.make_async_copy(
                held.at[number, place],
                target.at[:, (number % 2) * half : (number % 2 + 1) * half],
                sems.at[2 * number + side],
            )
        )
    return copies


def self_mask(ids_row):
    tokens = ids_row.shape[1]
    wide = jnp.broadcast_to(ids_row.astype(jnp.float32), (tokens, tokens))
    query = lax.broadcasted_iota(jnp.int32, (tokens, tokens), 0)
    key = lax.broadcasted_iota(jnp.int32, (tokens, tokens), 1)
    allowed = jnp.where((wide == wide.T) & (key <= query), 1.0, 0.0)
    return jnp.concatenate([allowed, allowed], axis=0) > 0.5


def self_probs(queries, keys, allowed):
    scores = jnp.where(allowed, contract(pair_rows(queries), keys, 1, 1) * 0.125, masked_score)
    weights = jnp.exp(scores - jnp.max(scores, axis=-1, keepdims=True))
    return weights / jnp.sum(weights, axis=-1, keepdims=True)


def self_forward_kernel(
    core_ref, ids, tokens, gains, first_mine, first_sibling, second_mine, second_sibling,
    projected, context, after, kept, sems,
):
    core = core_ref[0]
    copies = weight_copies(
        core, ((first_mine, first_sibling), (second_mine, second_sibling)), kept, sems
    )
    for copy in copies:
        copy.start()
    model = tokens.shape[1]
    hidden = tokens[...].astype(jnp.float32)
    normed = low(normalize(hidden, gains[0:1, :]))
    for number in range(3):
        copies[2 * number].wait()
        copies[2 * number + 1].wait()
        projected[number] = low(times(normed, kept, number))
    allowed = self_mask(ids[...])
    for j in range(model // PAIR):
        columns = slice(j * PAIR, (j + 1) * PAIR)
        probs = self_probs(projected[0, :, columns], projected[1, :, columns], allowed)
        context[:, columns] = low(pair_lanes(contract(low(probs), projected[2, :, columns], 1, 0)))
    copies[6].wait()
    copies[7].wait()
    after[...] = hidden + times(context[...], kept, 3)


def self_backward_kernel(
    core_ref, ids, tokens, gains, grad_after, gain_grads, projected, context,
    first_mine, first_sibling, second_mine, second_sibling,
    tokens_grad, first_grad, first_other, second_grad, second_other,
    kept, held, gain_held, sems, out_sems,
):
    core = core_ref[0]
    copies = weight_copies(
        core, ((first_mine, first_sibling), (second_mine, second_sibling)), kept, sems
    )
    for copy in copies:
        copy.start()
    model = tokens.shape[1]
    count = tokens.shape[0]
    hidden = tokens[...].astype(jnp.float32)
    normed = low(normalize(hidden, gains[0:1, :]))
    branch = low(grad_after[...])
    targets = ((first_grad, first_other), (second_grad, second_other))
    started = []

    def send(number):
        for copy in grad_copies(core, targets, held, number, out_sems):
            copy.start()
            started.append(copy)

    grad_into(context[...], branch, held, 3)
    send(3)
    for copy in copies:
        copy.wait()
    grad_context = low(times_back(branch, kept, 3))
    allowed = self_mask(ids[...])
    found = ([], [], [])
    for j in range(model // PAIR):
        columns = slice(j * PAIR, (j + 1) * PAIR)
        queries, keys = projected[0, :, columns], projected[1, :, columns]
        probs = self_probs(queries, keys, allowed)
        pulled = pair_rows(grad_context[:, columns])
        prob_grad = contract(pulled, projected[2, :, columns], 1, 1)
        inner = jnp.sum(probs * prob_grad, axis=-1, keepdims=True)
        score_grad = low(probs * (prob_grad - inner))
        found[0].append(low(pair_lanes(contract(score_grad, keys, 1, 0)) * 0.125))
        found[1].append(low(contract(score_grad, pair_rows(queries), 0, 0) * 0.125))
        found[2].append(low(contract(low(probs), pulled, 0, 0)))
    grad_normed = None
    for number in range(3):
        whole = jnp.concatenate(found[number], axis=1)
        grad_into(normed, whole, held, number)
        send(number)
        part = times_back(whole, kept, number)
        grad_normed = part if grad_normed is None else grad_normed + part
    grad_hidden, grad_gain = norm_backward(hidden, gains[0:1, :], grad_normed)
    tokens_grad[...] = grad_after[...] + grad_hidden
    row = lax.broadcasted_iota(jnp.int32, (count, model), 0)
    others = gain_grads[...]
    wide = jnp.where(
        row == 0, grad_gain, jnp.where(row == 1, others[0:1], jnp.where(row == 2, others[1:2], 0.0))
    )
    gain_held[...] = low(wide.T)
    for slot, target in enumerate((first_grad, first_other)):
        copy = pltpu.make_async_copy(gain_held, target.at[:, model : model + PAIR], out_sems.at[8 + slot])
        copy.start()
        started.append(copy)
    for copy in started:
        copy.wait()


def row_copies(encoded, rows_ref, sems, segs):
    size = encoded.shape[0] // segs
    return [
        pltpu.make_async_copy(
            encoded.at[pl.ds(s * size, size)], rows_ref.at[pl.ds(s * size, size)], sems.at[s]
        )
        for s in range(segs)
    ]


def segment_length(ids, s):
    return lax.fori_loop(
        0, ids.shape[1], lambda at, found: found + (ids[0, at] == s).astype(jnp.int32), 0
    )


def in_segment(token, begin, end, heads):
    row = lax.broadcasted_iota(jnp.int32, (heads, CHUNK, 1), 1) + token
    return (row >= begin) & (row < end)


def pair_weight(kept, number, j):
    per_half = kept.shape[-1] // PAIR
    return kept[number, j // per_half, :, (j % per_half) * PAIR : (j % per_half + 1) * PAIR]


def cross_forward_kernel(
    core_ref, ids, groups, after_self, gains, encoded,
    first_mine, first_sibling, second_mine, second_sibling,
    queries, context, after_cross, probs_out, mixed_out, spread_out,
    rows_ref, kept, sems, weight_sems,
):
    core = core_ref[0]
    heads, tokens, model = spread_out.shape
    segs = groups.shape[1]
    block_rows = encoded.shape[0] // segs
    copies = weight_copies(
        core, ((first_mine, first_sibling), (second_mine, second_sibling)), kept, weight_sems
    )
    for copy in copies[:4]:
        copy.start()
    row_moves = row_copies(encoded, rows_ref, sems, segs)
    for copy in row_moves:
        copy.start()
    for copy in copies[4:]:
        copy.start()
    normed = low(normalize(after_self[...], gains[1:2, :]))
    for copy in copies[:4]:
        copy.wait()
    queries[...] = low(times(normed, kept, 0))
    for j in range(heads // 2):
        block = queries[:, j * PAIR : (j + 1) * PAIR] * jnp.bfloat16(0.125)
        spread = low(contract(pair_rows(block), pair_weight(kept, 1, j), 1, 1))
        spread_out[2 * j] = spread[:tokens]
        spread_out[2 * j + 1] = spread[tokens:]
    for copy in row_moves:
        copy.wait()

    def segment(s, begin):
        end = begin + segment_length(ids, s)
        base = pl.multiple_of(groups[0, s] * block_rows, block_rows)

        def chunk(c, carry):
            token = pl.multiple_of(c * CHUNK, CHUNK)
            rows = rows_ref[pl.ds(base, block_rows), :]
            left = spread_out[:, pl.ds(token, CHUNK), :].reshape(heads * CHUNK, model)
            scores = contract(left, rows, 1, 1)
            weights = jnp.exp(scores - jnp.max(scores, axis=-1, keepdims=True))
            totals = jnp.sum(weights, axis=-1, keepdims=True)
            probs = low(weights * (1.0 / totals))
            mixed = low(contract(probs, rows, 1, 0))
            inside = in_segment(token, begin, end, heads)
            at = (slice(None), pl.ds(token, CHUNK), slice(None))
            probs = probs.reshape(heads, CHUNK, block_rows)
            mixed = mixed.reshape(heads, CHUNK, model)
            probs_out[at] = jnp.where(inside, probs, probs_out[at])
            mixed_out[at] = jnp.where(inside, mixed, mixed_out[at])
            return carry

        lax.fori_loop(begin >> 4, (end + CHUNK - 1) >> 4, chunk, 0)
        return end

    lax.fori_loop(0, segs, segment, 0)
    for copy in copies[4:]:
        copy.wait()
    for j in range(heads // 2):
        both = jnp.concatenate([mixed_out[2 * j], mixed_out[2 * j + 1]], axis=0)
        found = contract(both, pair_weight(kept, 2, j), 1, 0)
        context[:, j * PAIR : (j + 1) * PAIR] = low(pair_lanes(found))
    after_cross[...] = after_self[...] + times(context[...], kept, 3)


def cross_backward_kernel(
    core_ref, ids, groups, grad_after, after_self, gains, ffn_gain_grad, queries, context, encoded,
    probs_ref, mixed, spread, first_mine, first_sibling, second_mine, second_sibling,
    grad_self, gain_grads, grad_rows, first_grad, first_other, second_grad, second_other,
    rows_ref, pulled_ref, moved_ref, sum_ref, kept, held, sems, row_sems, weight_sems, out_sems,
):
    core = core_ref[0]
    heads, tokens, model = spread.shape
    segs = groups.shape[1]
    block_rows = encoded.shape[0] // segs
    half = kept.shape[-1]
    copies = weight_copies(
        core, ((first_mine, first_sibling), (second_mine, second_sibling)), kept, weight_sems
    )
    for copy in copies[4:] + copies[:4]:
        copy.start()
    row_moves = row_copies(encoded, rows_ref, sems, segs)
    for copy in row_moves:
        copy.start()
    targets = ((first_grad, first_other), (second_grad, second_other))
    started = []

    def send(number):
        for copy in grad_copies(core, targets, held, number, out_sems):
            copy.start()
            started.append(copy)

    branch = low(grad_after[...])
    grad_into(context[...], branch, held, 3)
    send(3)
    for copy in copies:
        copy.wait()
    grad_context = low(times_back(branch, kept, 3))
    for j in range(heads // 2):
        block = grad_context[:, j * PAIR : (j + 1) * PAIR]
        pulled = low(contract(pair_rows(block), pair_weight(kept, 2, j), 1, 1))
        pulled_ref[2 * j] = pulled[:tokens]
        pulled_ref[2 * j + 1] = pulled[tokens:]
    for copy in row_moves:
        copy.wait()

    def write_out(s):
        slot = s & 1
        base = pl.multiple_of(groups[0, s] * block_rows, block_rows)
        return pltpu.make_async_copy(
            sum_ref.at[slot], grad_rows.at[pl.ds(base, block_rows)], row_sems.at[slot]
        )

    def segment(s, begin):
        end = begin + segment_length(ids, s)
        base = pl.multiple_of(groups[0, s] * block_rows, block_rows)
        slot = s & 1

        @pl.when(s >= 2)
        def _():
            write_out(s - 2).wait()

        sum_ref[slot] = jnp.zeros((block_rows, model), jnp.float32)

        def chunk(c, carry):
            token = pl.multiple_of(c * CHUNK, CHUNK)
            at = (slice(None), pl.ds(token, CHUNK), slice(None))
            rows = rows_ref[pl.ds(base, block_rows), :]
            inside = in_segment(token, begin, end, heads)
            pulled = jnp.where(inside, pulled_ref[at], jnp.zeros((), jnp.bfloat16))
            pulled = pulled.reshape(heads * CHUNK, model)
            probs = probs_ref[at].reshape(heads * CHUNK, block_rows)
            prob_grad = contract(pulled, rows, 1, 1)
            wide = probs.astype(jnp.float32)
            inner = jnp.sum(wide * prob_grad, axis=-1, keepdims=True)
            score_grad = low(wide * (prob_grad - inner))
            moved = low(contract(score_grad, rows, 1, 0)).reshape(heads, CHUNK, model)
            moved_ref[at] = jnp.where(inside, moved, moved_ref[at])
            left = jnp.concatenate([score_grad, probs], axis=0)
            right = jnp.concatenate([spread[at].reshape(heads * CHUNK, model), pulled], axis=0)
            sum_ref[slot] += contract(left, right, 0, 0)
            return carry

        lax.fori_loop(begin >> 4, (end + CHUNK - 1) >> 4, chunk, 0)
        write_out(s).start()
        return end

    lax.fori_loop(0, segs, segment, 0)
    found = []
    per_half = half // PAIR
    for j in range(heads // 2):
        columns = slice((j % per_half) * PAIR, (j % per_half + 1) * PAIR)
        both = jnp.concatenate([moved_ref[2 * j], moved_ref[2 * j + 1]], axis=0)
        found.append(low(pair_lanes(contract(both, pair_weight(kept, 1, j), 1, 0)) * 0.125))
        block = queries[:, j * PAIR : (j + 1) * PAIR] * jnp.bfloat16(0.125)
        held[1, j // per_half, :, columns] = low(contract(both, pair_rows(block), 0, 0))
    send(1)
    for j in range(heads // 2):
        columns = slice((j % per_half) * PAIR, (j % per_half + 1) * PAIR)
        block = grad_context[:, j * PAIR : (j + 1) * PAIR]
        both = jnp.concatenate([mixed[2 * j], mixed[2 * j + 1]], axis=0)
        held[2, j // per_half, :, columns] = low(contract(both, pair_rows(block), 0, 0))
    send(2)
    grad_queries = jnp.concatenate(found, axis=1)
    values = after_self[...]
    grad_into(low(normalize(values, gains[1:2, :])), grad_queries, held, 0)
    send(0)
    grad_values, grad_gain = norm_backward(values, gains[1:2, :], times_back(grad_queries, kept, 0))
    grad_self[...] = grad_after[...] + grad_values
    gain_grads[0:1, :] = grad_gain
    gain_grads[1:2, :] = ffn_gain_grad[0:1, :]
    for copy in started:
        copy.wait()
    for s in range(segs - 2, segs):
        write_out(s).wait()


def gelu_both(values):
    scale = 0.7978845608028654
    square = values * values
    bend = jnp.tanh(scale * (values + 0.044715 * (square * values)))
    half = 0.5 * (1.0 + bend)
    slope = half + 0.5 * values * (1.0 - bend * bend) * (scale * (1.0 + 3.0 * 0.044715 * square))
    return values * half, slope


def ffn_kernel(
    direct,
    core_ref, after_cross, gains, cotangent, weight_in, gathered,
    block_out, grad_after, gain_grad, in_mine, in_other, down_mine, down_other,
    kept_in, kept_down, held_in, held_down, sems, out_sems,
):
    core = core_ref[0]
    blocks, model, width = weight_in.shape
    per_block, rows_down = kept_down.shape[1:3]
    copies = []
    for j in range(blocks):
        copies.append(pltpu.make_async_copy(weight_in.at[j], kept_in.at[j], sems.at[2 * j]))
        copies.append(
            pltpu.make_async_copy(
                gathered.at[pl.ds(j * per_block, per_block), pl.ds(gathered.shape[1] - rows_down, rows_down)]
                if direct
                else gathered.at[j],
                kept_down.at[j],
                sems.at[2 * j + 1],
            )
        )
    for copy in copies:
        copy.start()
    values = after_cross[...]
    normed = low(normalize(values, gains[2:3, :]))
    pull = cotangent[...]
    total = values
    grad_normed = jnp.zeros(values.shape, jnp.float32)
    chips = per_block // 2
    started = []
    for j in range(blocks):
        copies[2 * j].wait()
        copies[2 * j + 1].wait()
        weight_up = kept_in[j]
        weight_down = kept_down[j].reshape(width, model)
        activated, slope = gelu_both(contract(normed, weight_up, 1, 0))
        activated = low(activated)
        total = total + contract(activated, weight_down, 1, 0)
        grad_act = low(contract(pull, weight_down, 1, 1)).astype(jnp.float32)
        grad_pre = low(slope * grad_act)
        grad_normed = grad_normed + contract(grad_pre, weight_up, 1, 1)
        held_in[j] = low(contract(normed, grad_pre, 0, 0))
        grad_down = low(contract(activated, pull, 0, 0))
        if direct:
            for k in range(per_block):
                at = (j * chips + k // 2) * rows_down
                held_down[k % 2, at : at + rows_down] = grad_down[k * rows_down : (k + 1) * rows_down]
        else:
            held_down[j // 2, (j % 2) * width : (j % 2 + 1) * width] = grad_down
    half = blocks // 2
    for side, target in enumerate((in_mine, in_other)):
        place = core if side == 0 else 1 - core
        for j in range(half):
            copy = pltpu.make_async_copy(
                held_in.at[place * half + j],
                target.at[:, j * width : (j + 1) * width],
                out_sems.at[side * half + j],
            )
            copy.start()
            started.append(copy)
    for side, target in enumerate((down_mine, down_other)):
        place = (core if side == 0 else 1 - core) if direct else side
        copy = pltpu.make_async_copy(held_down.at[place], target, out_sems.at[2 * half + side])
        copy.start()
        started.append(copy)
    block_out[...] = low(total)
    grad_values, grad_gain = norm_backward(values, gains[2:3, :], grad_normed)
    grad_after[...] = pull.astype(jnp.float32) + grad_values
    gain_grad[0:1, :] = grad_gain
    for copy in started:
        copy.wait()

AXES = ("dp", "fsdp")


def swap_with(piece, mask, devices):
    pairs = [(index, index ^ mask) for index in range(devices)]
    return lax.ppermute(piece, AXES, pairs)


def bit_of(me, bit):
    return (me >> bit) & 1


def pair_up(mine, theirs, my_bit, axis):
    first = jnp.where(my_bit == 0, mine, theirs)
    second = jnp.where(my_bit == 0, theirs, mine)
    return jnp.stack([first, second], axis=axis)


def gather_bits(block, order, me, devices):
    held = block
    done = []
    for bit in order:
        theirs = swap_with(held, 1 << bit, devices)
        place = sum(1 for other in done if other > bit)
        held = pair_up(held, theirs, bit_of(me, bit), place)
        done.append(bit)
    return held.reshape(-1, block.shape[-1])


def core_sum(mine, other, devices):
    theirs = swap_with(other, 1, devices)
    return low(mine.astype(jnp.float32) + theirs.astype(jnp.float32))


def scatter_bits(partial, order, me, devices):
    rows = partial.shape[0] >> len(order)
    held = partial.reshape((2,) * len(order) + (rows, partial.shape[-1]))
    left = sorted(order, reverse=True)
    for bit in order:
        place = left.index(bit)
        mine = lax.dynamic_index_in_dim(held, bit_of(me, bit), place, keepdims=False)
        other = lax.dynamic_index_in_dim(held, 1 - bit_of(me, bit), place, keepdims=False)
        theirs = swap_with(low(other), 1 << bit, devices)
        held = mine.astype(jnp.float32) + theirs.astype(jnp.float32)
        left.remove(bit)
    return held


def core_rows(total, core, devices):
    rows = total.shape[0] // 2
    keep = lax.dynamic_slice_in_dim(total, core * rows, rows, axis=0)
    send = lax.dynamic_slice_in_dim(total, (1 - core) * rows, rows, axis=0)
    theirs = swap_with(send, 1, devices)
    return jnp.where(core == 0, keep, theirs), jnp.where(core == 0, theirs, keep)


VMEM = pl.BlockSpec(memory_space=pltpu.VMEM)
SMEM = pl.BlockSpec(memory_space=pltpu.SMEM)
HBM = pl.BlockSpec(memory_space=pl.ANY)


def shaped(shape, dtype):
    return jax.ShapeDtypeStruct(shape, dtype)


def call(kernel, name, flops, in_specs, out_specs, out_shape, scratch):
    return pl.pallas_call(
        kernel,
        out_shape=out_shape,
        in_specs=in_specs,
        out_specs=out_specs,
        scratch_shapes=scratch,
        compiler_params=pltpu.CompilerParams(vmem_limit_bytes=VMEM_BYTES),
        cost_estimate=pl.CostEstimate(flops=flops, bytes_accessed=10_000_000, transcendentals=0),
        name=name,
    )


def per_device(
    fsdp,
    devices,
    tokens,
    encoded,
    segment_ids,
    passage_group,
    cotangent,
    self_gain,
    cross_gain,
    ffn_gain,
    self_query,
    self_key,
    self_value,
    self_out,
    cross_query,
    cross_key,
    cross_value,
    cross_out,
    ffn_in,
    ffn_out,
):
    me = lax.axis_index("dp") * fsdp + lax.axis_index("fsdp")
    core = bit_of(me, 0)
    core_word = core.reshape(1).astype(jnp.int32)
    chip_bits = list(range(1, devices.bit_length() - 1))
    line_bits = [bit for bit in reversed(chip_bits) if bit > 2]
    forward_orders = (line_bits + [2, 1], line_bits + [1, 2])
    backward_orders = ([2, 1] + line_bits[::-1], [1, 2] + line_bits[::-1])
    count, model = tokens.shape
    encoder_count = encoded.shape[0]
    hidden_units = ffn_in.shape[1]
    heads = model // HEAD
    half = model // 2
    segs = passage_group.shape[1]
    low_type, wide_type = jnp.bfloat16, jnp.float32

    def my_columns(matrix, owner):
        width = matrix.shape[-1] // 2
        return lax.dynamic_slice_in_dim(matrix, owner * width, width, axis=matrix.ndim - 1)

    def gather_group(shards, extra):
        first, second = shards[:2], shards[2:]

        def chip_block(pair, also):
            send = jnp.concatenate([my_columns(shard, 1 - core) for shard in pair] + also, axis=1)
            keep = jnp.concatenate([my_columns(shard, core) for shard in pair] + also, axis=1)
            theirs = swap_with(send, 1, devices)
            return pair_up(keep, theirs, core, 0).reshape(-1, keep.shape[1])

        wholes = []
        for pair, also, order in zip((first, second), (extra, []), forward_orders):
            mine = gather_bits(chip_block(pair, also), order, me, devices)
            wholes.append((mine, swap_with(mine[:, :model], 1, devices)))
        return wholes

    gains = jnp.stack([self_gain, cross_gain, ffn_gain], axis=1)
    gains = jnp.pad(gains, ((0, 0), (0, PAIR - 3)))
    self_weights = gather_group([self_query, self_key, self_value, self_out], [gains])
    cross_weights = gather_group([cross_query, cross_key, cross_value, cross_out], [])
    gain_rows = jnp.pad(self_weights[0][0][:, model : model + 8].T.astype(wide_type), ((0, 0), (0, 0)))
    self_flat = self_weights[0] + self_weights[1]
    cross_flat = cross_weights[0] + cross_weights[1]

    blocks = hidden_units // model
    rows_in = ffn_in.shape[0]
    rows_down = ffn_out.shape[0]
    ffn_shard = jnp.concatenate(
        [ffn_in[:, n * model : (n + 1) * model] for n in range(blocks)] + [ffn_out], axis=0
    )
    gathered = lax.all_gather(ffn_shard, AXES, axis=0)
    weight_in = jnp.stack(
        [gathered[:, n * rows_in : (n + 1) * rows_in].reshape(model, model) for n in range(blocks)]
    )
    direct = rows_down % 16 == 0
    down_shape = (devices // blocks, rows_down) if direct else (1, model)
    down_source = gathered if direct else gathered[:, blocks * rows_in :].reshape(blocks, 1, model, model)

    dma = pltpu.SemaphoreType.DMA
    weights_kept = pltpu.VMEM((4, 2, model, half), low_type)
    projected, context_one, after_self = call(
        self_forward_kernel,
        "self_forward",
        2 * count * model * model * 5,
        [SMEM, VMEM, VMEM, VMEM] + [HBM] * 4,
        [VMEM] * 3,
        (
            shaped((3, count, model), low_type),
            shaped((count, model), low_type),
            shaped((count, model), wide_type),
        ),
        [weights_kept, dma((8,))],
    )(core_word, segment_ids, tokens, gain_rows, *self_flat)

    per_token = (heads, count, model)
    probs_shape = (heads, count, encoder_count // segs)
    queries_two, context_two, after_cross, probs, mixed, spread = call(
        cross_forward_kernel,
        "cross_forward",
        12_000_000_000,
        [SMEM, SMEM, SMEM, VMEM, VMEM] + [HBM] * 5,
        [VMEM] * 6,
        (
            shaped((count, model), low_type),
            shaped((count, model), low_type),
            shaped((count, model), wide_type),
            shaped(probs_shape, low_type),
            shaped(per_token, low_type),
            shaped(per_token, low_type),
        ),
        [pltpu.VMEM(encoded.shape, low_type), weights_kept, dma((segs,)), dma((8,))],
    )(core_word, segment_ids, passage_group, after_self, gain_rows, encoded, *cross_flat)

    (block_out, grad_after_cross, ffn_gain_grad, in_mine, in_other, down_mine, down_other) = call(
        functools.partial(ffn_kernel, direct),
        "ffn",
        2 * count * model * hidden_units * 6,
        [SMEM, VMEM, VMEM, VMEM, HBM, HBM],
        [VMEM] * 3 + [HBM] * 4,
        (
            shaped((count, model), low_type),
            shaped((count, model), wide_type),
            shaped((8, model), wide_type),
            shaped((model, hidden_units // 2), low_type),
            shaped((model, hidden_units // 2), low_type),
            shaped((hidden_units // 2, model), low_type),
            shaped((hidden_units // 2, model), low_type),
        ),
        [
            pltpu.VMEM((blocks, model, model), low_type),
            pltpu.VMEM((blocks,) + down_shape + (model,), low_type),
            pltpu.VMEM((blocks, model, model), low_type),
            pltpu.VMEM((2, hidden_units // 2, model), low_type),
            dma((2 * blocks,)),
            dma((blocks + 2,)),
        ],
    )(core_word, after_cross, gain_rows, cotangent, weight_in, down_source)

    if not direct:
        whole = jnp.concatenate([down_mine, down_other], axis=0).reshape(devices // 2, 2, rows_down, model)
        down_mine, down_other = (
            lax.dynamic_index_in_dim(whole, place, 1, keepdims=False).reshape(-1, model) for place in (core, 1 - core)
        )
    summed_down = scatter_bits(core_sum(down_mine, down_other, devices), backward_orders[0], me, devices)
    in_chip = scatter_bits(core_sum(in_mine, in_other, devices), backward_orders[1], me, devices)
    summed_in = jnp.concatenate(core_rows(in_chip, core, devices), axis=1)

    grad_shapes = tuple(shaped((model, model), low_type) for n in range(4))
    (grad_after_self, gain_grads, encoded_grad, *cross_grads) = call(
        cross_backward_kernel,
        "cross_backward",
        25_000_000_000,
        [SMEM, SMEM, SMEM] + [VMEM] * 6 + [HBM] + [VMEM] * 3 + [HBM] * 4,
        [VMEM] * 2 + [HBM] * 5,
        (
            shaped((count, model), wide_type),
            shaped((8, model), wide_type),
            shaped(encoded.shape, wide_type),
        )
        + grad_shapes,
        [
            pltpu.VMEM(encoded.shape, low_type),
            pltpu.VMEM(per_token, low_type),
            pltpu.VMEM(per_token, low_type),
            pltpu.VMEM((2, encoder_count // segs, model), wide_type),
            weights_kept,
            weights_kept,
            dma((segs,)),
            dma((2,)),
            dma((8,)),
            dma((8,)),
        ],
    )(
        core_word, segment_ids, passage_group, grad_after_cross, after_self, gain_rows, ffn_gain_grad,
        queries_two, context_two, encoded, probs, mixed, spread, *cross_flat,
    )

    def reduce_group(grads):
        answers = []
        for side, order in enumerate(backward_orders):
            mine, other = grads[2 * side], grads[2 * side + 1]
            total = scatter_bits(core_sum(mine, other, devices), order, me, devices)
            pair = core_rows(total, core, devices)
            answers += [
                jnp.concatenate([piece[:, n * half : (n + 1) * half] for piece in pair], axis=1) for n in range(2)
            ]
            if mine.shape[1] > model:
                answers.append(jnp.where(core == 0, pair[0][:, model:], pair[1][:, model:]))
        return answers

    summed_cq, summed_ck, summed_cv, summed_co = reduce_group(cross_grads)

    with_gains = shaped((model, model + PAIR), low_type)
    (tokens_grad, *self_grads) = call(
        self_backward_kernel,
        "self_backward",
        2 * count * model * model * 10,
        [SMEM] + [VMEM] * 7 + [HBM] * 4,
        [VMEM] + [HBM] * 4,
        (shaped((count, model), wide_type), with_gains, with_gains, grad_shapes[0], grad_shapes[0]),
        [weights_kept, weights_kept, pltpu.VMEM((model, PAIR), low_type), dma((8,)), dma((10,))],
    )(
        core_word, segment_ids, tokens, gain_rows, grad_after_self, gain_grads, projected, context_one,
        *self_flat,
    )
    summed_query, summed_key, own_gains, summed_value, summed_out = reduce_group(self_grads)
    return (
        block_out,
        tokens_grad,
        encoded_grad,
        own_gains[:, 0],
        own_gains[:, 1],
        own_gains[:, 2],
        summed_query,
        summed_key,
        summed_value,
        summed_out,
        summed_cq,
        summed_ck,
        summed_cv,
        summed_co,
        summed_in,
        summed_down,
    )


def solution(mesh):
    return jax.shard_map(
        functools.partial(per_device, mesh.shape["fsdp"], mesh.size),
        mesh=mesh,
        in_specs=(
            P(("dp", "fsdp"), None),
            P(("dp", "fsdp"), None),
            P(("dp", "fsdp"), None),
            P(("dp", "fsdp"), None),
            P(("dp", "fsdp"), None),
            P(("dp", "fsdp")),
            P(("dp", "fsdp")),
            P(("dp", "fsdp")),
            P(("dp", "fsdp"), None),
            P(("dp", "fsdp"), None),
            P(("dp", "fsdp"), None),
            P(("dp", "fsdp"), None),
            P(("dp", "fsdp"), None),
            P(("dp", "fsdp"), None),
            P(("dp", "fsdp"), None),
            P(("dp", "fsdp"), None),
            P(("dp", "fsdp"), None),
            P(("dp", "fsdp"), None),
        ),
        out_specs=(
            P(("dp", "fsdp"), None),
            P(("dp", "fsdp"), None),
            P(("dp", "fsdp"), None),
            P(("dp", "fsdp")),
            P(("dp", "fsdp")),
            P(("dp", "fsdp")),
            P(("dp", "fsdp"), None),
            P(("dp", "fsdp"), None),
            P(("dp", "fsdp"), None),
            P(("dp", "fsdp"), None),
            P(("dp", "fsdp"), None),
            P(("dp", "fsdp"), None),
            P(("dp", "fsdp"), None),
            P(("dp", "fsdp"), None),
            P(("dp", "fsdp"), None),
            P(("dp", "fsdp"), None),
        ),
        check_vma=False,
    )
```

```python
import functools

import jax
import jax.numpy as jnp
from jax import lax
from jax.experimental import pallas as pl
from jax.experimental.pallas import tpu as pltpu
from jax.sharding import PartitionSpec as P

HEAD = 64
CHUNK = 16
PAIR = 2 * HEAD
epsilon = 1e-06
masked_score = -1e30
VMEM_BYTES = 60 << 20


def contract(left, right, left_dim, right_dim):
    return lax.dot_general(
        left, right, (((left_dim,), (right_dim,)), ((), ())), preferred_element_type=jnp.float32
    )


def low(values):
    return values.astype(jnp.bfloat16)


def normalize(values, gain_row):
    return values * lax.rsqrt(jnp.mean(values * values, axis=-1, keepdims=True) + epsilon) * gain_row


def norm_backward(values, gain_row, grad):
    scale = lax.rsqrt(jnp.mean(values * values, axis=-1, keepdims=True) + epsilon)
    grad_gain = jnp.sum(grad * values * scale, axis=0, keepdims=True)
    weighted = gain_row * grad
    inner = jnp.mean(weighted * values, axis=-1, keepdims=True)
    return scale * weighted - values * (scale * scale * scale) * inner, grad_gain


def pair_rows(block):
    lane = lax.broadcasted_iota(jnp.int32, block.shape, 1)
    zero = jnp.zeros_like(block)
    return jnp.concatenate(
        [jnp.where(lane < HEAD, block, zero), jnp.where(lane >= HEAD, block, zero)], axis=0
    )


def pair_lanes(both):
    rows = both.shape[0] // 2
    lane = lax.broadcasted_iota(jnp.int32, (rows, both.shape[1]), 1)
    return jnp.where(lane < HEAD, both[:rows], both[rows:])


def weight_copies(core, sources, kept, sems):
    half = kept.shape[-1]
    copies = []
    for number in range(kept.shape[0]):
        for side, source in enumerate(sources[number // 2]):
            place = core if side == 0 else 1 - core
            copies.append(
                pltpu.make_async_copy(
                    source.at[:, (number % 2) * half : (number % 2 + 1) * half],
                    kept.at[number, place],
                    sems.at[2 * number + side],
                )
            )
    return copies


def times(left, kept, number):
    return jnp.concatenate([contract(left, kept[number, side], 1, 0) for side in range(2)], axis=1)


def times_back(left, kept, number):
    half = kept.shape[-1]
    return contract(left[:, :half], kept[number, 0], 1, 1) + contract(left[:, half:], kept[number, 1], 1, 1)


def grad_into(left, right, held, number):
    half = held.shape[-1]
    for side in range(2):
        held[number, side] = low(contract(left, right[:, side * half : (side + 1) * half], 0, 0))


def grad_copies(core, targets, held, number, sems):
    half = held.shape[-1]
    copies = []
    for side, target in enumerate(targets):
        place = core if side == 0 else 1 - core
        copies.append(
            pltpu.make_async_copy(
                held.at[number, place],
                target.at[:, number * half : (number + 1) * half],
                sems.at[2 * number + side],
            )
        )
    return copies


def pack_kernel(core_ref, *refs):
    shards, gains, (send, keep) = refs[:-3], refs[-3], refs[-2:]
    core = core_ref[0]
    half = shards[0].shape[1] // 2
    for number, shard in enumerate(shards):
        for target, place in ((send, 1 - core), (keep, core)):
            target[:, number * half : (number + 1) * half] = shard[:, pl.ds(pl.multiple_of(place * half, PAIR), half)]
    for target in (send, keep):
        target[:, len(shards) * half :] = gains[...]


def self_mask(ids_row):
    tokens = ids_row.shape[1]
    wide = jnp.broadcast_to(ids_row.astype(jnp.float32), (tokens, tokens))
    query = lax.broadcasted_iota(jnp.int32, (tokens, tokens), 0)
    key = lax.broadcasted_iota(jnp.int32, (tokens, tokens), 1)
    allowed = jnp.where((wide == wide.T) & (key <= query), 1.0, 0.0)
    return jnp.concatenate([allowed, allowed], axis=0) > 0.5


def self_probs(queries, keys, allowed):
    scores = jnp.where(allowed, contract(pair_rows(queries), keys, 1, 1) * 0.125, masked_score)
    weights = jnp.exp(scores - jnp.max(scores, axis=-1, keepdims=True))
    return weights / jnp.sum(weights, axis=-1, keepdims=True)


def self_forward_kernel(
    core_ref, ids, tokens, gains, first_mine, first_sibling, second_mine, second_sibling,
    projected, context, after, kept, sems,
):
    core = core_ref[0]
    copies = weight_copies(
        core, ((first_mine, first_sibling), (second_mine, second_sibling)), kept, sems
    )
    for copy in copies:
        copy.start()
    model = tokens.shape[1]
    hidden = tokens[...].astype(jnp.float32)
    normed = low(normalize(hidden, gains[0:1, :]))
    for number in range(3):
        copies[2 * number].wait()
        copies[2 * number + 1].wait()
        projected[number] = low(times(normed, kept, number))
    allowed = self_mask(ids[...])
    for j in range(model // PAIR):
        columns = slice(j * PAIR, (j + 1) * PAIR)
        probs = self_probs(projected[0, :, columns], projected[1, :, columns], allowed)
        context[:, columns] = low(pair_lanes(contract(low(probs), projected[2, :, columns], 1, 0)))
    copies[6].wait()
    copies[7].wait()
    after[...] = hidden + times(context[...], kept, 3)


def self_backward_kernel(
    core_ref, ids, tokens, gains, grad_after, gain_grads, projected, context,
    first_mine, first_sibling, second_mine, second_sibling,
    tokens_grad, grad_mine, grad_other,
    kept, held, gain_held, sems, out_sems,
):
    core = core_ref[0]
    copies = weight_copies(
        core, ((first_mine, first_sibling), (second_mine, second_sibling)), kept, sems
    )
    for copy in copies:
        copy.start()
    model = tokens.shape[1]
    count = tokens.shape[0]
    hidden = tokens[...].astype(jnp.float32)
    normed = low(normalize(hidden, gains[0:1, :]))
    branch = low(grad_after[...])
    started = []

    def send(number):
        for copy in grad_copies(core, (grad_mine, grad_other), held, number, out_sems):
            copy.start()
            started.append(copy)

    grad_into(context[...], branch, held, 3)
    send(3)
    for copy in copies:
        copy.wait()
    grad_context = low(times_back(branch, kept, 3))
    allowed = self_mask(ids[...])
    found = ([], [], [])
    for j in range(model // PAIR):
        columns = slice(j * PAIR, (j + 1) * PAIR)
        queries, keys = projected[0, :, columns], projected[1, :, columns]
        probs = self_probs(queries, keys, allowed)
        pulled = pair_rows(grad_context[:, columns])
        prob_grad = contract(pulled, projected[2, :, columns], 1, 1)
        inner = jnp.sum(probs * prob_grad, axis=-1, keepdims=True)
        score_grad = low(probs * (prob_grad - inner))
        found[0].append(low(pair_lanes(contract(score_grad, keys, 1, 0)) * 0.125))
        found[1].append(low(contract(score_grad, pair_rows(queries), 0, 0) * 0.125))
        found[2].append(low(contract(low(probs), pulled, 0, 0)))
    grad_normed = None
    for number in range(3):
        whole = jnp.concatenate(found[number], axis=1)
        grad_into(normed, whole, held, number)
        send(number)
        part = times_back(whole, kept, number)
        grad_normed = part if grad_normed is None else grad_normed + part
    grad_hidden, grad_gain = norm_backward(hidden, gains[0:1, :], grad_normed)
    tokens_grad[...] = grad_after[...] + grad_hidden
    row = lax.broadcasted_iota(jnp.int32, (count, model), 0)
    others = gain_grads[...]
    wide = jnp.where(
        row == 0, grad_gain, jnp.where(row == 1, others[0:1], jnp.where(row == 2, others[1:2], 0.0))
    )
    gain_held[...] = low(wide.T)
    for slot, target in enumerate((grad_mine, grad_other)):
        copy = pltpu.make_async_copy(gain_held, target.at[:, 2 * model :], out_sems.at[8 + slot])
        copy.start()
        started.append(copy)
    for copy in started:
        copy.wait()


def row_copies(encoded, rows_ref, sems, segs):
    size = encoded.shape[0] // segs
    return [
        pltpu.make_async_copy(
            encoded.at[pl.ds(s * size, size)], rows_ref.at[pl.ds(s * size, size)], sems.at[s]
        )
        for s in range(segs)
    ]


def segment_length(ids, s):
    return lax.fori_loop(
        0, ids.shape[1], lambda at, found: found + (ids[0, at] == s).astype(jnp.int32), 0
    )


def in_segment(token, begin, end, heads):
    row = lax.broadcasted_iota(jnp.int32, (heads, CHUNK, 1), 1) + token
    return (row >= begin) & (row < end)


def pair_weight(kept, number, j):
    per_half = kept.shape[-1] // PAIR
    return kept[number, j // per_half, :, (j % per_half) * PAIR : (j % per_half + 1) * PAIR]


def cross_forward_kernel(
    core_ref, ids, groups, after_self, gains, encoded,
    first_mine, first_sibling, second_mine, second_sibling,
    queries, context, after_cross, normed_out, probs_out, mixed_out, spread_out,
    rows_ref, kept, sems, weight_sems,
):
    core = core_ref[0]
    heads, tokens, model = spread_out.shape
    segs = groups.shape[1]
    block_rows = encoded.shape[0] // segs
    copies = weight_copies(
        core, ((first_mine, first_sibling), (second_mine, second_sibling)), kept, weight_sems
    )
    for copy in copies[:4]:
        copy.start()
    row_moves = row_copies(encoded, rows_ref, sems, segs)
    for copy in row_moves:
        copy.start()
    for copy in copies[4:]:
        copy.start()
    normed = low(normalize(after_self[...], gains[1:2, :]))
    for copy in copies[:4]:
        copy.wait()
    queries[...] = low(times(normed, kept, 0))
    for j in range(heads // 2):
        block = queries[:, j * PAIR : (j + 1) * PAIR] * jnp.bfloat16(0.125)
        spread = low(contract(pair_rows(block), pair_weight(kept, 1, j), 1, 1))
        spread_out[2 * j] = spread[:tokens]
        spread_out[2 * j + 1] = spread[tokens:]
    for copy in row_moves:
        copy.wait()

    def segment(s, begin):
        end = begin + segment_length(ids, s)
        base = pl.multiple_of(groups[0, s] * block_rows, block_rows)

        def chunk(c, carry):
            token = pl.multiple_of(c * CHUNK, CHUNK)
            rows = rows_ref[pl.ds(base, block_rows), :]
            left = spread_out[:, pl.ds(token, CHUNK), :].reshape(heads * CHUNK, model)
            scores = contract(left, rows, 1, 1)
            weights = jnp.exp(scores - jnp.max(scores, axis=-1, keepdims=True))
            totals = jnp.sum(weights, axis=-1, keepdims=True)
            probs = low(weights * (1.0 / totals))
            mixed = low(contract(probs, rows, 1, 0))
            inside = in_segment(token, begin, end, heads)
            at = (slice(None), pl.ds(token, CHUNK), slice(None))
            probs = probs.reshape(heads, CHUNK, block_rows)
            mixed = mixed.reshape(heads, CHUNK, model)
            probs_out[at] = jnp.where(inside, probs, probs_out[at])
            mixed_out[at] = jnp.where(inside, mixed, mixed_out[at])
            return carry

        lax.fori_loop(begin >> 4, (end + CHUNK - 1) >> 4, chunk, 0)
        return end

    lax.fori_loop(0, segs, segment, 0)
    for copy in copies[4:]:
        copy.wait()
    for j in range(heads // 2):
        both = jnp.concatenate([mixed_out[2 * j], mixed_out[2 * j + 1]], axis=0)
        found = contract(both, pair_weight(kept, 2, j), 1, 0)
        context[:, j * PAIR : (j + 1) * PAIR] = low(pair_lanes(found))
    after_cross[...] = after_self[...] + times(context[...], kept, 3)
    normed_out[...] = low(normalize(after_cross[...], gains[2:3, :]))


def cross_backward_first(
    core_ref, after_cross, gains, cotangent, pull_mine, pull_theirs, context, mixed, second_mine, second_sibling,
    grad_after, gain_grad, grad_context_out, pulled_ref, grad_mine, grad_other,
    kept, held, weight_sems, out_sems,
):
    core = core_ref[0]
    heads, tokens, model = pulled_ref.shape
    copies = weight_copies(core, ((second_mine, second_sibling),), kept, weight_sems)
    for copy in copies[2:] + copies[:2]:
        copy.start()
    grad_normed = pull_mine[...] + pull_theirs[...].astype(jnp.float32)
    grad_values, found_gain = norm_backward(after_cross[...], gains[2:3, :], grad_normed)
    grad_after[...] = cotangent[...].astype(jnp.float32) + grad_values
    gain_grad[0:1, :] = found_gain
    branch = low(grad_after[...])
    grad_into(context[...], branch, held, 1)
    started = []

    def send(number):
        for copy in grad_copies(core, (grad_mine, grad_other), held, number, out_sems):
            copy.start()
            started.append(copy)

    send(1)
    for copy in copies[2:] + copies[:2]:
        copy.wait()
    grad_context_out[...] = low(times_back(branch, kept, 1))
    per_half = held.shape[-1] // PAIR
    for j in range(heads // 2):
        columns = slice((j % per_half) * PAIR, (j % per_half + 1) * PAIR)
        rows = pair_rows(grad_context_out[:, j * PAIR : (j + 1) * PAIR])
        both = jnp.concatenate([mixed[2 * j], mixed[2 * j + 1]], axis=0)
        held[0, j // per_half, :, columns] = low(contract(both, rows, 0, 0))
        pulled = low(contract(rows, pair_weight(kept, 0, j), 1, 1))
        pulled_ref[2 * j] = pulled[:tokens]
        pulled_ref[2 * j + 1] = pulled[tokens:]
    send(0)
    for copy in started:
        copy.wait()


def cross_backward_second(
    core_ref, ids, groups, grad_after, after_self, gains, ffn_gain_grad, queries, encoded,
    probs_ref, pulled_ref, first_mine, first_sibling,
    grad_self, gain_grads, score_out, grad_mine, grad_other,
    rows_ref, moved_ref, kept, held, sems, weight_sems, out_sems,
):
    core = core_ref[0]
    heads, tokens, model = pulled_ref.shape
    segs = groups.shape[1]
    block_rows = encoded.shape[0] // segs
    half = kept.shape[-1]
    row_moves = row_copies(encoded, rows_ref, sems, segs)
    for copy in row_moves:
        copy.start()
    copies = weight_copies(core, ((first_mine, first_sibling),), kept, weight_sems)
    for copy in copies:
        copy.start()
    started = []

    def send(number):
        for copy in grad_copies(core, (grad_mine, grad_other), held, number, out_sems):
            copy.start()
            started.append(copy)

    for copy in row_moves:
        copy.wait()

    def segment(s, begin):
        end = begin + segment_length(ids, s)
        base = pl.multiple_of(groups[0, s] * block_rows, block_rows)

        def chunk(c, carry):
            token = pl.multiple_of(c * CHUNK, CHUNK)
            at = (slice(None), pl.ds(token, CHUNK), slice(None))
            rows = rows_ref[pl.ds(base, block_rows), :]
            inside = in_segment(token, begin, end, heads)
            pulled = jnp.where(inside, pulled_ref[at], jnp.zeros((), jnp.bfloat16))
            pulled = pulled.reshape(heads * CHUNK, model)
            probs = probs_ref[at].reshape(heads * CHUNK, block_rows)
            prob_grad = contract(pulled, rows, 1, 1)
            wide = probs.astype(jnp.float32)
            inner = jnp.sum(wide * prob_grad, axis=-1, keepdims=True)
            score_grad = low(wide * (prob_grad - inner))
            moved = low(contract(score_grad, rows, 1, 0)).reshape(heads, CHUNK, model)
            moved_ref[at] = jnp.where(inside, moved, moved_ref[at])
            score_grad = score_grad.reshape(heads, CHUNK, block_rows)
            score_out[at] = jnp.where(inside, score_grad, score_out[at])
            return carry

        lax.fori_loop(begin >> 4, (end + CHUNK - 1) >> 4, chunk, 0)
        return end

    lax.fori_loop(0, segs, segment, 0)
    for copy in copies:
        copy.wait()
    found = []
    per_half = half // PAIR
    for j in range(heads // 2):
        columns = slice((j % per_half) * PAIR, (j % per_half + 1) * PAIR)
        both = jnp.concatenate([moved_ref[2 * j], moved_ref[2 * j + 1]], axis=0)
        found.append(low(pair_lanes(contract(both, pair_weight(kept, 1, j), 1, 0)) * 0.125))
        block = queries[:, j * PAIR : (j + 1) * PAIR] * jnp.bfloat16(0.125)
        held[1, j // per_half, :, columns] = low(contract(both, pair_rows(block), 0, 0))
    send(1)
    grad_queries = jnp.concatenate(found, axis=1)
    values = after_self[...]
    grad_into(low(normalize(values, gains[1:2, :])), grad_queries, held, 0)
    send(0)
    grad_values, grad_gain = norm_backward(values, gains[1:2, :], times_back(grad_queries, kept, 0))
    grad_self[...] = grad_after[...] + grad_values
    gain_grads[0:1, :] = grad_gain
    gain_grads[1:2, :] = ffn_gain_grad[0:1, :]
    for copy in started:
        copy.wait()


def rows_backward_kernel(
    ids, groups, score_grads, probs_ref, spread, pulled_ref, grad_rows, sum_ref, row_sems,
):
    heads, tokens, model = spread.shape
    segs = groups.shape[1]
    block_rows = grad_rows.shape[0] // segs

    def write_out(s):
        slot = s & 1
        base = pl.multiple_of(groups[0, s] * block_rows, block_rows)
        return pltpu.make_async_copy(
            sum_ref.at[slot], grad_rows.at[pl.ds(base, block_rows)], row_sems.at[slot]
        )

    def segment(s, begin):
        end = begin + segment_length(ids, s)
        slot = s & 1

        @pl.when(s >= 2)
        def _():
            write_out(s - 2).wait()

        def terms(c):
            token = pl.multiple_of(c * CHUNK, CHUNK)
            at = (slice(None), pl.ds(token, CHUNK), slice(None))
            inside = in_segment(token, begin, end, heads)
            zero = jnp.zeros((), jnp.bfloat16)
            scores = jnp.where(inside, score_grads[at], zero).reshape(heads * CHUNK, block_rows)
            left = jnp.concatenate([scores, probs_ref[at].reshape(heads * CHUNK, block_rows)], axis=0)
            right = jnp.concatenate(
                [jnp.where(inside, piece[at], zero).reshape(heads * CHUNK, model) for piece in (spread, pulled_ref)],
                axis=0,
            )
            return contract(left, right, 0, 0)

        def chunk(c, carry):
            sum_ref[slot] += terms(c)
            return carry

        first = begin >> 4
        sum_ref[slot] = terms(first)
        lax.fori_loop(first + 1, (end + CHUNK - 1) >> 4, chunk, 0)
        write_out(s).start()
        return end

    lax.fori_loop(0, segs, segment, 0)
    for s in range(segs - 2, segs):
        write_out(s).wait()


def gelu_both(values):
    scale = 0.7978845608028654
    square = values * values
    bend = jnp.tanh(scale * (values + 0.044715 * (square * values)))
    half = 0.5 * (1.0 + bend)
    slope = half + 0.5 * values * (1.0 - bend * bend) * (scale * (1.0 + 3.0 * 0.044715 * square))
    return values * half, slope


def ffn_kernel(
    direct,
    core_ref, normed, normed_theirs, cotangent, cotangent_theirs, *refs,
):
    if direct:
        mine, sibling = refs[:2]
        rows = mine.shape[1] // 2
        sources = ((mine.at[:, :rows], sibling.at[:, :rows]), (mine.at[:, rows:], sibling.at[:, rows:]))
    else:
        sources = refs[:2]
    out_mine, out_other, pull_mine, pull_other, grad_mine, grad_other = refs[2:8]
    kept_in, kept_down, held_in, held_down, sems, out_sems = refs[8:]
    core = core_ref[0]
    blocks, groups, unused, width = kept_in.shape
    model = kept_in.shape[1] * kept_in.shape[2]
    count = normed.shape[0]
    if direct:
        copies = [
            pltpu.make_async_copy(source, target, sems.at[n])
            for n, (source, target) in enumerate(
                (
                    (sources[0][0], kept_in.at[core]),
                    (sources[1][0], kept_down.at[:, core]),
                    (sources[0][1], kept_in.at[1 - core]),
                    (sources[1][1], kept_down.at[:, 1 - core]),
                )
            )
        ]
    else:
        copies = [
            pltpu.make_async_copy(source, target, sems.at[n])
            for n, (source, target) in enumerate(zip(sources, (kept_in, kept_down)))
        ]
    for copy in copies:
        copy.start()
    tokens = jnp.concatenate([normed[...], normed_theirs[...]], axis=0)
    pull = jnp.concatenate([cotangent[...], cotangent_theirs[...]], axis=0)
    for copy in copies:
        copy.wait()
    total = grad_tokens = None
    started = []
    for b in range(blocks):
        weight_up = kept_in[b].reshape(model, width)
        part = slice(b * groups // blocks, (b + 1) * groups // blocks) if direct else slice(0, 1)
        if direct:
            weight_down = kept_down[part].reshape(width, model)
        else:
            weight_down = kept_down[0, 0, b * width : (b + 1) * width]
        activated, slope = gelu_both(contract(tokens, weight_up, 1, 0))
        activated = low(activated)
        grad_act = low(contract(pull, weight_down, 1, 1)).astype(jnp.float32)
        grad_pre = low(slope * grad_act)
        added = contract(grad_pre, weight_up, 1, 1)
        grad_tokens = added if b == 0 else grad_tokens + added
        added = contract(activated, weight_down, 1, 0)
        total = added if b == 0 else total + added
        held_in[b] = low(contract(tokens, grad_pre, 0, 0)).reshape(held_in.shape[1:])
        grad_down = low(contract(activated, pull, 0, 0))
        if direct:
            held_down[part] = grad_down.reshape((groups // blocks,) + held_down.shape[1:])
        else:
            held_down[0, 0, b * width : (b + 1) * width] = grad_down
    if direct:
        targets = (
            (held_in.at[1 - core], grad_other.at[:, :rows]),
            (held_down.at[:, 1 - core], grad_other.at[:, rows:]),
            (held_in.at[core], grad_mine.at[:, :rows]),
            (held_down.at[:, core], grad_mine.at[:, rows:]),
        )
    else:
        targets = ((held_in, grad_mine), (held_down, grad_other))
    started = [pltpu.make_async_copy(source, target, out_sems.at[n]) for n, (source, target) in enumerate(targets)]
    for copy in started:
        copy.start()
    out_mine[...] = total[:count]
    out_other[...] = low(total[count:])
    pull_mine[...] = grad_tokens[:count]
    pull_other[...] = low(grad_tokens[count:])
    for copy in started:
        copy.wait()

AXES = ("dp", "fsdp")


def swap_with(piece, mask, devices):
    pairs = [(index, index ^ mask) for index in range(devices)]
    return lax.ppermute(piece, AXES, pairs)


def bit_of(me, bit):
    return (me >> bit) & 1


def pair_up(mine, theirs, my_bit, axis):
    first = jnp.where(my_bit == 0, mine, theirs)
    second = jnp.where(my_bit == 0, theirs, mine)
    return jnp.stack([first, second], axis=axis)


def arranged(found, bits, me):
    found = {mask: [block] for mask, block in found.items()}
    for n, bit in enumerate(sorted(bits)):
        low_side = bit_of(me, bit) == 0
        merged = {}
        for mask in found:
            if not mask >> n & 1:
                both = list(zip(found[mask], found[mask | 1 << n]))
                merged[mask] = [jnp.where(low_side, x, y) for x, y in both] + [
                    jnp.where(low_side, y, x) for x, y in both
                ]
        found = merged
    return jnp.stack(found[0])


def wide_mask(mask, bits):
    return sum(1 << bit for n, bit in enumerate(sorted(bits)) if mask >> n & 1)


def exchange(send, bits, me, devices):
    found = {0: send(0)}
    for mask in range(1, 1 << len(bits)):
        found[mask] = swap_with(send(mask), wide_mask(mask, bits), devices)
    return arranged(found, bits, me)


def gather_line(block, bits, me, devices):
    if len(bits) > 2:
        held = block[None]
        for bit in sorted(bits):
            theirs = swap_with(held, 1 << bit, devices)
            held = pair_up(held, theirs, bit_of(me, bit), 0).reshape((-1,) + block.shape)
        return held
    return exchange(lambda mask: block, bits, me, devices)


def taken(source, places, columns):
    array, bits, offset = source
    begin = [places[bit] if bit in places else 0 for bit in bits] + [0, offset + columns[0]]
    size = [1 if bit in places else 2 for bit in bits] + [array.shape[-2], columns[1] - columns[0]]
    part = lax.dynamic_slice(array, begin, size)
    return part.reshape([2 for bit in bits if bit not in places] + size[-2:])


def summed(entry, places):
    sources, columns = entry
    total = None
    for source in sources:
        part = taken(source, places, columns).astype(jnp.float32)
        total = part if total is None else total + part
    return total


def sum_over(entries, bit, done, me, devices):
    places = {other: bit_of(me, other) for other in done}
    send = [low(summed(entry, {**places, bit: 1 - bit_of(me, bit)})) for entry in entries]
    theirs = swap_with(jnp.concatenate(send, axis=-1), 1 << bit, devices)
    found, at = [], 0
    for sources, columns in entries:
        bits = [other for other in sources[0][1] if other not in done and other != bit]
        found.append((sources + [(theirs, bits, at - columns[0])], columns))
        at += columns[1] - columns[0]
    return found


def sum_line(stacks, bits, done, me, devices):
    places = {bit: bit_of(me, bit) for bit in done}

    def block(line):
        return jnp.concatenate(
            [jnp.concatenate([summed(entry, {**places, **line}) for entry in entries], axis=-1) for entries in stacks],
            axis=-2,
        )

    mine = {bit: bit_of(me, bit) for bit in bits}
    total = None
    for mask in range(1, 1 << len(bits)):
        wide = wide_mask(mask, bits)
        send = low(block({bit: mine[bit] ^ (wide >> bit & 1) for bit in bits}))
        theirs = swap_with(send, wide, devices).astype(jnp.float32)
        total = theirs if total is None else total + theirs
    return block(mine) + total


def core_rows(total, core, devices):
    rows = total.shape[0] // 2
    keep = lax.dynamic_slice_in_dim(total, core * rows, rows, axis=0)
    send = lax.dynamic_slice_in_dim(total, (1 - core) * rows, rows, axis=0)
    theirs = swap_with(send, 1, devices)
    return jnp.where(core == 0, keep, theirs), jnp.where(core == 0, theirs, keep)


VMEM = pl.BlockSpec(memory_space=pltpu.VMEM)
SMEM = pl.BlockSpec(memory_space=pltpu.SMEM)
HBM = pl.BlockSpec(memory_space=pl.ANY)


def shaped(shape, dtype):
    return jax.ShapeDtypeStruct(shape, dtype)


def call(kernel, name, flops, in_specs, out_specs, out_shape, scratch, aliases={}):
    return pl.pallas_call(
        kernel,
        out_shape=out_shape,
        in_specs=in_specs,
        out_specs=out_specs,
        scratch_shapes=scratch,
        compiler_params=pltpu.CompilerParams(vmem_limit_bytes=VMEM_BYTES),
        cost_estimate=pl.CostEstimate(flops=flops, bytes_accessed=1_000_000, transcendentals=0),
        name=name,
        input_output_aliases=aliases,
    )


def per_device(
    fsdp,
    devices,
    tokens,
    encoded,
    segment_ids,
    passage_group,
    cotangent,
    self_gain,
    cross_gain,
    ffn_gain,
    self_query,
    self_key,
    self_value,
    self_out,
    cross_query,
    cross_key,
    cross_value,
    cross_out,
    ffn_in,
    ffn_out,
):
    me = lax.axis_index("dp") * fsdp + lax.axis_index("fsdp")
    core = bit_of(me, 0)
    core_word = core.reshape(1).astype(jnp.int32)
    chip_bits = list(range(1, devices.bit_length() - 1))
    line_bits = [bit for bit in reversed(chip_bits) if bit > 2]
    pair_orders = ([2, 1], [1, 2])
    count, model = tokens.shape
    encoder_count = encoded.shape[0]
    hidden_units = ffn_in.shape[1]
    heads = model // HEAD
    half = model // 2
    segs = passage_group.shape[1]
    low_type, wide_type = jnp.bfloat16, jnp.float32

    def my_columns(matrix, owner):
        width = matrix.shape[-1] // 2
        return lax.dynamic_slice_in_dim(matrix, owner * width, width, axis=matrix.ndim - 1)

    barrier = lax.optimization_barrier
    gains = jnp.stack([self_gain, cross_gain, ffn_gain], axis=1)
    gains = jnp.pad(gains, ((0, 0), (0, PAIR - 3)))
    shards = [self_query, self_key, self_value, self_out, cross_query, cross_key, cross_value, cross_out]
    packed = shaped((self_query.shape[0], len(shards) * half + PAIR), low_type)
    send, keep = call(
        pack_kernel, "pack", 0, [SMEM] + [VMEM] * 9, [VMEM] * 2, (packed, packed), []
    )(core_word, *shards, gains)
    theirs = swap_with(send, 1, devices)
    chip_block = pair_up(keep, theirs, core, 0).reshape(-1, keep.shape[1])
    self_block = jnp.concatenate([chip_block[:, : 2 * model], chip_block[:, 4 * model :]], axis=1)
    cross_block = chip_block[:, 2 * model : 4 * model]

    def double(held, bit, first_bit, me):
        place = 1 if first_bit is None or bit > first_bit else 2
        return pair_up(held, swap_with(held, 1 << bit, devices), bit_of(me, bit), place)

    def first_step(line, width):
        return [double(part, order[0], None, me) for part, order in zip((line[:, :, :width], line[:, :, width:]), pair_orders)]

    def second_step(parts):
        return [
            double(part, order[1], order[0], me).reshape(-1, part.shape[-1])
            for part, order in zip(parts, pair_orders)
        ]

    rows_in = ffn_in.shape[0]
    rows_down = ffn_out.shape[0]
    direct = rows_down % 16 == 0
    chip_groups = devices // 4
    group_bits = [0, 1]
    cotangent_theirs = swap_with(cotangent, 2, devices)
    in_blocks = ffn_in.reshape(rows_in, 2, chip_groups // 2, 2, 2 * rows_down)
    in_blocks = in_blocks.transpose(3, 1, 0, 2, 4).reshape(2, 2, rows_in, model)

    def block_for(array, mask):
        first = [bit_of(me, 1) ^ (mask >> 1 & 1), core ^ (mask & 1)]
        return lax.dynamic_slice(array, first + [0, 0], (1, 1) + array.shape[2:]).reshape(array.shape[2:])

    self_line = gather_line(self_block, line_bits, me, devices)
    self_line, cross_block, in_blocks = barrier((self_line, cross_block, in_blocks))
    in_rows = exchange(lambda mask: block_for(in_blocks, mask), group_bits, me, devices)
    ffn_block = jnp.concatenate([in_rows.reshape(4 * rows_in, model), ffn_out], axis=0)
    self_parts = first_step(self_line, model)
    cross_line = gather_line(cross_block, line_bits, me, devices)
    ffn_steps = line_bits + [2]

    def ffn_step(held, number):
        bit = ffn_steps[number]
        place = sum(1 for other in ffn_steps[:number] if other > bit)
        return pair_up(held, swap_with(held, 1 << bit, devices), bit_of(me, bit), place)

    self_parts, cross_line, ffn_held = barrier((self_parts, cross_line, ffn_block))
    self_mine = second_step(self_parts)
    cross_parts = first_step(cross_line, model)
    for number in range(len(line_bits) - 1):
        ffn_held = ffn_step(ffn_held, number)
    cross_parts, ffn_held, self_mine = barrier((cross_parts, ffn_held, self_mine))
    cross_mine = second_step(cross_parts)
    ffn_held = ffn_step(ffn_held, len(line_bits) - 1)
    self_weights = [(mine, swap_with(mine[:, :model], 1, devices)) for mine in self_mine]

    gain_rows = self_weights[1][0][:, model : model + 8].T.astype(wide_type)
    self_flat = self_weights[0] + self_weights[1]

    dma = pltpu.SemaphoreType.DMA
    weights_kept = pltpu.VMEM((4, 2, model, half), low_type)
    projected, context_one, after_self = call(
        self_forward_kernel,
        "self_forward",
        2 * count * model * model * 5,
        [SMEM, VMEM, VMEM, VMEM] + [HBM] * 4,
        [VMEM] * 3,
        (
            shaped((3, count, model), low_type),
            shaped((count, model), low_type),
            shaped((count, model), wide_type),
        ),
        [weights_kept, dma((8,))],
    )(core_word, segment_ids, tokens, gain_rows, *self_flat)

    cross_mine, ffn_held, after_self, cotangent_theirs = barrier(
        (cross_mine, ffn_held, after_self, cotangent_theirs)
    )
    ffn_theirs = swap_with(ffn_held, 4, devices)
    cross_weights = [(mine, swap_with(mine, 1, devices)) for mine in cross_mine]
    cross_flat = cross_weights[0] + cross_weights[1]

    per_token = (heads, count, model)
    probs_shape = (heads, count, encoder_count // segs)
    queries_two, context_two, after_cross, normed_three, probs, mixed, spread = call(
        cross_forward_kernel,
        "cross_forward",
        12_000_000_000,
        [SMEM, SMEM, SMEM, VMEM, VMEM] + [HBM] * 5,
        [VMEM] * 7,
        (
            shaped((count, model), low_type),
            shaped((count, model), low_type),
            shaped((count, model), wide_type),
            shaped((count, model), low_type),
            shaped(probs_shape, low_type),
            shaped(per_token, low_type),
            shaped(per_token, low_type),
        ),
        [pltpu.VMEM(encoded.shape, low_type), weights_kept, dma((segs,)), dma((8,))],
    )(core_word, segment_ids, passage_group, after_self, gain_rows, encoded, *cross_flat)

    ffn_theirs, normed_three = barrier((ffn_theirs, normed_three))
    normed_theirs = swap_with(normed_three, 2, devices)
    ffn_mine = pair_up(ffn_held, ffn_theirs, bit_of(me, 2), len(line_bits)).reshape(chip_groups, -1, model)
    ffn_sibling = swap_with(ffn_mine, 1, devices)
    half_units = hidden_units // 2
    if direct:
        in_shape = (2, chip_groups, rows_down, model)
        down_shape = (chip_groups, 2, rows_down, model)
        ffn_weights = (ffn_mine, ffn_sibling)
        grad_shapes = (shaped(ffn_mine.shape, low_type),) * 2
    else:
        in_shape, down_shape = (2, 1, model, model), (1, 1, half_units, model)
        both = pair_up(ffn_mine, ffn_sibling, core, 0)
        ffn_weights = (
            both[:, :, : 4 * rows_in].reshape(in_shape),
            both[:, :, 4 * rows_in :].swapaxes(0, 1).reshape(down_shape),
        )
        grad_shapes = (shaped(in_shape, low_type), shaped(down_shape, low_type))
    token_shapes = (shaped((count, model), wide_type), shaped((count, model), low_type))
    out_mine, out_other, pull_mine, pull_other, ffn_grad, ffn_other = call(
        functools.partial(ffn_kernel, direct),
        "ffn",
        4_000_000_000,
        [SMEM] + [VMEM] * 4 + [HBM] * 2,
        [VMEM] * 4 + [HBM] * 2,
        token_shapes + token_shapes + grad_shapes,
        [
            pltpu.VMEM(in_shape, low_type),
            pltpu.VMEM(down_shape, low_type),
            pltpu.VMEM(in_shape, low_type),
            pltpu.VMEM(down_shape, low_type),
            dma((4,)),
            dma((4,)),
        ],
    )(core_word, normed_three, normed_theirs, cotangent, cotangent_theirs, *ffn_weights)
    pull_theirs = swap_with(pull_other, 2, devices)
    if not direct:
        in_parts = ffn_grad.reshape(2, chip_groups, 4 * rows_in, model)
        down_parts = ffn_other.reshape(chip_groups, 2, rows_down, model).swapaxes(0, 1)
        both = jnp.concatenate([in_parts, down_parts], axis=2)
        ffn_grad, ffn_other = (
            lax.dynamic_index_in_dim(both, place, 0, keepdims=False) for place in (core, 1 - core)
        )
    ffn_theirs = swap_with(ffn_other, 1, devices)
    pull_theirs, ffn_theirs = barrier((pull_theirs, ffn_theirs))
    out_theirs = swap_with(out_other, 2, devices)
    high_bits = [bit for bit in sorted(chip_bits, reverse=True) if bit > 1]

    def group_source(array):
        return (array.reshape((2,) * len(high_bits) + array.shape[-2:]), high_bits, 0)

    ffn_sum = sum_over([([group_source(ffn_grad), group_source(ffn_theirs)], (0, model))], 2, [], me, devices)

    all_bits = sorted(chip_bits, reverse=True)

    def chips_of(array):
        return array.reshape((2,) * len(all_bits) + (array.shape[0] >> len(all_bits), array.shape[-1]))

    def entry_of(mine, theirs, begin, end):
        return ([(chips_of(mine), all_bits, 0), (chips_of(theirs), all_bits, 0)], (begin, end))

    def first_sum(sides):
        return [sum_over(entries, order[0], [], me, devices) for entries, order in zip(sides, pair_orders)]

    def second_sum(sides):
        return [sum_over(entries, order[1], order[:1], me, devices) for entries, order in zip(sides, pair_orders)]

    def received(sides):
        return [entries[0][0][-1][0] for entries in sides]

    def with_received(sides, arrays):
        return [
            [(sources[:-1] + [(array,) + sources[-1][1:]], columns) for sources, columns in entries]
            for entries, array in zip(sides, arrays)
        ]

    grads_shape = shaped((model, model), low_type)
    rows_kept = pltpu.VMEM(encoded.shape, low_type)
    two_kept = pltpu.VMEM((2, 2, model, half), low_type)
    grad_after_cross, ffn_gain_grad, grad_context, pulled, late_mine, late_other = call(
        cross_backward_first,
        "cross_backward_first",
        1_000_000_000,
        [SMEM] + [VMEM] * 7 + [HBM] * 2,
        [VMEM] * 4 + [HBM] * 2,
        (
            shaped((count, model), wide_type),
            shaped((8, model), wide_type),
            shaped((count, model), low_type),
            shaped(per_token, low_type),
            grads_shape,
            grads_shape,
        ),
        [two_kept, two_kept, dma((4,)), dma((4,))],
    )(
        core_word, after_cross, gain_rows, cotangent, pull_mine, pull_theirs, context_two, mixed, *cross_weights[1]
    )
    late_theirs = swap_with(late_other, 1, devices)
    block_out = low(after_cross + (out_mine + out_theirs.astype(wide_type)))
    grad_after_self, gain_grads, score_grads, early_mine, early_other = call(
        cross_backward_second,
        "cross_backward_second",
        3_000_000_000,
        [SMEM, SMEM, SMEM] + [VMEM] * 5 + [HBM] + [VMEM] * 2 + [HBM] * 2,
        [VMEM] * 3 + [HBM] * 2,
        (
            shaped((count, model), wide_type),
            shaped((8, model), wide_type),
            shaped(probs_shape, low_type),
            grads_shape,
            grads_shape,
        ),
        [rows_kept, pltpu.VMEM(per_token, low_type), two_kept, two_kept, dma((segs,)), dma((4,)), dma((4,))],
    )(
        core_word, segment_ids, passage_group, grad_after_cross, after_self, gain_rows, ffn_gain_grad,
        queries_two, encoded, probs, pulled, *cross_weights[0],
    )
    arrays, grad_after_self, early_mine, early_other = barrier(
        (received([ffn_sum]), grad_after_self, early_mine, early_other)
    )
    ffn_sum = with_received([ffn_sum], arrays)[0]
    ffn_done = [2]
    for bit in sorted(line_bits)[:-1]:
        ffn_sum = sum_over(ffn_sum, bit, ffn_done, me, devices)
        ffn_done = ffn_done + [bit]
    early_theirs = swap_with(early_other, 1, devices)

    with_gains = shaped((model, 2 * model + PAIR), low_type)
    tokens_grad, self_mine, self_other = call(
        self_backward_kernel,
        "self_backward",
        2 * count * model * model * 10,
        [SMEM] + [VMEM] * 7 + [HBM] * 4,
        [VMEM] + [HBM] * 2,
        (shaped((count, model), wide_type), with_gains, with_gains),
        [weights_kept, weights_kept, pltpu.VMEM((model, PAIR), low_type), dma((8,)), dma((10,))],
    )(
        core_word, segment_ids, tokens, gain_rows, grad_after_self, gain_grads, projected, context_one,
        *self_flat,
    )
    arrays, late_theirs, early_theirs, self_mine, self_other = barrier(
        (received([ffn_sum]), late_theirs, early_theirs, self_mine, self_other)
    )
    ffn_sum = with_received([ffn_sum], arrays)[0]
    ffn_sum = sum_over(ffn_sum, max(line_bits), ffn_done, me, devices)
    self_theirs = swap_with(self_other, 1, devices)
    crossed = [
        [entry_of(late_mine, late_theirs, *cut), entry_of(early_mine, early_theirs, *cut)]
        for cut in ((0, half), (half, model))
    ]
    crossed = first_sum(crossed)
    self_theirs, score_grads = barrier((self_theirs, score_grads))
    attention = [
        [entry_of(self_mine, self_theirs, *cut)] for cut in ((0, model), (model, 2 * model + PAIR))
    ]
    attention = first_sum(attention)
    encoded_grad = call(
        rows_backward_kernel,
        "rows_backward",
        3_000_000_000,
        [SMEM, SMEM] + [VMEM] * 4,
        HBM,
        shaped(encoded.shape, wide_type),
        [pltpu.VMEM((2, encoder_count // segs, model), wide_type), dma((2,))],
    )(segment_ids, passage_group, score_grads, probs, spread, pulled)
    crossed_arrays, arrays, ffn_arrays, encoded_grad = barrier(
        (received(crossed), received(attention), received([ffn_sum]), encoded_grad)
    )
    ffn_sum = with_received([ffn_sum], ffn_arrays)[0]
    ffn_rows = summed(ffn_sum[0], {bit: bit_of(me, bit) for bit in high_bits})
    summed_down = ffn_rows[4 * rows_in :]
    in_parts = ffn_rows[: 4 * rows_in].reshape(2, 2, rows_in, model)
    in_parts = exchange(lambda mask: block_for(in_parts, mask), group_bits, me, devices)
    in_parts = in_parts.reshape(2, 2, rows_in, chip_groups // 2, 2 * rows_down)
    summed_in = in_parts.transpose(2, 1, 3, 0, 4).reshape(rows_in, hidden_units)
    crossed, attention = with_received(crossed, crossed_arrays), with_received(attention, arrays)
    attention = second_sum([crossed[side] + attention[side] for side in range(2)])
    found = sum_line([attention[0] + attention[1]], line_bits, [2, 1], me, devices)
    pair = core_rows(found, core, devices)
    (
        summed_cv, summed_cq, summed_query, summed_key, summed_co, summed_ck, summed_value, summed_out,
    ) = (
        jnp.concatenate([piece[:, n * half : (n + 1) * half] for piece in pair], axis=1) for n in range(8)
    )
    own_gains = jnp.where(core == 0, pair[0][:, 8 * half :], pair[1][:, 8 * half :])
    return (
        block_out,
        tokens_grad,
        encoded_grad,
        own_gains[:, 0],
        own_gains[:, 1],
        own_gains[:, 2],
        summed_query,
        summed_key,
        summed_value,
        summed_out,
        summed_cq,
        summed_ck,
        summed_cv,
        summed_co,
        summed_in,
        summed_down,
    )


def solution(mesh):
    return jax.shard_map(
        functools.partial(per_device, mesh.shape["fsdp"], mesh.size),
        mesh=mesh,
        in_specs=(
            P(("dp", "fsdp"), None),
            P(("dp", "fsdp"), None),
            P(("dp", "fsdp"), None),
            P(("dp", "fsdp"), None),
            P(("dp", "fsdp"), None),
            P(("dp", "fsdp")),
            P(("dp", "fsdp")),
            P(("dp", "fsdp")),
            P(("dp", "fsdp"), None),
            P(("dp", "fsdp"), None),
            P(("dp", "fsdp"), None),
            P(("dp", "fsdp"), None),
            P(("dp", "fsdp"), None),
            P(("dp", "fsdp"), None),
            P(("dp", "fsdp"), None),
            P(("dp", "fsdp"), None),
            P(("dp", "fsdp"), None),
            P(("dp", "fsdp"), None),
        ),
        out_specs=(
            P(("dp", "fsdp"), None),
            P(("dp", "fsdp"), None),
            P(("dp", "fsdp"), None),
            P(("dp", "fsdp")),
            P(("dp", "fsdp")),
            P(("dp", "fsdp")),
            P(("dp", "fsdp"), None),
            P(("dp", "fsdp"), None),
            P(("dp", "fsdp"), None),
            P(("dp", "fsdp"), None),
            P(("dp", "fsdp"), None),
            P(("dp", "fsdp"), None),
            P(("dp", "fsdp"), None),
            P(("dp", "fsdp"), None),
            P(("dp", "fsdp"), None),
            P(("dp", "fsdp"), None),
        ),
        check_vma=False,
    )
```

```python
import functools

import jax
import jax.numpy as jnp
from jax import lax
from jax.experimental import pallas as pl
from jax.experimental.pallas import tpu as pltpu
from jax.sharding import PartitionSpec as P

HEAD = 64
CHUNK = 16
PAIR = 2 * HEAD
epsilon = 1e-06
masked_score = -1e30
VMEM_BYTES = 60 << 20
MIDDLE_BYTES = 32 << 20


def contract(left, right, left_dim, right_dim):
    return lax.dot_general(
        left, right, (((left_dim,), (right_dim,)), ((), ())), preferred_element_type=jnp.float32
    )


def low(values):
    return values.astype(jnp.bfloat16)


def normalize(values, gain_row):
    return values * lax.rsqrt(jnp.mean(values * values, axis=-1, keepdims=True) + epsilon) * gain_row


def norm_backward(values, gain_row, grad):
    scale = lax.rsqrt(jnp.mean(values * values, axis=-1, keepdims=True) + epsilon)
    grad_gain = jnp.sum(grad * values * scale, axis=0, keepdims=True)
    weighted = gain_row * grad
    inner = jnp.mean(weighted * values, axis=-1, keepdims=True)
    return scale * weighted - values * (scale * scale * scale) * inner, grad_gain


def pair_rows(block):
    lane = lax.broadcasted_iota(jnp.int32, block.shape, 1)
    zero = jnp.zeros_like(block)
    return jnp.concatenate(
        [jnp.where(lane < HEAD, block, zero), jnp.where(lane >= HEAD, block, zero)], axis=0
    )


def pair_lanes(both):
    rows = both.shape[0] // 2
    lane = lax.broadcasted_iota(jnp.int32, (rows, both.shape[1]), 1)
    return jnp.where(lane < HEAD, both[:rows], both[rows:])


def weight_copies(core, sources, kept, sems):
    half = kept.shape[-1]
    copies = []
    for number in range(kept.shape[0]):
        for side, source in enumerate(sources[number // 2]):
            place = core if side == 0 else 1 - core
            copies.append(
                pltpu.make_async_copy(
                    source.at[:, (number % 2) * half : (number % 2 + 1) * half],
                    kept.at[number, place],
                    sems.at[2 * number + side],
                )
            )
    return copies


def times(left, kept, number):
    return jnp.concatenate([contract(left, kept[number, side], 1, 0) for side in range(2)], axis=1)


def times_back(left, kept, number):
    half = kept.shape[-1]
    return contract(left[:, :half], kept[number, 0], 1, 1) + contract(left[:, half:], kept[number, 1], 1, 1)


def grad_into(left, right, held, number):
    half = held.shape[-1]
    for side in range(2):
        held[number, side] = low(contract(left, right[:, side * half : (side + 1) * half], 0, 0))


def grad_copies(core, targets, held, number, sems):
    half = held.shape[-1]
    copies = []
    for side, target in enumerate(targets):
        place = core if side == 0 else 1 - core
        copies.append(
            pltpu.make_async_copy(
                held.at[number, place],
                target.at[:, number * half : (number + 1) * half],
                sems.at[2 * number + side],
            )
        )
    return copies


def pack_kernel(core_ref, *refs):
    shards, gains, in_blocks, (send, keep) = refs[:-4], refs[-4], refs[-3], refs[-2:]
    core = core_ref[0]
    half = shards[0].shape[1] // 2
    for number, shard in enumerate(shards):
        for target, place in ((send, 1 - core), (keep, core)):
            target[:, number * half : (number + 1) * half] = shard[:, pl.ds(pl.multiple_of(place * half, PAIR), half)]
    at = len(shards) * half
    for target, place in ((send, 1 - core), (keep, core)):
        target[:, at : at + PAIR] = gains[...]
        for side in range(2):
            begin = at + PAIR + side * 2 * half
            target[:, begin : begin + 2 * half] = in_blocks[side, place]


def self_mask(ids_row):
    tokens = ids_row.shape[1]
    wide = jnp.broadcast_to(ids_row.astype(jnp.float32), (tokens, tokens))
    query = lax.broadcasted_iota(jnp.int32, (tokens, tokens), 0)
    key = lax.broadcasted_iota(jnp.int32, (tokens, tokens), 1)
    allowed = jnp.where((wide == wide.T) & (key <= query), 1.0, 0.0)
    return jnp.concatenate([allowed, allowed], axis=0) > 0.5


def self_probs(queries, keys, allowed):
    scores = jnp.where(allowed, contract(pair_rows(queries), keys, 1, 1) * 0.125, masked_score)
    weights = jnp.exp(scores - jnp.max(scores, axis=-1, keepdims=True))
    return weights / jnp.sum(weights, axis=-1, keepdims=True)


def self_forward_kernel(
    core_ref, ids, tokens, gains, first_mine, first_sibling, second_mine, second_sibling,
    projected, context, after, kept, sems,
):
    core = core_ref[0]
    copies = weight_copies(
        core, ((first_mine, first_sibling), (second_mine, second_sibling)), kept, sems
    )
    for copy in copies:
        copy.start()
    model = tokens.shape[1]
    hidden = tokens[...].astype(jnp.float32)
    normed = low(normalize(hidden, gains[0:1, :]))
    for number in range(3):
        copies[2 * number].wait()
        copies[2 * number + 1].wait()
        projected[number] = low(times(normed, kept, number))
    allowed = self_mask(ids[...])
    for j in range(model // PAIR):
        columns = slice(j * PAIR, (j + 1) * PAIR)
        probs = self_probs(projected[0, :, columns], projected[1, :, columns], allowed)
        context[:, columns] = low(pair_lanes(contract(low(probs), projected[2, :, columns], 1, 0)))
    copies[6].wait()
    copies[7].wait()
    after[...] = hidden + times(context[...], kept, 3)


def self_backward_kernel(
    core_ref, ids, tokens, gains, grad_after, gain_grads, projected, context,
    first_mine, first_sibling, second_mine, second_sibling,
    tokens_grad, grad_mine, grad_other,
    kept, held, gain_held, sems, out_sems,
):
    core = core_ref[0]
    copies = weight_copies(
        core, ((first_mine, first_sibling), (second_mine, second_sibling)), kept, sems
    )
    for copy in copies:
        copy.start()
    model = tokens.shape[1]
    count = tokens.shape[0]
    hidden = tokens[...].astype(jnp.float32)
    normed = low(normalize(hidden, gains[0:1, :]))
    branch = low(grad_after[...])
    started = []

    def send(number):
        for copy in grad_copies(core, (grad_mine, grad_other), held, number, out_sems):
            copy.start()
            started.append(copy)

    grad_into(context[...], branch, held, 3)
    send(3)
    for copy in copies:
        copy.wait()
    grad_context = low(times_back(branch, kept, 3))
    allowed = self_mask(ids[...])
    found = ([], [], [])
    for j in range(model // PAIR):
        columns = slice(j * PAIR, (j + 1) * PAIR)
        queries, keys = projected[0, :, columns], projected[1, :, columns]
        probs = self_probs(queries, keys, allowed)
        pulled = pair_rows(grad_context[:, columns])
        prob_grad = contract(pulled, projected[2, :, columns], 1, 1)
        inner = jnp.sum(probs * prob_grad, axis=-1, keepdims=True)
        score_grad = low(probs * (prob_grad - inner))
        found[0].append(low(pair_lanes(contract(score_grad, keys, 1, 0)) * 0.125))
        found[1].append(low(contract(score_grad, pair_rows(queries), 0, 0) * 0.125))
        found[2].append(low(contract(low(probs), pulled, 0, 0)))
    grad_normed = None
    for number in range(3):
        whole = jnp.concatenate(found[number], axis=1)
        grad_into(normed, whole, held, number)
        send(number)
        part = times_back(whole, kept, number)
        grad_normed = part if grad_normed is None else grad_normed + part
    grad_hidden, grad_gain = norm_backward(hidden, gains[0:1, :], grad_normed)
    tokens_grad[...] = grad_after[...] + grad_hidden
    row = lax.broadcasted_iota(jnp.int32, (count, model), 0)
    others = gain_grads[...]
    wide = jnp.where(
        row == 0, grad_gain, jnp.where(row == 1, others[0:1], jnp.where(row == 2, others[1:2], 0.0))
    )
    gain_held[...] = low(wide.T)
    for slot, target in enumerate((grad_mine, grad_other)):
        copy = pltpu.make_async_copy(gain_held, target.at[:, 2 * model :], out_sems.at[8 + slot])
        copy.start()
        started.append(copy)
    for copy in started:
        copy.wait()


def row_copies(encoded, rows_ref, sems, segs):
    size = encoded.shape[0] // segs
    return [
        pltpu.make_async_copy(
            encoded.at[pl.ds(s * size, size)], rows_ref.at[pl.ds(s * size, size)], sems.at[s]
        )
        for s in range(segs)
    ]


def block_copy(encoded, rows_ref, sems, groups, s):
    size = encoded.shape[0] // groups.shape[1]
    at = pl.ds(pl.multiple_of(groups[0, s] * size, size), size)
    return pltpu.make_async_copy(encoded.at[at], rows_ref.at[at], sems.at[s])


def chunk_copies(pairs, sems, c):
    at = (slice(None), pl.ds(pl.multiple_of(c * CHUNK, CHUNK), CHUNK), slice(None))
    return [pltpu.make_async_copy(source.at[at], target.at[at], sems.at[n, c]) for n, (source, target) in enumerate(pairs)]


def list_chunks(starts, table):
    def query(s, count):
        begin, end = starts[0, s], starts[0, s + 1]

        def chunk(c, count):
            table[0, count] = c * CHUNK
            table[1, count] = s
            table[2, count] = (c == begin >> 4).astype(jnp.int32)
            table[3, count] = ((c * CHUNK >= begin) | (begin & (CHUNK - 1) == 0)).astype(jnp.int32)
            return count + 1

        return lax.fori_loop(begin >> 4, (end + CHUNK - 1) >> 4, chunk, count)

    return lax.fori_loop(0, starts.shape[1] - 1, query, 0)


def listed(starts, table, at):
    s = table[1, at]
    return pl.multiple_of(table[0, at], CHUNK), s, starts[0, s], starts[0, s + 1]


def in_segment(token, begin, end, heads):
    row = lax.broadcasted_iota(jnp.int32, (heads, CHUNK, 1), 1) + token
    return (row >= begin) & (row < end)


def pair_weight(kept, number, j):
    per_half = kept.shape[-1] // PAIR
    return kept[number, j // per_half, :, (j % per_half) * PAIR : (j % per_half + 1) * PAIR]


def cross_forward_kernel(
    core_ref, starts, groups, after_self, gains, encoded,
    first_mine, first_sibling, second_mine, second_sibling,
    queries, context, after_cross, normed_out, probs_hbm, mixed_hbm, spread_hbm,
    probs_out, mixed_out, spread_out, rows_ref, kept, table, sems, weight_sems, out_sems,
):
    core = core_ref[0]
    heads, tokens, model = spread_out.shape
    segs = groups.shape[1]
    block_rows = encoded.shape[0] // segs
    copies = weight_copies(
        core, ((first_mine, first_sibling), (second_mine, second_sibling)), kept, weight_sems
    )
    for copy in copies[:4]:
        copy.start()
    for s in range(segs):
        block_copy(encoded, rows_ref, sems, groups, s).start()
    leaving = [
        pltpu.make_async_copy(source, target, out_sems.at[n])
        for n, (source, target) in enumerate(
            ((spread_out, spread_hbm), (probs_out, probs_hbm), (mixed_out, mixed_hbm))
        )
    ]
    for copy in copies[4:]:
        copy.start()
    normed = low(normalize(after_self[...], gains[1:2, :]))
    for copy in copies[:4]:
        copy.wait()
    queries[...] = low(times(normed, kept, 0))
    for j in range(heads // 2):
        block = queries[:, j * PAIR : (j + 1) * PAIR] * jnp.bfloat16(0.125)
        spread = low(contract(pair_rows(block), pair_weight(kept, 1, j), 1, 1))
        spread_out[2 * j] = spread[:tokens]
        spread_out[2 * j + 1] = spread[tokens:]
    leaving[0].start()

    count = list_chunks(starts, table)

    def two_chunks(i, carry):
        places = [2 * i, jnp.minimum(2 * i + 1, count - 1)]
        for n, place in enumerate(places):

            @pl.when((2 * i + n < count) & (table[2, place] == 1))
            def _():
                block_copy(encoded, rows_ref, sems, groups, table[1, place]).wait()

        found, scores, blocks = [], [], []
        for place in places:
            token, s, begin, end = listed(starts, table, place)
            base = pl.multiple_of(groups[0, s] * block_rows, block_rows)
            found.append((token, begin, end))
            blocks.append(rows_ref[pl.ds(base, block_rows), :])
            left = spread_out[:, pl.ds(token, CHUNK), :].reshape(heads * CHUNK, model)
            scores.append(contract(left, blocks[-1], 1, 1))
        for (token, begin, end), score, rows in zip(found, scores, blocks):
            weights = jnp.exp(score - jnp.max(score, axis=-1, keepdims=True))
            totals = jnp.sum(weights, axis=-1, keepdims=True)
            probs = low(weights * (1.0 / totals))
            mixed = low(contract(probs, rows, 1, 0))
            inside = in_segment(token, begin, end, heads)
            at = (slice(None), pl.ds(token, CHUNK), slice(None))
            probs = probs.reshape(heads, CHUNK, block_rows)
            mixed = mixed.reshape(heads, CHUNK, model)
            probs_out[at] = jnp.where(inside, probs, probs_out[at])
            mixed_out[at] = jnp.where(inside, mixed, mixed_out[at])
        return carry

    lax.fori_loop(0, (count + 1) >> 1, two_chunks, 0)
    for copy in leaving[1:]:
        copy.start()
    for copy in copies[4:]:
        copy.wait()
    for j in range(heads // 2):
        both = jnp.concatenate([mixed_out[2 * j], mixed_out[2 * j + 1]], axis=0)
        found = contract(both, pair_weight(kept, 2, j), 1, 0)
        context[:, j * PAIR : (j + 1) * PAIR] = low(pair_lanes(found))
    after_cross[...] = after_self[...] + times(context[...], kept, 3)
    normed_out[...] = low(normalize(after_cross[...], gains[2:3, :]))
    for copy in leaving:
        copy.wait()


def cross_backward_first(
    core_ref, after_cross, gains, cotangent, pull_mine, pull_theirs, context, mixed_hbm, second_mine, second_sibling,
    grad_after, gain_grad, grad_context_out, pulled_hbm, grad_mine, grad_other,
    mixed, pulled_ref, kept, held, weight_sems, out_sems,
):
    core = core_ref[0]
    heads, tokens, model = pulled_ref.shape
    copies = weight_copies(core, ((second_mine, second_sibling),), kept, weight_sems)
    coming = pltpu.make_async_copy(mixed_hbm, mixed, out_sems.at[4])
    for copy in copies[2:] + copies[:2] + [coming]:
        copy.start()
    grad_normed = pull_mine[...] + pull_theirs[...].astype(jnp.float32)
    grad_values, found_gain = norm_backward(after_cross[...], gains[2:3, :], grad_normed)
    grad_after[...] = cotangent[...].astype(jnp.float32) + grad_values
    gain_grad[0:1, :] = found_gain
    branch = low(grad_after[...])
    grad_into(context[...], branch, held, 1)
    started = []

    def send(number):
        for copy in grad_copies(core, (grad_mine, grad_other), held, number, out_sems):
            copy.start()
            started.append(copy)

    send(1)
    for copy in copies[2:] + copies[:2]:
        copy.wait()
    grad_context_out[...] = low(times_back(branch, kept, 1))
    coming.wait()
    per_half = held.shape[-1] // PAIR
    for j in range(heads // 2):
        columns = slice((j % per_half) * PAIR, (j % per_half + 1) * PAIR)
        rows = pair_rows(grad_context_out[:, j * PAIR : (j + 1) * PAIR])
        both = jnp.concatenate([mixed[2 * j], mixed[2 * j + 1]], axis=0)
        held[0, j // per_half, :, columns] = low(contract(both, rows, 0, 0))
        pulled = low(contract(rows, pair_weight(kept, 0, j), 1, 1))
        pulled_ref[2 * j] = pulled[:tokens]
        pulled_ref[2 * j + 1] = pulled[tokens:]
    send(0)
    leaving = pltpu.make_async_copy(pulled_ref, pulled_hbm, out_sems.at[5])
    leaving.start()
    started.append(leaving)
    for copy in started:
        copy.wait()


def cross_backward_second(
    core_ref, starts, groups, grad_after, after_self, gains, ffn_gain_grad, queries, encoded,
    probs_hbm, pulled_hbm, first_mine, first_sibling,
    grad_self, gain_grads, score_hbm, grad_mine, grad_other,
    probs_ref, pulled_ref, score_out, rows_ref, moved_ref, kept, held, table, sems, weight_sems, out_sems, chunk_sems,
):
    core = core_ref[0]
    heads, tokens, model = pulled_ref.shape
    segs = groups.shape[1]
    block_rows = encoded.shape[0] // segs
    half = kept.shape[-1]
    chunk_pairs = ((pulled_hbm, pulled_ref), (probs_hbm, probs_ref))
    block_copy(encoded, rows_ref, sems, groups, 0).start()
    for c in range(tokens // CHUNK):
        for copy in chunk_copies(chunk_pairs, chunk_sems, c):
            copy.start()
        if c % 2 and c // 2 + 1 < segs:
            block_copy(encoded, rows_ref, sems, groups, c // 2 + 1).start()
    copies = weight_copies(core, ((first_mine, first_sibling),), kept, weight_sems)
    for copy in copies:
        copy.start()
    started = []

    def send(number):
        for copy in grad_copies(core, (grad_mine, grad_other), held, number, out_sems):
            copy.start()
            started.append(copy)


    count = list_chunks(starts, table)

    def two_chunks(i, carry):
        places = [2 * i, jnp.minimum(2 * i + 1, count - 1)]
        for n, place in enumerate(places):

            @pl.when((2 * i + n < count) & (table[2, place] == 1))
            def _():
                block_copy(encoded, rows_ref, sems, groups, table[1, place]).wait()

            @pl.when((2 * i + n < count) & (table[3, place] == 1))
            def _():
                for copy in chunk_copies(chunk_pairs, chunk_sems, table[0, place] >> 4):
                    copy.wait()

        found, prob_grads, blocks = [], [], []
        for place in places:
            token, s, begin, end = listed(starts, table, place)
            base = pl.multiple_of(groups[0, s] * block_rows, block_rows)
            blocks.append(rows_ref[pl.ds(base, block_rows), :])
            at = (slice(None), pl.ds(token, CHUNK), slice(None))
            inside = in_segment(token, begin, end, heads)
            found.append((at, inside))
            pulled = jnp.where(inside, pulled_ref[at], jnp.zeros((), jnp.bfloat16))
            prob_grads.append(contract(pulled.reshape(heads * CHUNK, model), blocks[-1], 1, 1))
        for (at, inside), prob_grad, rows in zip(found, prob_grads, blocks):
            wide = probs_ref[at].reshape(heads * CHUNK, block_rows).astype(jnp.float32)
            inner = jnp.sum(wide * prob_grad, axis=-1, keepdims=True)
            score_grad = low(wide * (prob_grad - inner))
            moved = low(contract(score_grad, rows, 1, 0)).reshape(heads, CHUNK, model)
            moved_ref[at] = jnp.where(inside, moved, moved_ref[at])
            score_grad = score_grad.reshape(heads, CHUNK, block_rows)
            score_out[at] = jnp.where(inside, score_grad, score_out[at])
        return carry

    lax.fori_loop(0, (count + 1) >> 1, two_chunks, 0)
    leaving = pltpu.make_async_copy(score_out, score_hbm, out_sems.at[4])
    leaving.start()
    started.append(leaving)
    for copy in copies:
        copy.wait()
    found = []
    per_half = half // PAIR
    for j in range(heads // 2):
        columns = slice((j % per_half) * PAIR, (j % per_half + 1) * PAIR)
        both = jnp.concatenate([moved_ref[2 * j], moved_ref[2 * j + 1]], axis=0)
        found.append(low(pair_lanes(contract(both, pair_weight(kept, 1, j), 1, 0)) * 0.125))
        block = queries[:, j * PAIR : (j + 1) * PAIR] * jnp.bfloat16(0.125)
        held[1, j // per_half, :, columns] = low(contract(both, pair_rows(block), 0, 0))
    send(1)
    grad_queries = jnp.concatenate(found, axis=1)
    values = after_self[...]
    grad_into(low(normalize(values, gains[1:2, :])), grad_queries, held, 0)
    send(0)
    grad_values, grad_gain = norm_backward(values, gains[1:2, :], times_back(grad_queries, kept, 0))
    grad_self[...] = grad_after[...] + grad_values
    gain_grads[0:1, :] = grad_gain
    gain_grads[1:2, :] = ffn_gain_grad[0:1, :]
    for copy in started:
        copy.wait()


def rows_backward_kernel(
    starts, groups, score_hbm, probs_hbm, spread_hbm, pulled_hbm, grad_rows,
    score_grads, probs_ref, spread, pulled_ref, sum_ref, row_sems, chunk_sems,
):
    heads, tokens, model = spread.shape
    segs = groups.shape[1]
    block_rows = grad_rows.shape[0] // segs

    chunk_pairs = (
        (score_hbm, score_grads), (probs_hbm, probs_ref), (spread_hbm, spread), (pulled_hbm, pulled_ref),
    )
    for c in range(tokens // CHUNK):
        for copy in chunk_copies(chunk_pairs, chunk_sems, c):
            copy.start()

    def write_out(s):
        slot = s & 1
        base = pl.multiple_of(groups[0, s] * block_rows, block_rows)
        return pltpu.make_async_copy(
            sum_ref.at[slot], grad_rows.at[pl.ds(base, block_rows)], row_sems.at[slot]
        )

    def segment(s, begin):
        end = starts[0, s + 1]
        slot = s & 1

        @pl.when(s >= 2)
        def _():
            write_out(s - 2).wait()

        def terms(c):
            @pl.when((c * CHUNK >= begin) | (begin & (CHUNK - 1) == 0))
            def _():
                for copy in chunk_copies(chunk_pairs, chunk_sems, c):
                    copy.wait()

            token = pl.multiple_of(c * CHUNK, CHUNK)
            at = (slice(None), pl.ds(token, CHUNK), slice(None))
            inside = in_segment(token, begin, end, heads)
            zero = jnp.zeros((), jnp.bfloat16)
            scores = jnp.where(inside, score_grads[at], zero).reshape(heads * CHUNK, block_rows)
            left = jnp.concatenate([scores, probs_ref[at].reshape(heads * CHUNK, block_rows)], axis=0)
            right = jnp.concatenate(
                [jnp.where(inside, piece[at], zero).reshape(heads * CHUNK, model) for piece in (spread, pulled_ref)],
                axis=0,
            )
            return contract(left, right, 0, 0)

        def chunk(c, carry):
            sum_ref[slot] += terms(c)
            return carry

        first = begin >> 4
        sum_ref[slot] = terms(first)
        lax.fori_loop(first + 1, (end + CHUNK - 1) >> 4, chunk, 0)
        write_out(s).start()
        return end

    lax.fori_loop(0, segs, segment, 0)
    for s in range(segs - 2, segs):
        write_out(s).wait()


def gelu_both(values):
    scale = 0.7978845608028654
    square = values * values
    bend = jnp.tanh(scale * (values + 0.044715 * (square * values)))
    half = 0.5 * (1.0 + bend)
    slope = half + 0.5 * values * (1.0 - bend * bend) * (scale * (1.0 + 3.0 * 0.044715 * square))
    return values * half, slope


def ffn_kernel(
    direct,
    core_ref, normed, normed_theirs, cotangent, cotangent_theirs, *refs,
):
    sources, refs = (refs[:4], refs[4:]) if direct else (refs[:2], refs[2:])
    out_mine, out_other, pull_mine, pull_other, grad_mine, grad_other = refs[:6]
    kept_in, kept_down, held_in, held_down, sems, out_sems = refs[6:]
    core = core_ref[0]
    blocks, groups, unused, width = kept_in.shape
    model = kept_in.shape[1] * kept_in.shape[2]
    count = normed.shape[0]
    if direct:
        copies = [
            pltpu.make_async_copy(source, target, sems.at[n])
            for n, (source, target) in enumerate(
                (
                    (sources[0], kept_in.at[core]),
                    (sources[1], kept_down.at[:, core]),
                    (sources[2], kept_in.at[1 - core]),
                    (sources[3], kept_down.at[:, 1 - core]),
                )
            )
        ]
    else:
        copies = [
            pltpu.make_async_copy(source, target, sems.at[n])
            for n, (source, target) in enumerate(zip(sources, (kept_in, kept_down)))
        ]
    for copy in copies:
        copy.start()
    tokens = jnp.concatenate([normed[...], normed_theirs[...]], axis=0)
    pull = jnp.concatenate([cotangent[...], cotangent_theirs[...]], axis=0)
    for copy in copies:
        copy.wait()
    total = grad_tokens = None
    started = []
    for b in range(blocks):
        weight_up = kept_in[b].reshape(model, width)
        part = slice(b * groups // blocks, (b + 1) * groups // blocks) if direct else slice(0, 1)
        if direct:
            weight_down = kept_down[part].reshape(width, model)
        else:
            weight_down = kept_down[0, 0, b * width : (b + 1) * width]
        activated, slope = gelu_both(contract(tokens, weight_up, 1, 0))
        activated = low(activated)
        grad_act = low(contract(pull, weight_down, 1, 1)).astype(jnp.float32)
        grad_pre = low(slope * grad_act)
        added = contract(grad_pre, weight_up, 1, 1)
        grad_tokens = added if b == 0 else grad_tokens + added
        added = contract(activated, weight_down, 1, 0)
        total = added if b == 0 else total + added
        held_in[b] = low(contract(tokens, grad_pre, 0, 0)).reshape(held_in.shape[1:])
        grad_down = low(contract(activated, pull, 0, 0))
        if direct:
            held_down[part] = grad_down.reshape((groups // blocks,) + held_down.shape[1:])
        else:
            held_down[0, 0, b * width : (b + 1) * width] = grad_down
    if direct:
        rows = held_down.shape[2]
        targets = (
            (held_in.at[1 - core], grad_other.at[:, :rows]),
            (held_down.at[:, 1 - core], grad_other.at[:, rows:]),
            (held_in.at[core], grad_mine.at[:, :rows]),
            (held_down.at[:, core], grad_mine.at[:, rows:]),
        )
    else:
        targets = ((held_in, grad_mine), (held_down, grad_other))
    started = [pltpu.make_async_copy(source, target, out_sems.at[n]) for n, (source, target) in enumerate(targets)]
    for copy in started:
        copy.start()
    out_mine[...] = total[:count]
    out_other[...] = low(total[count:])
    pull_mine[...] = grad_tokens[:count]
    pull_other[...] = low(grad_tokens[count:])
    for copy in started:
        copy.wait()

VMEM = pl.BlockSpec(memory_space=pltpu.VMEM)
SMEM = pl.BlockSpec(memory_space=pltpu.SMEM)
HBM = pl.BlockSpec(memory_space=pltpu.HBM)
ANY = pl.BlockSpec(memory_space=pl.ANY)


def shaped(shape, dtype):
    return jax.ShapeDtypeStruct(shape, dtype)


def call(kernel, name, flops, in_specs, out_specs, out_shape, scratch, aliases={}, room=VMEM_BYTES):
    return pl.pallas_call(
        kernel,
        out_shape=out_shape,
        in_specs=in_specs,
        out_specs=out_specs,
        scratch_shapes=scratch,
        compiler_params=pltpu.CompilerParams(vmem_limit_bytes=room),
        cost_estimate=pl.CostEstimate(flops=flops, bytes_accessed=1_000_000, transcendentals=0),
        name=name,
        input_output_aliases=aliases,
    )


AXES = ("dp", "fsdp")


def swap_with(piece, mask, devices):
    pairs = [(index, index ^ mask) for index in range(devices)]
    return lax.ppermute(piece, AXES, pairs)


def bit_of(me, bit):
    return (me >> bit) & 1


def pair_up(mine, theirs, my_bit, axis):
    first = jnp.where(my_bit == 0, mine, theirs)
    second = jnp.where(my_bit == 0, theirs, mine)
    return jnp.stack([first, second], axis=axis)


def arranged(found, bits, me):
    found = {mask: [block] for mask, block in found.items()}
    for n, bit in enumerate(sorted(bits)):
        low_side = bit_of(me, bit) == 0
        merged = {}
        for mask in found:
            if not mask >> n & 1:
                both = list(zip(found[mask], found[mask | 1 << n]))
                merged[mask] = [jnp.where(low_side, x, y) for x, y in both] + [
                    jnp.where(low_side, y, x) for x, y in both
                ]
        found = merged
    return jnp.stack(found[0])


def wide_mask(mask, bits):
    return sum(1 << bit for n, bit in enumerate(sorted(bits)) if mask >> n & 1)


def exchange(send, bits, me, devices):
    found = {0: send(0)}
    for mask in range(1, 1 << len(bits)):
        found[mask] = swap_with(send(mask), wide_mask(mask, bits), devices)
    return arranged(found, bits, me)


def gather_line(block, bits, me, devices):
    if len(bits) > 2:
        held = block[None]
        for bit in sorted(bits):
            theirs = swap_with(held, 1 << bit, devices)
            held = pair_up(held, theirs, bit_of(me, bit), 0).reshape((-1,) + block.shape)
        return held
    return exchange(lambda mask: block, bits, me, devices)


def taken(source, places, columns):
    array, bits, offset = source
    begin = [places[bit] if bit in places else 0 for bit in bits] + [0, offset + columns[0]]
    size = [1 if bit in places else 2 for bit in bits] + [array.shape[-2], columns[1] - columns[0]]
    part = lax.dynamic_slice(array, begin, size)
    return part.reshape([2 for bit in bits if bit not in places] + size[-2:])


def summed(entry, places):
    sources, columns = entry
    total = None
    for source in sources:
        part = taken(source, places, columns).astype(jnp.float32)
        total = part if total is None else total + part
    return total


def with_brought(entry, theirs, bit, done):
    sources, columns = entry
    bits = [other for other in sources[0][1] if other not in done and other != bit]
    return (sources + [(theirs, bits, -columns[0])], columns)


def sum_over(entries, bit, done, me, devices):
    places = {other: bit_of(me, other) for other in done}
    send = [low(summed(entry, {**places, bit: 1 - bit_of(me, bit)})) for entry in entries]
    theirs = swap_with(jnp.concatenate(send, axis=-1), 1 << bit, devices)
    found, at = [], 0
    for sources, columns in entries:
        bits = [other for other in sources[0][1] if other not in done and other != bit]
        found.append((sources + [(theirs, bits, at - columns[0])], columns))
        at += columns[1] - columns[0]
    return found


def combine(me_word, outputs):
    arrays, buffers, plan, shapes = [], {}, [], []
    for pieces, dtype in outputs:
        at, steps = 0, []
        for (sources, columns), flips, late in pieces:
            keys = []
            for array, bits, offset in sources:
                number = next((n for n, other in enumerate(arrays) if other is array), len(arrays))
                if number == len(arrays):
                    arrays.append(array)
                picked = tuple(flips.get(bit) for bit in bits)
                key = (number, tuple(bits), picked, offset + columns[0], columns[1] - columns[0])
                buffers.setdefault(key, len(buffers))
                keys.append(key)
            steps.append((at, keys, late))
            at += columns[1] - columns[0]
        sources = pieces[0][0][0]
        left = [bit for bit in sources[0][1] if bit not in pieces[0][1] and bit not in pieces[0][2]]
        plan.append(steps)
        shapes.append(shaped((2,) * len(left) + (sources[0][0].shape[-2], at), dtype))

    def kernel(me_ref, *refs):
        inputs, targets = refs[: len(arrays)], refs[len(arrays) : len(arrays) + len(outputs)]
        held, sems = refs[len(arrays) + len(outputs) : -1], refs[-1]
        me = me_ref[0]
        copies = {}
        for key, n in buffers.items():
            number, bits, picked, begin, width = key
            index = tuple(
                slice(None) if flip is None else ((me >> bit) & 1) ^ flip for bit, flip in zip(bits, picked)
            )
            copies[key] = pltpu.make_async_copy(
                inputs[number].at[index + (slice(None), slice(begin, begin + width))], held[n], sems.at[n]
            )
            copies[key].start()
        waited = set()
        for target, steps in zip(targets, plan):
            for at, keys, late in steps:
                total = None
                for key in keys:
                    if key not in waited:
                        copies[key].wait()
                        waited.add(key)
                    left = [bit for bit, flip in zip(key[1], key[2]) if flip is None]
                    index = tuple(((me >> bit) & 1) ^ late[bit] if bit in late else slice(None) for bit in left)
                    part = held[buffers[key]][index].astype(jnp.float32)
                    total = part if total is None else total + part
                target[..., at : at + keys[0][4]] = total.astype(target.dtype)

    scratch = []
    for number, bits, picked, begin, width in buffers:
        lead = tuple(2 for flip in picked if flip is None)
        scratch.append(pltpu.VMEM(lead + (arrays[number].shape[-2], width), arrays[number].dtype))
    scratch.append(pltpu.SemaphoreType.DMA((len(buffers),)))
    found = call(
        kernel, "combine", 1_000_000, [SMEM] + [ANY] * len(arrays), [VMEM] * len(outputs), tuple(shapes), scratch
    )(me_word, *arrays)
    return list(found)


def line_terms(me_word, entries, bits, done, devices):
    flips = {bit: 0 for bit in done}
    if len(bits) > 2:
        for bit in sorted(bits):
            entries = sum_over(entries, bit, list(flips), me_word[0], devices)
            flips[bit] = 0
        return combine(me_word, [([(entry, flips, {}) for entry in entries], jnp.float32)])
    masks = [wide_mask(mask, bits) for mask in range(1 << len(bits))]
    outputs = [
        (
            [(entry, flips, {bit: mask >> bit & 1 for bit in bits}) for entry in entries],
            jnp.bfloat16 if mask else jnp.float32,
        )
        for mask in masks
    ]
    blocks = combine(me_word, outputs)
    return blocks[:1] + [swap_with(block, mask, devices) for block, mask in zip(blocks[1:], masks[1:])]


def core_rows(total, core, devices):
    rows = total.shape[0] // 2
    keep = lax.dynamic_slice_in_dim(total, core * rows, rows, axis=0)
    send = lax.dynamic_slice_in_dim(total, (1 - core) * rows, rows, axis=0)
    theirs = swap_with(send, 1, devices)
    return jnp.where(core == 0, keep, theirs), jnp.where(core == 0, theirs, keep)


def per_device(
    fsdp,
    devices,
    tokens,
    encoded,
    segment_ids,
    passage_group,
    cotangent,
    self_gain,
    cross_gain,
    ffn_gain,
    self_query,
    self_key,
    self_value,
    self_out,
    cross_query,
    cross_key,
    cross_value,
    cross_out,
    ffn_in,
    ffn_out,
):
    me = lax.axis_index("dp") * fsdp + lax.axis_index("fsdp")
    core = bit_of(me, 0)
    core_word = core.reshape(1).astype(jnp.int32)
    me_word = me.reshape(1).astype(jnp.int32)
    bounds = lax.broadcasted_iota(jnp.int32, (1, passage_group.shape[1] + 1), 1)
    starts = jnp.sum((segment_ids[0, :, None] < bounds).astype(jnp.int32), axis=0, keepdims=True)
    chip_bits = list(range(1, devices.bit_length() - 1))
    line_bits = [bit for bit in reversed(chip_bits) if bit > 2]
    pair_orders = ([2, 1], [1, 2])
    count, model = tokens.shape
    encoder_count = encoded.shape[0]
    hidden_units = ffn_in.shape[1]
    heads = model // HEAD
    half = model // 2
    segs = passage_group.shape[1]
    low_type, wide_type = jnp.bfloat16, jnp.float32

    def my_columns(matrix, owner):
        width = matrix.shape[-1] // 2
        return lax.dynamic_slice_in_dim(matrix, owner * width, width, axis=matrix.ndim - 1)

    barrier = lax.optimization_barrier
    gains = jnp.stack([self_gain, cross_gain, ffn_gain], axis=1)
    gains = jnp.pad(gains, ((0, 0), (0, PAIR - 3)))
    shards = [self_query, self_key, self_value, self_out, cross_query, cross_key, cross_value, cross_out]
    rows_in = ffn_in.shape[0]
    rows_down = ffn_out.shape[0]
    direct = rows_down % 16 == 0
    chip_groups = devices // 4
    group_bits = [0, 1]
    in_blocks = ffn_in.reshape(rows_in, 2, chip_groups // 2, 2, 2 * rows_down)
    in_blocks = in_blocks.transpose(3, 1, 0, 2, 4).reshape(2, 2, rows_in, model)
    packed = shaped((rows_in, len(shards) * half + PAIR + 2 * model), low_type)
    send, keep = call(
        pack_kernel, "pack", 0, [SMEM] + [VMEM] * 10, [VMEM] * 2, (packed, packed), []
    )(core_word, *shards, gains, in_blocks)
    theirs = swap_with(send, 1, devices)
    chip_block = pair_up(keep, theirs, core, 0).reshape(-1, keep.shape[1])
    self_block = jnp.concatenate([chip_block[:, : 2 * model], chip_block[:, 4 * model : 4 * model + PAIR]], axis=1)
    in_halves = chip_block[:, 4 * model + PAIR :]
    cross_block = chip_block[:, 2 * model : 4 * model]

    def double(held, bit, first_bit, me):
        place = 1 if first_bit is None or bit > first_bit else 2
        return pair_up(held, swap_with(held, 1 << bit, devices), bit_of(me, bit), place)

    def first_step(line, width):
        return [double(part, order[0], None, me) for part, order in zip((line[:, :, :width], line[:, :, width:]), pair_orders)]

    def second_step(parts):
        return [
            double(part, order[1], order[0], me).reshape(-1, part.shape[-1])
            for part, order in zip(parts, pair_orders)
        ]

    cotangent_theirs = swap_with(cotangent, 2, devices)

    def block_for(array, mask):
        first = [bit_of(me, 1) ^ (mask >> 1 & 1), core ^ (mask & 1)]
        return lax.dynamic_slice(array, first + [0, 0], (1, 1) + array.shape[2:]).reshape(array.shape[2:])

    ffn_steps = line_bits + [2]

    def merged(held, theirs, steps, number):
        bit = steps[number]
        place = sum(1 for other in steps[:number] if other > bit)
        return pair_up(held, theirs, bit_of(me, bit), place)

    def brought(held, steps, number):
        return swap_with(held, 1 << steps[number], devices)

    def half_at(array, place):
        return lax.dynamic_slice_in_dim(array, place * model, model, axis=1)

    self_line = gather_line(self_block, line_bits, me, devices)
    self_line, cross_held, in_halves, cotangent_theirs, down_held = barrier(
        (self_line, cross_block, in_halves, cotangent_theirs, ffn_out)
    )
    y_bit = bit_of(me, 1)
    in_theirs = swap_with(half_at(in_halves, 1 - y_bit), 2, devices)
    last = len(line_bits) - 1
    self_parts = first_step(self_line, model)
    for number in range(last):
        cross_held = merged(cross_held, brought(cross_held, line_bits, number), line_bits, number)
        down_held = merged(down_held, brought(down_held, ffn_steps, number), ffn_steps, number)
    self_parts, cross_held, in_theirs, down_held = barrier((self_parts, cross_held, in_theirs, down_held))
    in_held = pair_up(half_at(in_halves, y_bit), in_theirs, y_bit, 0).reshape(4 * rows_in, model)
    self_theirs = [brought(part, [2, 1, 2], n + 1) for n, part in enumerate(self_parts)]
    cross_line = merged(cross_held, brought(cross_held, line_bits, last), line_bits, last)
    cross_line = cross_line.reshape((-1,) + cross_block.shape)
    for number in range(last):
        in_held = merged(in_held, brought(in_held, ffn_steps, number), ffn_steps, number)
    down_theirs = brought(down_held, ffn_steps, last)
    cross_line, in_held, down_theirs, self_theirs = barrier((cross_line, in_held, down_theirs, self_theirs))
    cross_parts = first_step(cross_line, model)
    in_theirs = brought(in_held, ffn_steps, last)
    cross_parts, in_theirs = barrier((cross_parts, in_theirs))
    in_held = merged(in_held, in_theirs, ffn_steps, last)
    down_held = merged(down_held, down_theirs, ffn_steps, last)

    def second_merge(parts, theirs):
        return [
            pair_up(part, other, bit_of(me, order[1]), 1 if order[1] > order[0] else 2).reshape(-1, part.shape[-1])
            for part, other, order in zip(parts, theirs, pair_orders)
        ]

    self_mine = second_merge(self_parts, self_theirs)
    cross_theirs = [brought(part, [2, 1, 2], n + 1) for n, part in enumerate(cross_parts)]
    self_weights = [(mine, swap_with(mine[:, :model], 1, devices)) for mine in self_mine]

    gain_rows = self_weights[1][0][:, model : model + 8].T.astype(wide_type)
    self_flat = self_weights[0] + self_weights[1]

    dma = pltpu.SemaphoreType.DMA
    weights_kept = pltpu.VMEM((4, 2, model, half), low_type)
    projected, context_one, after_self = call(
        self_forward_kernel,
        "self_forward",
        2 * count * model * model * 5,
        [SMEM, VMEM, VMEM, VMEM] + [ANY] * 4,
        [VMEM] * 3,
        (
            shaped((3, count, model), low_type),
            shaped((count, model), low_type),
            shaped((count, model), wide_type),
        ),
        [weights_kept, dma((8,))],
        room=MIDDLE_BYTES,
    )(core_word, segment_ids, tokens, gain_rows, *self_flat)

    cross_theirs, in_held, down_held, after_self = barrier((cross_theirs, in_held, down_held, after_self))
    in_theirs, down_theirs = swap_with(in_held, 4, devices), swap_with(down_held, 4, devices)
    cross_mine = second_merge(cross_parts, cross_theirs)
    cross_weights = [(mine, swap_with(mine, 1, devices)) for mine in cross_mine]
    cross_flat = cross_weights[0] + cross_weights[1]

    per_token = (heads, count, model)
    probs_shape = (heads, count, encoder_count // segs)
    probs_kept, tokens_kept = pltpu.VMEM(probs_shape, low_type), pltpu.VMEM(per_token, low_type)
    chunk_count = count // CHUNK
    chunk_table = pltpu.SMEM((4, chunk_count + segs), jnp.int32)
    queries_two, context_two, after_cross, normed_three, probs, mixed, spread = call(
        cross_forward_kernel,
        "cross_forward",
        12_000_000_000,
        [SMEM, SMEM, SMEM, VMEM, VMEM] + [HBM] * 5,
        [VMEM] * 4 + [HBM] * 3,
        (
            shaped((count, model), low_type),
            shaped((count, model), low_type),
            shaped((count, model), wide_type),
            shaped((count, model), low_type),
            shaped(probs_shape, low_type),
            shaped(per_token, low_type),
            shaped(per_token, low_type),
        ),
        [
            probs_kept, tokens_kept, tokens_kept, pltpu.VMEM(encoded.shape, low_type), weights_kept,
            chunk_table, dma((segs,)), dma((8,)), dma((3,)),
        ],
    )(core_word, starts, passage_group, after_self, gain_rows, encoded, *cross_flat)

    normed_theirs = swap_with(normed_three, 2, devices)
    in_theirs, down_theirs, normed_theirs = barrier((in_theirs, down_theirs, normed_theirs))
    ffn_mine = [
        pair_up(held, theirs, bit_of(me, 2), len(line_bits)).reshape((chip_groups,) + held.shape[-2:])
        for held, theirs in ((in_held, in_theirs), (down_held, down_theirs))
    ]
    ffn_sibling = [swap_with(mine, 1, devices) for mine in ffn_mine]
    half_units = hidden_units // 2
    if direct:
        in_shape = (2, chip_groups, rows_down, model)
        down_shape = (chip_groups, 2, rows_down, model)
        ffn_weights = ffn_mine + ffn_sibling
        grad_shapes = (shaped((chip_groups, 2 * rows_down, model), low_type),) * 2
    else:
        in_shape, down_shape = (2, 1, model, model), (1, 1, half_units, model)
        ffn_weights = (
            pair_up(ffn_mine[0], ffn_sibling[0], core, 0).reshape(in_shape),
            pair_up(ffn_mine[1], ffn_sibling[1], core, 1).reshape(down_shape),
        )
        grad_shapes = (shaped(in_shape, low_type), shaped(down_shape, low_type))
    token_shapes = (shaped((count, model), wide_type), shaped((count, model), low_type))
    out_mine, out_other, pull_mine, pull_other, ffn_grad, ffn_other = call(
        functools.partial(ffn_kernel, direct),
        "ffn",
        4_000_000_000,
        [SMEM] + [VMEM] * 4 + [ANY] * len(ffn_weights),
        [VMEM] * 4 + [HBM] * 2,
        token_shapes + token_shapes + grad_shapes,
        [
            pltpu.VMEM(in_shape, low_type),
            pltpu.VMEM(down_shape, low_type),
            pltpu.VMEM(in_shape, low_type),
            pltpu.VMEM(down_shape, low_type),
            dma((4,)),
            dma((4,)),
        ],
        room=MIDDLE_BYTES,
    )(core_word, normed_three, normed_theirs, cotangent, cotangent_theirs, *ffn_weights)
    pull_theirs = swap_with(pull_other, 2, devices)
    if not direct:
        in_parts = ffn_grad.reshape(2, chip_groups, 4 * rows_in, model)
        down_parts = ffn_other.reshape(chip_groups, 2, rows_down, model).swapaxes(0, 1)
        both = jnp.concatenate([in_parts, down_parts], axis=2)
        ffn_grad, ffn_other = (
            lax.dynamic_index_in_dim(both, place, 0, keepdims=False) for place in (core, 1 - core)
        )
    ffn_theirs = swap_with(ffn_other, 1, devices)
    high_bits = [bit for bit in sorted(chip_bits, reverse=True) if bit > 1]

    def group_source(array):
        return (array.reshape((2,) * len(high_bits) + array.shape[-2:]), high_bits, 0)

    ffn_entry = ([group_source(ffn_grad), group_source(ffn_theirs)], (0, model))
    ffn_send = low(summed(ffn_entry, {2: 1 - bit_of(me, 2)}))
    pull_theirs, ffn_send, out_other = barrier((pull_theirs, ffn_send, out_other))
    ffn_sum = [with_brought(ffn_entry, swap_with(ffn_send, 4, devices), 2, [])]
    out_theirs = swap_with(out_other, 2, devices)

    all_bits = sorted(chip_bits, reverse=True)

    def chips_of(array):
        return array.reshape((2,) * len(all_bits) + (array.shape[0] >> len(all_bits), array.shape[-1]))

    def entry_of(mine, theirs, begin, end):
        return ([(chips_of(mine), all_bits, 0), (chips_of(theirs), all_bits, 0)], (begin, end))

    def first_sum(sides):
        return [sum_over(entries, order[0], [], me, devices) for entries, order in zip(sides, pair_orders)]

    def second_sum(sides):
        return [sum_over(entries, order[1], order[:1], me, devices) for entries, order in zip(sides, pair_orders)]

    def received(sides):
        return [entries[0][0][-1][0] for entries in sides]

    def with_received(sides, arrays):
        return [
            [(sources[:-1] + [(array,) + sources[-1][1:]], columns) for sources, columns in entries]
            for entries, array in zip(sides, arrays)
        ]

    grads_shape = shaped((model, model), low_type)
    rows_kept = pltpu.VMEM(encoded.shape, low_type)
    two_kept = pltpu.VMEM((2, 2, model, half), low_type)
    grad_after_cross, ffn_gain_grad, grad_context, pulled, late_mine, late_other = call(
        cross_backward_first,
        "cross_backward_first",
        1_000_000_000,
        [SMEM] + [VMEM] * 6 + [HBM] * 3,
        [VMEM] * 3 + [HBM] * 3,
        (
            shaped((count, model), wide_type),
            shaped((8, model), wide_type),
            shaped((count, model), low_type),
            shaped(per_token, low_type),
            grads_shape,
            grads_shape,
        ),
        [tokens_kept, tokens_kept, two_kept, two_kept, dma((4,)), dma((6,))],
    )(
        core_word, after_cross, gain_rows, cotangent, pull_mine, pull_theirs, context_two, mixed, *cross_weights[1]
    )
    late_theirs = swap_with(late_other, 1, devices)
    grad_after_self, gain_grads, score_grads, early_mine, early_other = call(
        cross_backward_second,
        "cross_backward_second",
        3_000_000_000,
        [SMEM, SMEM, SMEM] + [VMEM] * 5 + [HBM] * 5,
        [VMEM] * 2 + [HBM] * 3,
        (
            shaped((count, model), wide_type),
            shaped((8, model), wide_type),
            shaped(probs_shape, low_type),
            grads_shape,
            grads_shape,
        ),
        [
            probs_kept, tokens_kept, probs_kept, rows_kept, tokens_kept, two_kept, two_kept,
            chunk_table, dma((segs,)), dma((4,)), dma((5,)), dma((2, chunk_count)),
        ],
    )(
        core_word, starts, passage_group, grad_after_cross, after_self, gain_rows, ffn_gain_grad,
        queries_two, encoded, probs, pulled, *cross_weights[0],
    )
    arrays, grad_after_self, early_mine, early_other, out_theirs = barrier(
        (received([ffn_sum]), grad_after_self, early_mine, early_other, out_theirs)
    )
    block_out = low(after_cross + (out_mine + out_theirs.astype(wide_type)))
    ffn_sum = with_received([ffn_sum], arrays)[0]
    ffn_done = [2]
    for bit in sorted(line_bits)[:-1]:
        ffn_sum = sum_over(ffn_sum, bit, ffn_done, me, devices)
        ffn_done = ffn_done + [bit]
    early_theirs = swap_with(early_other, 1, devices)

    with_gains = shaped((model, 2 * model + PAIR), low_type)
    tokens_grad, self_mine, self_other = call(
        self_backward_kernel,
        "self_backward",
        2 * count * model * model * 10,
        [SMEM] + [VMEM] * 7 + [ANY] * 4,
        [VMEM] + [HBM] * 2,
        (shaped((count, model), wide_type), with_gains, with_gains),
        [weights_kept, weights_kept, pltpu.VMEM((model, PAIR), low_type), dma((8,)), dma((10,))],
        room=MIDDLE_BYTES,
    )(
        core_word, segment_ids, tokens, gain_rows, grad_after_self, gain_grads, projected, context_one,
        *self_flat,
    )
    arrays, late_theirs, early_theirs, self_mine, self_other = barrier(
        (received([ffn_sum]), late_theirs, early_theirs, self_mine, self_other)
    )
    ffn_sum = with_received([ffn_sum], arrays)[0]
    ffn_sum = sum_over(ffn_sum, max(line_bits), ffn_done, me, devices)
    self_theirs = swap_with(self_other, 1, devices)
    crossed = [
        [entry_of(late_mine, late_theirs, *cut), entry_of(early_mine, early_theirs, *cut)]
        for cut in ((0, half), (half, model))
    ]
    crossed = first_sum(crossed)
    self_theirs, score_grads = barrier((self_theirs, score_grads))
    attention = [
        [entry_of(self_mine, self_theirs, *cut)] for cut in ((0, model), (model, 2 * model + PAIR))
    ]
    attention = first_sum(attention)
    encoded_grad = call(
        rows_backward_kernel,
        "rows_backward",
        3_000_000_000,
        [SMEM, SMEM] + [HBM] * 4,
        HBM,
        shaped(encoded.shape, wide_type),
        [
            probs_kept, probs_kept, tokens_kept, tokens_kept,
            pltpu.VMEM((2, encoder_count // segs, model), wide_type), dma((2,)), dma((4, chunk_count)),
        ],
    )(starts, passage_group, score_grads, probs, spread, pulled)
    crossed_arrays, arrays, ffn_arrays, encoded_grad = barrier(
        (received(crossed), received(attention), received([ffn_sum]), encoded_grad)
    )
    ffn_sum = with_received([ffn_sum], ffn_arrays)[0]
    ffn_rows = summed(ffn_sum[0], {bit: bit_of(me, bit) for bit in high_bits})
    summed_down = ffn_rows[4 * rows_in :]
    in_parts = ffn_rows[: 4 * rows_in].reshape(2, 2, rows_in, model)
    in_parts = exchange(lambda mask: block_for(in_parts, mask), group_bits, me, devices)
    in_parts = in_parts.reshape(2, 2, rows_in, chip_groups // 2, 2 * rows_down)
    summed_in = in_parts.transpose(2, 1, 3, 0, 4).reshape(rows_in, hidden_units)
    crossed, attention = with_received(crossed, crossed_arrays), with_received(attention, arrays)
    attention = second_sum([crossed[side] + attention[side] for side in range(2)])
    terms = line_terms(me_word, attention[0] + attention[1], line_bits, [2, 1], devices)
    found = terms[0]
    for term in terms[1:]:
        found = found + term.astype(wide_type)
    pair = core_rows(found, core, devices)
    (
        summed_cv, summed_cq, summed_query, summed_key, summed_co, summed_ck, summed_value, summed_out,
    ) = (
        jnp.concatenate([piece[:, n * half : (n + 1) * half] for piece in pair], axis=1) for n in range(8)
    )
    own_gains = jnp.where(core == 0, pair[0][:, 8 * half :], pair[1][:, 8 * half :])
    return (
        block_out,
        tokens_grad,
        encoded_grad,
        own_gains[:, 0],
        own_gains[:, 1],
        own_gains[:, 2],
        summed_query,
        summed_key,
        summed_value,
        summed_out,
        summed_cq,
        summed_ck,
        summed_cv,
        summed_co,
        summed_in,
        summed_down,
    )


def solution(mesh):
    return jax.shard_map(
        functools.partial(per_device, mesh.shape["fsdp"], mesh.size),
        mesh=mesh,
        in_specs=(
            P(("dp", "fsdp"), None),
            P(("dp", "fsdp"), None),
            P(("dp", "fsdp"), None),
            P(("dp", "fsdp"), None),
            P(("dp", "fsdp"), None),
            P(("dp", "fsdp")),
            P(("dp", "fsdp")),
            P(("dp", "fsdp")),
            P(("dp", "fsdp"), None),
            P(("dp", "fsdp"), None),
            P(("dp", "fsdp"), None),
            P(("dp", "fsdp"), None),
            P(("dp", "fsdp"), None),
            P(("dp", "fsdp"), None),
            P(("dp", "fsdp"), None),
            P(("dp", "fsdp"), None),
            P(("dp", "fsdp"), None),
            P(("dp", "fsdp"), None),
        ),
        out_specs=(
            P(("dp", "fsdp"), None),
            P(("dp", "fsdp"), None),
            P(("dp", "fsdp"), None),
            P(("dp", "fsdp")),
            P(("dp", "fsdp")),
            P(("dp", "fsdp")),
            P(("dp", "fsdp"), None),
            P(("dp", "fsdp"), None),
            P(("dp", "fsdp"), None),
            P(("dp", "fsdp"), None),
            P(("dp", "fsdp"), None),
            P(("dp", "fsdp"), None),
            P(("dp", "fsdp"), None),
            P(("dp", "fsdp"), None),
            P(("dp", "fsdp"), None),
            P(("dp", "fsdp"), None),
        ),
        check_vma=False,
    )
```

```python
import functools

import jax
import jax.numpy as jnp
from jax import lax
from jax.experimental import pallas as pl
from jax.experimental.pallas import tpu as pltpu
from jax.sharding import PartitionSpec as P

HEAD = 64
CHUNK = 16
PAIR = 2 * HEAD
epsilon = 1e-06
masked_score = -1e30
VMEM_BYTES = 60 << 20
MIDDLE_BYTES = 32 << 20
SMALL_BYTES = 20 << 20


def contract(left, right, left_dim, right_dim):
    return lax.dot_general(
        left, right, (((left_dim,), (right_dim,)), ((), ())), preferred_element_type=jnp.float32
    )


def low(values):
    return values.astype(jnp.bfloat16)


def normalize(values, gain_row):
    return values * lax.rsqrt(jnp.mean(values * values, axis=-1, keepdims=True) + epsilon) * gain_row


def norm_backward(values, gain_row, grad):
    scale = lax.rsqrt(jnp.mean(values * values, axis=-1, keepdims=True) + epsilon)
    grad_gain = jnp.sum(grad * values * scale, axis=0, keepdims=True)
    weighted = gain_row * grad
    inner = jnp.mean(weighted * values, axis=-1, keepdims=True)
    return scale * weighted - values * (scale * scale * scale) * inner, grad_gain


def pair_rows(block):
    lane = lax.broadcasted_iota(jnp.int32, block.shape, 1)
    zero = jnp.zeros_like(block)
    return jnp.concatenate(
        [jnp.where(lane < HEAD, block, zero), jnp.where(lane >= HEAD, block, zero)], axis=0
    )


def pair_lanes(both):
    rows = both.shape[0] // 2
    lane = lax.broadcasted_iota(jnp.int32, (rows, both.shape[1]), 1)
    return jnp.where(lane < HEAD, both[:rows], both[rows:])


def weight_copies(core, sources, kept, sems):
    half = kept.shape[-1]
    copies = []
    for number in range(kept.shape[0]):
        for side, source in enumerate(sources[number // 2]):
            place = core if side == 0 else 1 - core
            copies.append(
                pltpu.make_async_copy(
                    source.at[:, (number % 2) * half : (number % 2 + 1) * half],
                    kept.at[number, place],
                    sems.at[2 * number + side],
                )
            )
    return copies


def piece_copies(me, pairs, kept, sems):
    core = me & 1
    half = kept.shape[-1]
    copies = []
    for number in range(kept.shape[0]):
        bit, pieces = pairs[number // 2]
        columns = slice((number % 2) * half, (number % 2 + 1) * half)
        for n, piece in enumerate(pieces):
            whole = len(pieces) == 2
            place = core if n < len(pieces) // 2 else 1 - core
            target = kept.at[number, place]
            if not whole:
                at = ((me >> bit) & 1) ^ (n & 1)
                target = kept.at[number, place, :, :, at] if bit == 1 else kept.at[number, place, :, at]
                piece = piece.at[:, :, :, columns]
            else:
                piece = piece.at[:, columns]
            copies.append(pltpu.make_async_copy(piece, target, sems.at[len(pieces) * number + n]))
    return copies


def whole_rows(kept, number, side):
    return kept[number, side].reshape(-1, kept.shape[-1])


def times(left, kept, number):
    return jnp.concatenate([contract(left, whole_rows(kept, number, side), 1, 0) for side in range(2)], axis=1)


def times_back(left, kept, number):
    half = kept.shape[-1]
    return contract(left[:, :half], whole_rows(kept, number, 0), 1, 1) + contract(
        left[:, half:], whole_rows(kept, number, 1), 1, 1
    )


def grad_into(left, right, held, number):
    half = held.shape[-1]
    for side in range(2):
        held[number, side] = low(contract(left, right[:, side * half : (side + 1) * half], 0, 0))


def grad_copies(core, targets, held, number, sems, place_of=None):
    half = held.shape[-1]
    at = number if place_of is None else place_of[number]
    copies = []
    for side, target in enumerate(targets):
        place = core if side == 0 else 1 - core
        copies.append(
            pltpu.make_async_copy(
                held.at[number, place],
                target.at[:, at * half : (at + 1) * half],
                sems.at[2 * number + side],
            )
        )
    return copies


def spread_kernel(core_ref, keep, theirs, *targets):
    core = core_ref[0]
    half = targets[0].shape[1] // 2
    for number, target in enumerate(targets[:-1]):
        columns = slice(number * half, (number + 1) * half)
        for side in range(2):
            target[:, side * half : (side + 1) * half] = jnp.where(core == side, keep[:, columns], theirs[:, columns])
    targets[-1][...] = keep[:, (len(targets) - 1) * half :]


def pack_kernel(core_ref, *refs):
    shards, gains, wide_shard, (send, keep) = refs[:-4], refs[-4], refs[-3], refs[-2:]
    core = core_ref[0]
    half = shards[0].shape[1] // 2
    wide = wide_shard.shape[1] // 2
    at = len(shards) * half
    for target, place in ((send, 1 - core), (keep, core)):
        for number, shard in enumerate(shards):
            target[:, number * half : (number + 1) * half] = shard[:, pl.ds(pl.multiple_of(place * half, PAIR), half)]
        target[:, at : at + PAIR] = gains[...]
        target[:, at + PAIR :] = wide_shard[:, pl.ds(pl.multiple_of(place * wide, PAIR), wide)]


def self_mask(ids_row):
    tokens = ids_row.shape[1]
    wide = jnp.broadcast_to(ids_row.astype(jnp.float32), (tokens, tokens))
    query = lax.broadcasted_iota(jnp.int32, (tokens, tokens), 0)
    key = lax.broadcasted_iota(jnp.int32, (tokens, tokens), 1)
    allowed = jnp.where((wide == wide.T) & (key <= query), 1.0, 0.0)
    return jnp.concatenate([allowed, allowed], axis=0) > 0.5


def self_probs(queries, keys, allowed):
    scores = jnp.where(allowed, contract(pair_rows(queries), keys, 1, 1) * 0.125, masked_score)
    weights = jnp.exp(scores - jnp.max(scores, axis=-1, keepdims=True))
    return weights / jnp.sum(weights, axis=-1, keepdims=True)


def self_forward_kernel(
    core_ref, ids, tokens, gains, first_mine, first_sibling, second_mine, second_sibling,
    projected, context, after, kept, sems,
):
    core = core_ref[0]
    copies = weight_copies(
        core, ((first_mine, first_sibling), (second_mine, second_sibling)), kept, sems
    )
    for copy in copies:
        copy.start()
    model = tokens.shape[1]
    hidden = tokens[...].astype(jnp.float32)
    normed = low(normalize(hidden, gains[0:1, :]))
    for number in range(3):
        copies[2 * number].wait()
        copies[2 * number + 1].wait()
        projected[number] = low(times(normed, kept, number))
    allowed = self_mask(ids[...])
    for j in range(model // PAIR):
        columns = slice(j * PAIR, (j + 1) * PAIR)
        probs = self_probs(projected[0, :, columns], projected[1, :, columns], allowed)
        context[:, columns] = low(pair_lanes(contract(low(probs), projected[2, :, columns], 1, 0)))
    copies[6].wait()
    copies[7].wait()
    after[...] = hidden + times(context[...], kept, 3)


def self_backward_kernel(
    core_ref, ids, tokens, gains, grad_after, gain_grads, projected, context,
    first_mine, first_sibling, second_mine, second_sibling,
    tokens_grad, grad_mine, grad_other,
    kept, held, gain_held, sems, out_sems,
):
    core = core_ref[0]
    copies = weight_copies(
        core, ((first_mine, first_sibling), (second_mine, second_sibling)), kept, sems
    )
    for copy in copies:
        copy.start()
    model = tokens.shape[1]
    count = tokens.shape[0]
    hidden = tokens[...].astype(jnp.float32)
    normed = low(normalize(hidden, gains[0:1, :]))
    branch = low(grad_after[...])
    started = []

    def send(number):
        for copy in grad_copies(core, (grad_mine, grad_other), held, number, out_sems):
            copy.start()
            started.append(copy)

    grad_into(context[...], branch, held, 3)
    send(3)
    for copy in copies:
        copy.wait()
    grad_context = low(times_back(branch, kept, 3))
    allowed = self_mask(ids[...])
    found = ([], [], [])
    for j in range(model // PAIR):
        columns = slice(j * PAIR, (j + 1) * PAIR)
        queries, keys = projected[0, :, columns], projected[1, :, columns]
        probs = self_probs(queries, keys, allowed)
        pulled = pair_rows(grad_context[:, columns])
        prob_grad = contract(pulled, projected[2, :, columns], 1, 1)
        inner = jnp.sum(probs * prob_grad, axis=-1, keepdims=True)
        score_grad = low(probs * (prob_grad - inner))
        found[0].append(low(pair_lanes(contract(score_grad, keys, 1, 0)) * 0.125))
        found[1].append(low(contract(score_grad, pair_rows(queries), 0, 0) * 0.125))
        found[2].append(low(contract(low(probs), pulled, 0, 0)))
    grad_normed = None
    for number in range(3):
        whole = jnp.concatenate(found[number], axis=1)
        grad_into(normed, whole, held, number)
        send(number)
        part = times_back(whole, kept, number)
        grad_normed = part if grad_normed is None else grad_normed + part
    grad_hidden, grad_gain = norm_backward(hidden, gains[0:1, :], grad_normed)
    tokens_grad[...] = grad_after[...] + grad_hidden
    row = lax.broadcasted_iota(jnp.int32, (count, model), 0)
    others = gain_grads[...]
    wide = jnp.where(
        row == 0, grad_gain, jnp.where(row == 1, others[0:1], jnp.where(row == 2, others[1:2], 0.0))
    )
    gain_held[...] = low(wide.T)
    for slot, target in enumerate((grad_mine, grad_other)):
        copy = pltpu.make_async_copy(gain_held, target.at[:, 2 * model :], out_sems.at[8 + slot])
        copy.start()
        started.append(copy)
    for copy in started:
        copy.wait()


def row_copies(encoded, rows_ref, sems, segs):
    size = encoded.shape[0] // segs
    return [
        pltpu.make_async_copy(
            encoded.at[pl.ds(s * size, size)], rows_ref.at[pl.ds(s * size, size)], sems.at[s]
        )
        for s in range(segs)
    ]


def block_copy(encoded, rows_ref, sems, groups, s):
    size = encoded.shape[0] // groups.shape[1]
    at = pl.ds(pl.multiple_of(groups[0, s] * size, size), size)
    return pltpu.make_async_copy(encoded.at[at], rows_ref.at[at], sems.at[s])


def chunk_copies(pairs, sems, c):
    at = (slice(None), pl.ds(pl.multiple_of(c * CHUNK, CHUNK), CHUNK), slice(None))
    return [pltpu.make_async_copy(source.at[at], target.at[at], sems.at[n, c]) for n, (source, target) in enumerate(pairs)]


def list_chunks(starts, table):
    def query(s, count):
        begin, end = starts[0, s], starts[0, s + 1]

        def chunk(c, count):
            table[0, count] = c * CHUNK
            table[1, count] = s
            table[2, count] = (c == begin >> 4).astype(jnp.int32)
            table[3, count] = ((c * CHUNK >= begin) | (begin & (CHUNK - 1) == 0)).astype(jnp.int32)
            return count + 1

        return lax.fori_loop(begin >> 4, (end + CHUNK - 1) >> 4, chunk, count)

    return lax.fori_loop(0, starts.shape[1] - 1, query, 0)


def listed(starts, table, at):
    s = table[1, at]
    return pl.multiple_of(table[0, at], CHUNK), s, starts[0, s], starts[0, s + 1]


def in_segment(token, begin, end, heads):
    row = lax.broadcasted_iota(jnp.int32, (heads, CHUNK, 1), 1) + token
    return (row >= begin) & (row < end)


def pair_weight(kept, number, j):
    per_half = kept.shape[-1] // PAIR
    columns = slice((j % per_half) * PAIR, (j % per_half + 1) * PAIR)
    at = (number, j // per_half) + (slice(None),) * (len(kept.shape) - 3) + (columns,)
    return kept[at].reshape(-1, PAIR)


def cross_forward_kernel(
    pieces, me_ref, starts, groups, after_self, gains, encoded, *refs,
):
    first, second = refs[:pieces], refs[pieces : 2 * pieces]
    queries, context, after_cross, normed_out, probs_hbm, mixed_hbm, spread_hbm = refs[2 * pieces : 2 * pieces + 7]
    probs_out, mixed_out, spread_out, rows_ref, kept, table, sems, weight_sems, out_sems = refs[2 * pieces + 7 :]
    heads, tokens, model = spread_out.shape
    segs = groups.shape[1]
    block_rows = encoded.shape[0] // segs
    copies = piece_copies(me_ref[0], ((1, first), (2, second)), kept, weight_sems)
    early, late = copies[: 2 * pieces], copies[2 * pieces :]
    for copy in early:
        copy.start()
    for s in range(segs):
        block_copy(encoded, rows_ref, sems, groups, s).start()
    leaving = [
        pltpu.make_async_copy(source, target, out_sems.at[n])
        for n, (source, target) in enumerate(
            ((spread_out, spread_hbm), (probs_out, probs_hbm), (mixed_out, mixed_hbm))
        )
    ]
    for copy in late:
        copy.start()
    normed = low(normalize(after_self[...], gains[1:2, :]))
    for copy in early:
        copy.wait()
    queries[...] = low(times(normed, kept, 0))
    for j in range(heads // 2):
        block = queries[:, j * PAIR : (j + 1) * PAIR] * jnp.bfloat16(0.125)
        spread = low(contract(pair_rows(block), pair_weight(kept, 1, j), 1, 1))
        spread_out[2 * j] = spread[:tokens]
        spread_out[2 * j + 1] = spread[tokens:]
    leaving[0].start()

    count = list_chunks(starts, table)

    def two_chunks(i, carry):
        places = [2 * i, jnp.minimum(2 * i + 1, count - 1)]
        for n, place in enumerate(places):

            @pl.when((2 * i + n < count) & (table[2, place] == 1))
            def _():
                block_copy(encoded, rows_ref, sems, groups, table[1, place]).wait()

        found, scores, blocks = [], [], []
        for place in places:
            token, s, begin, end = listed(starts, table, place)
            base = pl.multiple_of(groups[0, s] * block_rows, block_rows)
            found.append((token, begin, end))
            blocks.append(rows_ref[pl.ds(base, block_rows), :])
            left = spread_out[:, pl.ds(token, CHUNK), :].reshape(heads * CHUNK, model)
            scores.append(contract(left, blocks[-1], 1, 1))
        for (token, begin, end), score, rows in zip(found, scores, blocks):
            weights = jnp.exp(score - jnp.max(score, axis=-1, keepdims=True))
            totals = jnp.sum(weights, axis=-1, keepdims=True)
            probs = low(weights * (1.0 / totals))
            mixed = low(contract(probs, rows, 1, 0))
            inside = in_segment(token, begin, end, heads)
            at = (slice(None), pl.ds(token, CHUNK), slice(None))
            probs = probs.reshape(heads, CHUNK, block_rows)
            mixed = mixed.reshape(heads, CHUNK, model)
            probs_out[at] = jnp.where(inside, probs, probs_out[at])
            mixed_out[at] = jnp.where(inside, mixed, mixed_out[at])
        return carry

    lax.fori_loop(0, (count + 1) >> 1, two_chunks, 0)
    for copy in leaving[1:]:
        copy.start()
    for copy in late:
        copy.wait()
    for j in range(heads // 2):
        both = jnp.concatenate([mixed_out[2 * j], mixed_out[2 * j + 1]], axis=0)
        found = contract(both, pair_weight(kept, 2, j), 1, 0)
        context[:, j * PAIR : (j + 1) * PAIR] = low(pair_lanes(found))
    after_cross[...] = after_self[...] + times(context[...], kept, 3)
    normed_out[...] = low(normalize(after_cross[...], gains[2:3, :]))
    for copy in leaving:
        copy.wait()


def cross_backward_first(
    pieces, me_ref, after_cross, gains, cotangent, pull_mine, pull_theirs, context, mixed_hbm, *refs,
):
    second, refs = refs[:pieces], refs[pieces:]
    grad_after, gain_grad, grad_context_out, pulled_hbm, grad_mine, grad_other = refs[:6]
    mixed, pulled_ref, kept, held, weight_sems, out_sems = refs[6:]
    core = me_ref[0] & 1
    heads, tokens, model = pulled_ref.shape
    copies = piece_copies(me_ref[0], ((2, second),), kept, weight_sems)
    copies = copies[pieces:] + copies[:pieces]
    coming = pltpu.make_async_copy(mixed_hbm, mixed, out_sems.at[4])
    for copy in copies + [coming]:
        copy.start()
    grad_normed = pull_mine[...] + pull_theirs[...].astype(jnp.float32)
    grad_values, found_gain = norm_backward(after_cross[...], gains[2:3, :], grad_normed)
    grad_after[...] = cotangent[...].astype(jnp.float32) + grad_values
    gain_grad[0:1, :] = found_gain
    branch = low(grad_after[...])
    grad_into(context[...], branch, held, 1)
    started = []

    def send(number):
        for copy in grad_copies(core, (grad_mine, grad_other), held, number, out_sems, (0, 2)):
            copy.start()
            started.append(copy)

    send(1)
    for copy in copies:
        copy.wait()
    grad_context_out[...] = low(times_back(branch, kept, 1))
    coming.wait()
    per_half = held.shape[-1] // PAIR
    for j in range(heads // 2):
        columns = slice((j % per_half) * PAIR, (j % per_half + 1) * PAIR)
        rows = pair_rows(grad_context_out[:, j * PAIR : (j + 1) * PAIR])
        both = jnp.concatenate([mixed[2 * j], mixed[2 * j + 1]], axis=0)
        held[0, j // per_half, :, columns] = low(contract(both, rows, 0, 0))
        pulled = low(contract(rows, pair_weight(kept, 0, j), 1, 1))
        pulled_ref[2 * j] = pulled[:tokens]
        pulled_ref[2 * j + 1] = pulled[tokens:]
    send(0)
    leaving = pltpu.make_async_copy(pulled_ref, pulled_hbm, out_sems.at[5])
    leaving.start()
    started.append(leaving)
    for copy in started:
        copy.wait()


def cross_backward_second(
    pieces, me_ref, starts, groups, grad_after, after_self, gains, ffn_gain_grad, queries, encoded,
    probs_hbm, pulled_hbm, late_mine, late_other, *refs,
):
    first, refs = refs[:pieces], refs[pieces:]
    grad_self, gain_grads, score_hbm, grad_mine, grad_other = refs[:5]
    probs_ref, pulled_ref, score_out, rows_ref, moved_ref, kept, held, table = refs[5:13]
    sems, weight_sems, out_sems, chunk_sems = refs[13:]
    core = me_ref[0] & 1
    heads, tokens, model = pulled_ref.shape
    segs = groups.shape[1]
    block_rows = encoded.shape[0] // segs
    half = kept.shape[-1]
    chunk_pairs = ((pulled_hbm, pulled_ref), (probs_hbm, probs_ref))
    block_copy(encoded, rows_ref, sems, groups, 0).start()
    for c in range(tokens // CHUNK):
        for copy in chunk_copies(chunk_pairs, chunk_sems, c):
            copy.start()
        if c % 2 and c // 2 + 1 < segs:
            block_copy(encoded, rows_ref, sems, groups, c // 2 + 1).start()
    copies = piece_copies(me_ref[0], ((1, first),), kept, weight_sems)
    for copy in copies:
        copy.start()
    started = []

    def send(number):
        for copy in grad_copies(core, (grad_mine, grad_other), held, number, out_sems, (1, 3)):
            copy.start()
            started.append(copy)


    count = list_chunks(starts, table)

    def two_chunks(i, carry):
        places = [2 * i, jnp.minimum(2 * i + 1, count - 1)]
        for n, place in enumerate(places):

            @pl.when((2 * i + n < count) & (table[2, place] == 1))
            def _():
                block_copy(encoded, rows_ref, sems, groups, table[1, place]).wait()

            @pl.when((2 * i + n < count) & (table[3, place] == 1))
            def _():
                for copy in chunk_copies(chunk_pairs, chunk_sems, table[0, place] >> 4):
                    copy.wait()

        found, prob_grads, blocks = [], [], []
        for place in places:
            token, s, begin, end = listed(starts, table, place)
            base = pl.multiple_of(groups[0, s] * block_rows, block_rows)
            blocks.append(rows_ref[pl.ds(base, block_rows), :])
            at = (slice(None), pl.ds(token, CHUNK), slice(None))
            inside = in_segment(token, begin, end, heads)
            found.append((at, inside))
            pulled = jnp.where(inside, pulled_ref[at], jnp.zeros((), jnp.bfloat16))
            prob_grads.append(contract(pulled.reshape(heads * CHUNK, model), blocks[-1], 1, 1))
        for (at, inside), prob_grad, rows in zip(found, prob_grads, blocks):
            wide = probs_ref[at].reshape(heads * CHUNK, block_rows).astype(jnp.float32)
            inner = jnp.sum(wide * prob_grad, axis=-1, keepdims=True)
            score_grad = low(wide * (prob_grad - inner))
            moved = low(contract(score_grad, rows, 1, 0)).reshape(heads, CHUNK, model)
            moved_ref[at] = jnp.where(inside, moved, moved_ref[at])
            score_grad = score_grad.reshape(heads, CHUNK, block_rows)
            score_out[at] = jnp.where(inside, score_grad, score_out[at])
        return carry

    lax.fori_loop(0, (count + 1) >> 1, two_chunks, 0)
    leaving = pltpu.make_async_copy(score_out, score_hbm, out_sems.at[4])
    leaving.start()
    started.append(leaving)
    for copy in copies:
        copy.wait()
    found = []
    per_half = half // PAIR
    for j in range(heads // 2):
        columns = slice((j % per_half) * PAIR, (j % per_half + 1) * PAIR)
        both = jnp.concatenate([moved_ref[2 * j], moved_ref[2 * j + 1]], axis=0)
        found.append(low(pair_lanes(contract(both, pair_weight(kept, 1, j), 1, 0)) * 0.125))
        block = queries[:, j * PAIR : (j + 1) * PAIR] * jnp.bfloat16(0.125)
        held[1, j // per_half, :, columns] = low(contract(both, pair_rows(block), 0, 0))
    send(1)
    grad_queries = jnp.concatenate(found, axis=1)
    values = after_self[...]
    grad_into(low(normalize(values, gains[1:2, :])), grad_queries, held, 0)
    send(0)
    grad_values, grad_gain = norm_backward(values, gains[1:2, :], times_back(grad_queries, kept, 0))
    grad_self[...] = grad_after[...] + grad_values
    gain_grads[0:1, :] = grad_gain
    gain_grads[1:2, :] = ffn_gain_grad[0:1, :]
    for copy in started:
        copy.wait()


def rows_backward_kernel(
    starts, groups, score_hbm, probs_hbm, spread_hbm, pulled_hbm, grad_rows,
    score_grads, probs_ref, spread, pulled_ref, sum_ref, row_sems, chunk_sems,
):
    heads, tokens, model = spread.shape
    segs = groups.shape[1]
    block_rows = grad_rows.shape[0] // segs

    chunk_pairs = (
        (score_hbm, score_grads), (probs_hbm, probs_ref), (spread_hbm, spread), (pulled_hbm, pulled_ref),
    )
    for c in range(tokens // CHUNK):
        for copy in chunk_copies(chunk_pairs, chunk_sems, c):
            copy.start()

    def write_out(s):
        slot = s & 1
        base = pl.multiple_of(groups[0, s] * block_rows, block_rows)
        return pltpu.make_async_copy(
            sum_ref.at[slot], grad_rows.at[pl.ds(base, block_rows)], row_sems.at[slot]
        )

    def segment(s, begin):
        end = starts[0, s + 1]
        slot = s & 1

        @pl.when(s >= 2)
        def _():
            write_out(s - 2).wait()

        def terms(c):
            @pl.when((c * CHUNK >= begin) | (begin & (CHUNK - 1) == 0))
            def _():
                for copy in chunk_copies(chunk_pairs, chunk_sems, c):
                    copy.wait()

            token = pl.multiple_of(c * CHUNK, CHUNK)
            at = (slice(None), pl.ds(token, CHUNK), slice(None))
            inside = in_segment(token, begin, end, heads)
            zero = jnp.zeros((), jnp.bfloat16)
            scores = jnp.where(inside, score_grads[at], zero).reshape(heads * CHUNK, block_rows)
            left = jnp.concatenate([scores, probs_ref[at].reshape(heads * CHUNK, block_rows)], axis=0)
            right = jnp.concatenate(
                [jnp.where(inside, piece[at], zero).reshape(heads * CHUNK, model) for piece in (spread, pulled_ref)],
                axis=0,
            )
            return contract(left, right, 0, 0)

        def chunk(c, carry):
            sum_ref[slot] += terms(c)
            return carry

        first = begin >> 4
        sum_ref[slot] = terms(first)
        lax.fori_loop(first + 1, (end + CHUNK - 1) >> 4, chunk, 0)
        write_out(s).start()
        return end

    lax.fori_loop(0, segs, segment, 0)
    for s in range(segs - 2, segs):
        write_out(s).wait()


def gelu_both(values):
    scale = 0.7978845608028654
    square = values * values
    bend = jnp.tanh(scale * (values + 0.044715 * (square * values)))
    half = 0.5 * (1.0 + bend)
    slope = half + 0.5 * values * (1.0 - bend * bend) * (scale * (1.0 + 3.0 * 0.044715 * square))
    return values * half, slope


def ffn_kernel(
    direct,
    me_ref, normed, normed_theirs, cotangent, cotangent_theirs, *refs,
):
    sources, refs = (refs[:8], refs[8:]) if direct else (refs[:2], refs[2:])
    out_mine, out_other, pull_mine, pull_other, grad_mine, grad_other = refs[:6]
    kept_in, kept_down, held_in, held_down, sems, out_sems = refs[6:]
    core = me_ref[0] & 1
    x_bit = (me_ref[0] >> 2) & 1
    blocks, groups, unused, width = held_in.shape
    model = held_in.shape[1] * held_in.shape[2]
    count = normed.shape[0]
    if direct:
        copies = []
        for n, source in enumerate(sources):
            place = core if n < 4 else 1 - core
            at = x_bit ^ (n >> 1 & 1)
            lead = (slice(None),) * (len(source.shape) - 2)
            target = kept_in.at[(place,) + lead + (at,)] if n % 2 == 0 else kept_down.at[lead + (at, place)]
            copies.append(pltpu.make_async_copy(source, target, sems.at[n]))
    else:
        copies = [
            pltpu.make_async_copy(source, target, sems.at[n])
            for n, (source, target) in enumerate(zip(sources, (kept_in, kept_down)))
        ]
    for copy in copies:
        copy.start()
    tokens = jnp.concatenate([normed[...], normed_theirs[...]], axis=0)
    pull = jnp.concatenate([cotangent[...], cotangent_theirs[...]], axis=0)
    for copy in copies:
        copy.wait()
    total = grad_tokens = None
    started = []
    for b in range(blocks):
        weight_up = kept_in[b].reshape(model, width)
        part = slice(b * groups // blocks, (b + 1) * groups // blocks) if direct else slice(0, 1)
        if direct:
            weight_down = kept_down[b].reshape(width, model)
        else:
            weight_down = kept_down[0, 0, b * width : (b + 1) * width]
        activated, slope = gelu_both(contract(tokens, weight_up, 1, 0))
        activated = low(activated)
        grad_act = low(contract(pull, weight_down, 1, 1)).astype(jnp.float32)
        grad_pre = low(slope * grad_act)
        added = contract(grad_pre, weight_up, 1, 1)
        grad_tokens = added if b == 0 else grad_tokens + added
        added = contract(activated, weight_down, 1, 0)
        total = added if b == 0 else total + added
        held_in[b] = low(contract(tokens, grad_pre, 0, 0)).reshape(held_in.shape[1:])
        grad_down = low(contract(activated, pull, 0, 0))
        if direct:
            held_down[part] = grad_down.reshape((groups // blocks,) + held_down.shape[1:])
        else:
            held_down[0, 0, b * width : (b + 1) * width] = grad_down
    if direct:
        rows = held_down.shape[2]
        targets = (
            (held_in.at[1 - core], grad_other.at[:, :rows]),
            (held_down.at[:, 1 - core], grad_other.at[:, rows:]),
            (held_in.at[core], grad_mine.at[:, :rows]),
            (held_down.at[:, core], grad_mine.at[:, rows:]),
        )
    else:
        targets = ((held_in, grad_mine), (held_down, grad_other))
    started = [pltpu.make_async_copy(source, target, out_sems.at[n]) for n, (source, target) in enumerate(targets)]
    for copy in started:
        copy.start()
    out_mine[...] = total[:count]
    out_other[...] = low(total[count:])
    pull_mine[...] = grad_tokens[:count]
    pull_other[...] = low(grad_tokens[count:])
    for copy in started:
        copy.wait()

VMEM = pl.BlockSpec(memory_space=pltpu.VMEM)
SMEM = pl.BlockSpec(memory_space=pltpu.SMEM)
HBM = pl.BlockSpec(memory_space=pltpu.HBM)
ANY = pl.BlockSpec(memory_space=pl.ANY)


def shaped(shape, dtype):
    return jax.ShapeDtypeStruct(shape, dtype)


def call(kernel, name, flops, in_specs, out_specs, out_shape, scratch, aliases={}, room=VMEM_BYTES):
    return pl.pallas_call(
        kernel,
        out_shape=out_shape,
        in_specs=in_specs,
        out_specs=out_specs,
        scratch_shapes=scratch,
        compiler_params=pltpu.CompilerParams(vmem_limit_bytes=room),
        cost_estimate=pl.CostEstimate(flops=flops, bytes_accessed=1_000_000, transcendentals=0),
        name=name,
        input_output_aliases=aliases,
    )


AXES = ("dp", "fsdp")


def swap_with(piece, mask, devices):
    pairs = [(index, index ^ mask) for index in range(devices)]
    return lax.ppermute(piece, AXES, pairs)


def bit_of(me, bit):
    return (me >> bit) & 1


def pair_up(mine, theirs, my_bit, axis):
    first = jnp.where(my_bit == 0, mine, theirs)
    second = jnp.where(my_bit == 0, theirs, mine)
    return jnp.stack([first, second], axis=axis)


def arranged(found, bits, me):
    found = {mask: [block] for mask, block in found.items()}
    for n, bit in enumerate(sorted(bits)):
        low_side = bit_of(me, bit) == 0
        merged = {}
        for mask in found:
            if not mask >> n & 1:
                both = list(zip(found[mask], found[mask | 1 << n]))
                merged[mask] = [jnp.where(low_side, x, y) for x, y in both] + [
                    jnp.where(low_side, y, x) for x, y in both
                ]
        found = merged
    return jnp.stack(found[0])


def wide_mask(mask, bits):
    return sum(1 << bit for n, bit in enumerate(sorted(bits)) if mask >> n & 1)


def exchange(send, bits, me, devices):
    found = {0: send(0)}
    for mask in range(1, 1 << len(bits)):
        found[mask] = swap_with(send(mask), wide_mask(mask, bits), devices)
    return arranged(found, bits, me)


def gather_line(block, bits, me, devices):
    if len(bits) > 2:
        held = block[None]
        for bit in sorted(bits):
            theirs = swap_with(held, 1 << bit, devices)
            held = pair_up(held, theirs, bit_of(me, bit), 0).reshape((-1,) + block.shape)
        return held
    return exchange(lambda mask: block, bits, me, devices)


def taken(source, places, columns):
    array, bits, offset = source
    begin = [places[bit] if bit in places else 0 for bit in bits] + [0, offset + columns[0]]
    size = [1 if bit in places else 2 for bit in bits] + [array.shape[-2], columns[1] - columns[0]]
    part = lax.dynamic_slice(array, begin, size)
    return part.reshape([2 for bit in bits if bit not in places] + size[-2:])


def summed(entry, places):
    sources, columns = entry
    total = None
    for source in sources:
        part = taken(source, places, columns).astype(jnp.float32)
        total = part if total is None else total + part
    return total


def with_brought(entry, theirs, bit, done):
    sources, columns = entry
    bits = [other for other in sources[0][1] if other not in done and other != bit]
    return (sources + [(theirs, bits, -columns[0])], columns)


def sum_over(entries, bit, done, me, devices):
    places = {other: bit_of(me, other) for other in done}
    send = [low(summed(entry, {**places, bit: 1 - bit_of(me, bit)})) for entry in entries]
    theirs = swap_with(jnp.concatenate(send, axis=-1), 1 << bit, devices)
    found, at = [], 0
    for sources, columns in entries:
        bits = [other for other in sources[0][1] if other not in done and other != bit]
        found.append((sources + [(theirs, bits, at - columns[0])], columns))
        at += columns[1] - columns[0]
    return found


def combine(me_word, outputs):
    arrays, buffers, plan, shapes = [], {}, [], []
    for pieces, dtype in outputs:
        at, steps = 0, []
        for (sources, columns), flips, late in pieces:
            keys = []
            for array, bits, offset in sources:
                number = next((n for n, other in enumerate(arrays) if other is array), len(arrays))
                if number == len(arrays):
                    arrays.append(array)
                picked = tuple(flips.get(bit) for bit in bits)
                key = (number, tuple(bits), picked, offset + columns[0], columns[1] - columns[0])
                buffers.setdefault(key, len(buffers))
                keys.append(key)
            steps.append((at, keys, late))
            at += columns[1] - columns[0]
        sources = pieces[0][0][0]
        left = [bit for bit in sources[0][1] if bit not in pieces[0][1] and bit not in pieces[0][2]]
        plan.append(steps)
        shapes.append(shaped((2,) * len(left) + (sources[0][0].shape[-2], at), dtype))

    def kernel(me_ref, *refs):
        inputs, targets = refs[: len(arrays)], refs[len(arrays) : len(arrays) + len(outputs)]
        held, sems = refs[len(arrays) + len(outputs) : -1], refs[-1]
        me = me_ref[0]
        copies = {}
        for key, n in buffers.items():
            number, bits, picked, begin, width = key
            index = tuple(
                slice(None) if flip is None else ((me >> bit) & 1) ^ flip for bit, flip in zip(bits, picked)
            )
            copies[key] = pltpu.make_async_copy(
                inputs[number].at[index + (slice(None), slice(begin, begin + width))], held[n], sems.at[n]
            )
            copies[key].start()
        waited = set()
        for target, steps in zip(targets, plan):
            for at, keys, late in steps:
                total = None
                for key in keys:
                    if key not in waited:
                        copies[key].wait()
                        waited.add(key)
                    left = [bit for bit, flip in zip(key[1], key[2]) if flip is None]
                    index = tuple(((me >> bit) & 1) ^ late[bit] if bit in late else slice(None) for bit in left)
                    part = held[buffers[key]][index].astype(jnp.float32)
                    total = part if total is None else total + part
                target[..., at : at + keys[0][4]] = total.astype(target.dtype)

    scratch = []
    for number, bits, picked, begin, width in buffers:
        lead = tuple(2 for flip in picked if flip is None)
        scratch.append(pltpu.VMEM(lead + (arrays[number].shape[-2], width), arrays[number].dtype))
    scratch.append(pltpu.SemaphoreType.DMA((len(buffers),)))
    found = call(
        kernel, "combine", 1_000_000, [SMEM] + [ANY] * len(arrays), [VMEM] * len(outputs), tuple(shapes), scratch
    )(me_word, *arrays)
    return list(found)


def line_terms(me_word, entries, bits, done, devices):
    flips = {bit: 0 for bit in done}
    if len(bits) > 2:
        for bit in sorted(bits):
            entries = sum_over(entries, bit, list(flips), me_word[0], devices)
            flips[bit] = 0
        return combine(me_word, [([(entry, flips, {}) for entry in entries], jnp.float32)])
    masks = [wide_mask(mask, bits) for mask in range(1 << len(bits))]
    outputs = [
        (
            [(entry, flips, {bit: mask >> bit & 1 for bit in bits}) for entry in entries],
            jnp.bfloat16 if mask else jnp.float32,
        )
        for mask in masks
    ]
    blocks = combine(me_word, outputs)
    return blocks[:1] + [swap_with(block, mask, devices) for block, mask in zip(blocks[1:], masks[1:])]


def core_rows(total, core, devices):
    rows = total.shape[0] // 2
    keep = lax.dynamic_slice_in_dim(total, core * rows, rows, axis=0)
    send = lax.dynamic_slice_in_dim(total, (1 - core) * rows, rows, axis=0)
    theirs = swap_with(send, 1, devices)
    return jnp.where(core == 0, keep, theirs), jnp.where(core == 0, theirs, keep)


def per_device(
    fsdp,
    devices,
    tokens,
    encoded,
    segment_ids,
    passage_group,
    cotangent,
    self_gain,
    cross_gain,
    ffn_gain,
    self_query,
    self_key,
    self_value,
    self_out,
    cross_query,
    cross_key,
    cross_value,
    cross_out,
    ffn_in,
    ffn_out,
):
    me = lax.axis_index("dp") * fsdp + lax.axis_index("fsdp")
    core = bit_of(me, 0)
    core_word = core.reshape(1).astype(jnp.int32)
    me_word = me.reshape(1).astype(jnp.int32)
    bounds = lax.broadcasted_iota(jnp.int32, (1, passage_group.shape[1] + 1), 1)
    starts = jnp.sum((segment_ids[0, :, None] < bounds).astype(jnp.int32), axis=0, keepdims=True)
    chip_bits = list(range(1, devices.bit_length() - 1))
    line_bits = [bit for bit in reversed(chip_bits) if bit > 2]
    pair_orders = ([2, 1], [1, 2])
    count, model = tokens.shape
    encoder_count = encoded.shape[0]
    hidden_units = ffn_in.shape[1]
    heads = model // HEAD
    half = model // 2
    segs = passage_group.shape[1]
    low_type, wide_type = jnp.bfloat16, jnp.float32

    def my_columns(matrix, owner):
        width = matrix.shape[-1] // 2
        return lax.dynamic_slice_in_dim(matrix, owner * width, width, axis=matrix.ndim - 1)

    barrier = lax.optimization_barrier
    gains = jnp.stack([self_gain, cross_gain, ffn_gain], axis=1)
    gains = jnp.pad(gains, ((0, 0), (0, PAIR - 3)))
    shards = [self_query, self_key, self_value, self_out, cross_query, cross_key, cross_value, cross_out]
    rows_in = ffn_in.shape[0]
    rows_down = ffn_out.shape[0]
    direct = rows_down % 16 == 0
    chip_groups = devices // 4
    group_bits = [0, 1]
    packed = shaped((rows_in, len(shards) * half + PAIR + 2 * model), low_type)
    send, keep = call(
        pack_kernel, "pack", 0, [SMEM] + [VMEM] * 10, [VMEM] * 2, (packed, packed), []
    )(core_word, *shards, gains, ffn_in)
    theirs = swap_with(send, 1, devices)
    chip_block = pair_up(keep, theirs, core, 0).reshape(-1, keep.shape[1])
    self_block = jnp.concatenate([chip_block[:, : 2 * model], chip_block[:, 4 * model : 4 * model + PAIR]], axis=1)
    in_halves = chip_block[:, 4 * model + PAIR :].reshape(2 * rows_in, chip_groups // 2, 2, 2 * rows_down)
    in_halves = in_halves.swapaxes(1, 2).reshape(2 * rows_in, 2 * model)
    cross_block = chip_block[:, 2 * model : 4 * model]

    def double(held, bit, first_bit, me):
        place = 1 if first_bit is None or bit > first_bit else 2
        return pair_up(held, swap_with(held, 1 << bit, devices), bit_of(me, bit), place)

    def first_step(line, width):
        return [double(part, order[0], None, me) for part, order in zip((line[:, :, :width], line[:, :, width:]), pair_orders)]

    def second_step(parts):
        return [
            double(part, order[1], order[0], me).reshape(-1, part.shape[-1])
            for part, order in zip(parts, pair_orders)
        ]

    cotangent_theirs = swap_with(cotangent, 2, devices)

    def block_for(array, mask):
        first = [bit_of(me, 1) ^ (mask >> 1 & 1), core ^ (mask & 1)]
        return lax.dynamic_slice(array, first + [0, 0], (1, 1) + array.shape[2:]).reshape(array.shape[2:])

    ffn_steps = line_bits + [2]

    def merged(held, theirs, steps, number):
        bit = steps[number]
        place = sum(1 for other in steps[:number] if other > bit)
        return pair_up(held, theirs, bit_of(me, bit), place)

    def brought(held, steps, number):
        return swap_with(held, 1 << steps[number], devices)

    def half_at(array, place):
        return lax.dynamic_slice_in_dim(array, place * model, model, axis=1)

    self_line = gather_line(self_block, line_bits, me, devices)
    self_line, cross_held, in_halves, cotangent_theirs, down_held = barrier(
        (self_line, cross_block, in_halves, cotangent_theirs, ffn_out)
    )
    y_bit = bit_of(me, 1)
    in_theirs = swap_with(half_at(in_halves, 1 - y_bit), 2, devices)
    last = len(line_bits) - 1
    self_parts = first_step(self_line, model)
    for number in range(last):
        cross_held = merged(cross_held, brought(cross_held, line_bits, number), line_bits, number)
        down_held = merged(down_held, brought(down_held, ffn_steps, number), ffn_steps, number)
    self_parts, cross_held, in_theirs, down_held = barrier((self_parts, cross_held, in_theirs, down_held))
    in_held = pair_up(half_at(in_halves, y_bit), in_theirs, y_bit, 0).reshape(4 * rows_in, model)
    self_theirs = [brought(part, [2, 1, 2], n + 1) for n, part in enumerate(self_parts)]
    cross_line = merged(cross_held, brought(cross_held, line_bits, last), line_bits, last)
    cross_line = cross_line.reshape((-1,) + cross_block.shape)
    for number in range(last):
        in_held = merged(in_held, brought(in_held, ffn_steps, number), ffn_steps, number)
    down_theirs = brought(down_held, ffn_steps, last)
    cross_line, in_held, down_theirs, self_theirs = barrier((cross_line, in_held, down_theirs, self_theirs))
    cross_parts = first_step(cross_line, model)
    in_theirs = brought(in_held, ffn_steps, last)
    cross_parts, in_theirs = barrier((cross_parts, in_theirs))
    in_held = merged(in_held, in_theirs, ffn_steps, last)
    down_held = merged(down_held, down_theirs, ffn_steps, last)

    def second_merge(parts, theirs):
        return [
            pair_up(part, other, bit_of(me, order[1]), 1 if order[1] > order[0] else 2).reshape(-1, part.shape[-1])
            for part, other, order in zip(parts, theirs, pair_orders)
        ]

    self_mine = second_merge(self_parts, self_theirs)
    cross_theirs = [brought(part, [2, 1, 2], n + 1) for n, part in enumerate(cross_parts)]
    self_weights = [(mine, swap_with(mine[:, :model], 1, devices)) for mine in self_mine]

    gain_rows = self_weights[1][0][:, model : model + 8].T.astype(wide_type)
    self_flat = self_weights[0] + self_weights[1]

    dma = pltpu.SemaphoreType.DMA
    weights_kept = pltpu.VMEM((4, 2, model, half), low_type)
    projected, context_one, after_self = call(
        self_forward_kernel,
        "self_forward",
        2 * count * model * model * 5,
        [SMEM, VMEM, VMEM, VMEM] + [ANY] * 4,
        [VMEM] * 3,
        (
            shaped((3, count, model), low_type),
            shaped((count, model), low_type),
            shaped((count, model), wide_type),
        ),
        [weights_kept, dma((8,))],
        room=MIDDLE_BYTES,
    )(core_word, segment_ids, tokens, gain_rows, *self_flat)

    cross_direct = 2 * rows_in % 16 == 0
    cross_sibling = [swap_with(part, 1, devices) for part in cross_parts]
    cross_theirs, cross_sibling, in_held, down_held, after_self = barrier(
        (cross_theirs, cross_sibling, in_held, down_held, after_self)
    )
    in_theirs, down_theirs = swap_with(in_held, 4, devices), swap_with(down_held, 4, devices)
    in_sibling, down_sibling = swap_with(in_held, 1, devices), swap_with(down_held, 1, devices)
    sibling_theirs = [swap_with(theirs, 1, devices) for theirs in cross_theirs]
    if cross_direct:
        cross_weights = list(zip(cross_parts, cross_theirs, cross_sibling, sibling_theirs))
        cross_rows = cross_parts[0].shape[:1] + (2, 2, 2 * rows_in, half)
    else:
        cross_weights = list(
            zip(second_merge(cross_parts, cross_theirs), second_merge(cross_sibling, sibling_theirs))
        )
        cross_rows = (model, half)
    pieces = len(cross_weights[0])
    cross_flat = list(cross_weights[0]) + list(cross_weights[1])
    cross_kept = pltpu.VMEM((4, 2) + cross_rows, low_type)
    pair_kept = pltpu.VMEM((2, 2) + cross_rows, low_type)

    per_token = (heads, count, model)
    probs_shape = (heads, count, encoder_count // segs)
    probs_kept, tokens_kept = pltpu.VMEM(probs_shape, low_type), pltpu.VMEM(per_token, low_type)
    chunk_count = count // CHUNK
    chunk_table = pltpu.SMEM((4, chunk_count + segs), jnp.int32)
    queries_two, context_two, after_cross, normed_three, probs, mixed, spread = call(
        functools.partial(cross_forward_kernel, pieces),
        "cross_forward",
        12_000_000_000,
        [SMEM, SMEM, SMEM, VMEM, VMEM] + [HBM] * (1 + 2 * pieces),
        [VMEM] * 4 + [HBM] * 3,
        (
            shaped((count, model), low_type),
            shaped((count, model), low_type),
            shaped((count, model), wide_type),
            shaped((count, model), low_type),
            shaped(probs_shape, low_type),
            shaped(per_token, low_type),
            shaped(per_token, low_type),
        ),
        [
            probs_kept, tokens_kept, tokens_kept, pltpu.VMEM(encoded.shape, low_type), cross_kept,
            chunk_table, dma((segs,)), dma((4 * pieces,)), dma((3,)),
        ],
    )(me_word, starts, passage_group, after_self, gain_rows, encoded, *cross_flat)

    normed_theirs = swap_with(normed_three, 2, devices)
    in_theirs, down_theirs, in_sibling, down_sibling, normed_theirs = barrier(
        (in_theirs, down_theirs, in_sibling, down_sibling, normed_theirs)
    )
    in_fourth, down_fourth = swap_with(in_theirs, 1, devices), swap_with(down_theirs, 1, devices)
    ffn_pieces = [in_held, down_held, in_theirs, down_theirs, in_sibling, down_sibling, in_fourth, down_fourth]
    half_units = hidden_units // 2
    high = (2,) * (len(chip_bits) - 1)
    if direct:
        in_shape = (2, chip_groups, rows_down, model)
        down_shape = (chip_groups, 2, rows_down, model)
        ffn_weights = ffn_pieces
        grad_shapes = (shaped((chip_groups, 2 * rows_down, model), low_type),) * 2
    else:
        in_shape, down_shape = (2, 1, model, model), (1, 1, half_units, model)
        ffn_mine = [
            pair_up(held, theirs, bit_of(me, 2), len(line_bits)).reshape((chip_groups,) + held.shape[-2:])
            for held, theirs in ((in_held, in_theirs), (down_held, down_theirs))
        ]
        ffn_sibling = [
            pair_up(held, theirs, bit_of(me, 2), len(line_bits)).reshape((chip_groups,) + held.shape[-2:])
            for held, theirs in ((in_sibling, in_fourth), (down_sibling, down_fourth))
        ]
        ffn_weights = (
            pair_up(ffn_mine[0], ffn_sibling[0], core, 0).reshape(in_shape),
            pair_up(ffn_mine[1], ffn_sibling[1], core, 1).reshape(down_shape),
        )
        grad_shapes = (shaped(in_shape, low_type), shaped(down_shape, low_type))
    token_shapes = (shaped((count, model), wide_type), shaped((count, model), low_type))
    out_mine, out_other, pull_mine, pull_other, ffn_grad, ffn_other = call(
        functools.partial(ffn_kernel, direct),
        "ffn",
        4_000_000_000,
        [SMEM] + [VMEM] * 4 + [ANY] * len(ffn_weights),
        [VMEM] * 4 + [HBM] * 2,
        token_shapes + token_shapes + grad_shapes,
        [
            pltpu.VMEM((2,) + high + in_shape[2:] if direct else in_shape, low_type),
            pltpu.VMEM(high + down_shape[1:] if direct else down_shape, low_type),
            pltpu.VMEM(in_shape, low_type),
            pltpu.VMEM(down_shape, low_type),
            dma((8,)),
            dma((4,)),
        ],
        room=MIDDLE_BYTES,
    )(me_word, normed_three, normed_theirs, cotangent, cotangent_theirs, *ffn_weights)
    pull_theirs = swap_with(pull_other, 2, devices)
    if not direct:
        in_parts = ffn_grad.reshape(2, chip_groups, 4 * rows_in, model)
        down_parts = ffn_other.reshape(chip_groups, 2, rows_down, model).swapaxes(0, 1)
        both = jnp.concatenate([in_parts, down_parts], axis=2)
        ffn_grad, ffn_other = (
            lax.dynamic_index_in_dim(both, place, 0, keepdims=False) for place in (core, 1 - core)
        )
    ffn_theirs = swap_with(ffn_other, 1, devices)
    high_bits = [bit for bit in sorted(chip_bits, reverse=True) if bit > 1]

    def group_source(array):
        return (array.reshape((2,) * len(high_bits) + array.shape[-2:]), high_bits, 0)

    ffn_entry = ([group_source(ffn_grad), group_source(ffn_theirs)], (0, model))
    ffn_send = low(summed(ffn_entry, {2: 1 - bit_of(me, 2)}))
    pull_theirs, ffn_send, out_other = barrier((pull_theirs, ffn_send, out_other))
    ffn_sum = [with_brought(ffn_entry, swap_with(ffn_send, 4, devices), 2, [])]
    out_theirs = swap_with(out_other, 2, devices)

    all_bits = sorted(chip_bits, reverse=True)

    def chips_of(array):
        return array.reshape((2,) * len(all_bits) + (array.shape[0] >> len(all_bits), array.shape[-1]))

    def entry_of(mine, theirs, begin, end):
        return ([(chips_of(mine), all_bits, 0), (chips_of(theirs), all_bits, 0)], (begin, end))

    def first_sum(sides):
        return [sum_over(entries, order[0], [], me, devices) for entries, order in zip(sides, pair_orders)]

    def second_sum(sides):
        return [sum_over(entries, order[1], order[:1], me, devices) for entries, order in zip(sides, pair_orders)]

    def received(sides):
        return [entries[0][0][-1][0] for entries in sides]

    def with_received(sides, arrays):
        return [
            [(sources[:-1] + [(array,) + sources[-1][1:]], columns) for sources, columns in entries]
            for entries, array in zip(sides, arrays)
        ]

    grads_shape = shaped((model, 2 * model), low_type)
    rows_kept = pltpu.VMEM(encoded.shape, low_type)
    two_kept = pltpu.VMEM((2, 2, model, half), low_type)
    grad_after_cross, ffn_gain_grad, grad_context, pulled, late_mine, late_other = call(
        functools.partial(cross_backward_first, pieces),
        "cross_backward_first",
        1_000_000_000,
        [SMEM] + [VMEM] * 6 + [HBM] * (1 + pieces),
        [VMEM] * 3 + [HBM] * 3,
        (
            shaped((count, model), wide_type),
            shaped((8, model), wide_type),
            shaped((count, model), low_type),
            shaped(per_token, low_type),
            grads_shape,
            grads_shape,
        ),
        [tokens_kept, tokens_kept, pair_kept, two_kept, dma((2 * pieces,)), dma((6,))],
    )(
        me_word, after_cross, gain_rows, cotangent, pull_mine, pull_theirs, context_two, mixed, *cross_weights[1]
    )
    grad_after_self, gain_grads, score_grads, cross_mine_grad, cross_other_grad = call(
        functools.partial(cross_backward_second, pieces),
        "cross_backward_second",
        3_000_000_000,
        [SMEM, SMEM, SMEM] + [VMEM] * 5 + [HBM] * (5 + pieces),
        [VMEM] * 2 + [HBM] * 3,
        (
            shaped((count, model), wide_type),
            shaped((8, model), wide_type),
            shaped(probs_shape, low_type),
            grads_shape,
            grads_shape,
        ),
        [
            probs_kept, tokens_kept, probs_kept, rows_kept, tokens_kept, pair_kept, two_kept,
            chunk_table, dma((segs,)), dma((2 * pieces,)), dma((5,)), dma((2, chunk_count)),
        ],
        aliases={11: 3, 12: 4},
    )(
        me_word, starts, passage_group, grad_after_cross, after_self, gain_rows, ffn_gain_grad,
        queries_two, encoded, probs, pulled, late_mine, late_other, *cross_weights[0],
    )
    arrays, grad_after_self, cross_mine_grad, cross_other_grad, out_theirs = barrier(
        (received([ffn_sum]), grad_after_self, cross_mine_grad, cross_other_grad, out_theirs)
    )
    block_out = low(after_cross + (out_mine + out_theirs.astype(wide_type)))
    ffn_sum = with_received([ffn_sum], arrays)[0]
    ffn_done = [2]
    for bit in sorted(line_bits)[:-1]:
        ffn_sum = sum_over(ffn_sum, bit, ffn_done, me, devices)
        ffn_done = ffn_done + [bit]
    cross_theirs_grad = swap_with(cross_other_grad, 1, devices)

    with_gains = shaped((model, 2 * model + PAIR), low_type)
    tokens_grad, self_mine, self_other = call(
        self_backward_kernel,
        "self_backward",
        2 * count * model * model * 10,
        [SMEM] + [VMEM] * 7 + [ANY] * 4,
        [VMEM] + [HBM] * 2,
        (shaped((count, model), wide_type), with_gains, with_gains),
        [weights_kept, weights_kept, pltpu.VMEM((model, PAIR), low_type), dma((8,)), dma((10,))],
        room=MIDDLE_BYTES,
    )(
        core_word, segment_ids, tokens, gain_rows, grad_after_self, gain_grads, projected, context_one,
        *self_flat,
    )
    arrays, cross_theirs_grad, self_mine, self_other = barrier(
        (received([ffn_sum]), cross_theirs_grad, self_mine, self_other)
    )
    ffn_sum = with_received([ffn_sum], arrays)[0]
    ffn_sum = sum_over(ffn_sum, max(line_bits), ffn_done, me, devices)
    self_theirs = swap_with(self_other, 1, devices)
    crossed = [
        [entry_of(cross_mine_grad, cross_theirs_grad, *cut)] for cut in ((0, model), (model, 2 * model))
    ]
    crossed = first_sum(crossed)
    self_theirs, score_grads = barrier((self_theirs, score_grads))
    attention = [
        [entry_of(self_mine, self_theirs, *cut)] for cut in ((0, model), (model, 2 * model + PAIR))
    ]
    attention = first_sum(attention)
    encoded_grad = call(
        rows_backward_kernel,
        "rows_backward",
        3_000_000_000,
        [SMEM, SMEM] + [HBM] * 4,
        HBM,
        shaped(encoded.shape, wide_type),
        [
            probs_kept, probs_kept, tokens_kept, tokens_kept,
            pltpu.VMEM((2, encoder_count // segs, model), wide_type), dma((2,)), dma((4, chunk_count)),
        ],
    )(starts, passage_group, score_grads, probs, spread, pulled)
    crossed_arrays, arrays, ffn_arrays, encoded_grad = barrier(
        (received(crossed), received(attention), received([ffn_sum]), encoded_grad)
    )
    ffn_sum = with_received([ffn_sum], ffn_arrays)[0]
    ffn_rows = summed(ffn_sum[0], {bit: bit_of(me, bit) for bit in high_bits})
    summed_down = ffn_rows[4 * rows_in :]
    in_parts = ffn_rows[: 4 * rows_in].reshape(2, 2, rows_in, model)
    in_parts = exchange(lambda mask: block_for(in_parts, mask), group_bits, me, devices)
    in_parts = in_parts.reshape(2, 2, rows_in, chip_groups // 2, 2 * rows_down)
    summed_in = in_parts.transpose(2, 1, 3, 0, 4).reshape(rows_in, hidden_units)
    crossed, attention = with_received(crossed, crossed_arrays), with_received(attention, arrays)
    attention = second_sum([crossed[side] + attention[side] for side in range(2)])
    terms = line_terms(me_word, attention[0] + attention[1], line_bits, [2, 1], devices)
    terms, summed_in = barrier((terms, summed_in))
    found = terms[0]
    for term in terms[1:]:
        found = found + term.astype(wide_type)
    keep = lax.dynamic_slice_in_dim(found, core * rows_in, rows_in, axis=0)
    send = lax.dynamic_slice_in_dim(found, (1 - core) * rows_in, rows_in, axis=0)
    (
        summed_cv, summed_cq, summed_query, summed_key, summed_co, summed_ck, summed_value, summed_out, own_gains,
    ) = call(
        spread_kernel,
        "spread",
        1_000_000,
        [SMEM, VMEM, VMEM],
        [VMEM] * 9,
        (shaped((rows_in, model), wide_type),) * 8 + (shaped((rows_in, PAIR), wide_type),),
        [],
        room=SMALL_BYTES,
    )(core_word, keep, swap_with(send, 1, devices))
    return (
        block_out,
        tokens_grad,
        encoded_grad,
        own_gains[:, 0],
        own_gains[:, 1],
        own_gains[:, 2],
        summed_query,
        summed_key,
        summed_value,
        summed_out,
        summed_cq,
        summed_ck,
        summed_cv,
        summed_co,
        summed_in,
        summed_down,
    )


def solution(mesh):
    return jax.shard_map(
        functools.partial(per_device, mesh.shape["fsdp"], mesh.size),
        mesh=mesh,
        in_specs=(
            P(("dp", "fsdp"), None),
            P(("dp", "fsdp"), None),
            P(("dp", "fsdp"), None),
            P(("dp", "fsdp"), None),
            P(("dp", "fsdp"), None),
            P(("dp", "fsdp")),
            P(("dp", "fsdp")),
            P(("dp", "fsdp")),
            P(("dp", "fsdp"), None),
            P(("dp", "fsdp"), None),
            P(("dp", "fsdp"), None),
            P(("dp", "fsdp"), None),
            P(("dp", "fsdp"), None),
            P(("dp", "fsdp"), None),
            P(("dp", "fsdp"), None),
            P(("dp", "fsdp"), None),
            P(("dp", "fsdp"), None),
            P(("dp", "fsdp"), None),
        ),
        out_specs=(
            P(("dp", "fsdp"), None),
            P(("dp", "fsdp"), None),
            P(("dp", "fsdp"), None),
            P(("dp", "fsdp")),
            P(("dp", "fsdp")),
            P(("dp", "fsdp")),
            P(("dp", "fsdp"), None),
            P(("dp", "fsdp"), None),
            P(("dp", "fsdp"), None),
            P(("dp", "fsdp"), None),
            P(("dp", "fsdp"), None),
            P(("dp", "fsdp"), None),
            P(("dp", "fsdp"), None),
            P(("dp", "fsdp"), None),
            P(("dp", "fsdp"), None),
            P(("dp", "fsdp"), None),
        ),
        check_vma=False,
    )
```

```python
import functools

import jax
import jax.numpy as jnp
from jax import lax
from jax.experimental import pallas as pl
from jax.experimental.layout import Layout, with_layout_constraint
from jax.experimental.pallas import tpu as pltpu
from jax.sharding import PartitionSpec as P

HEAD = 64
CHUNK = 16
PAIR = 2 * HEAD
epsilon = 1e-06
masked_score = -1e30
VMEM_BYTES = 60 << 20
MIDDLE_BYTES = 32 << 20
SMALL_BYTES = 20 << 20


def contract(left, right, left_dim, right_dim):
    return lax.dot_general(
        left, right, (((left_dim,), (right_dim,)), ((), ())), preferred_element_type=jnp.float32
    )


def low(values):
    return values.astype(jnp.bfloat16)


def normalize(values, gain_row):
    return values * lax.rsqrt(jnp.mean(values * values, axis=-1, keepdims=True) + epsilon) * gain_row


def norm_backward(values, gain_row, grad):
    scale = lax.rsqrt(jnp.mean(values * values, axis=-1, keepdims=True) + epsilon)
    grad_gain = jnp.sum(grad * values * scale, axis=0, keepdims=True)
    weighted = gain_row * grad
    inner = jnp.mean(weighted * values, axis=-1, keepdims=True)
    return scale * weighted - values * (scale * scale * scale) * inner, grad_gain


def pair_rows(block):
    lane = lax.broadcasted_iota(jnp.int32, block.shape, 1)
    zero = jnp.zeros_like(block)
    return jnp.concatenate(
        [jnp.where(lane < HEAD, block, zero), jnp.where(lane >= HEAD, block, zero)], axis=0
    )


def pair_lanes(both):
    rows = both.shape[0] // 2
    lane = lax.broadcasted_iota(jnp.int32, (rows, both.shape[1]), 1)
    return jnp.where(lane < HEAD, both[:rows], both[rows:])


def weight_copies(core, sources, kept, sems):
    half = kept.shape[-1]
    copies = []
    for number in range(kept.shape[0]):
        for side, source in enumerate(sources[number // 2]):
            place = core if side == 0 else 1 - core
            copies.append(
                pltpu.make_async_copy(
                    source.at[:, (number % 2) * half : (number % 2 + 1) * half],
                    kept.at[number, place],
                    sems.at[2 * number + side],
                )
            )
    return copies


def piece_copies(me, pairs, kept, sems):
    core = me & 1
    half = kept.shape[-1]
    copies = []
    for number in range(kept.shape[0]):
        bit, pieces = pairs[number // 2]
        columns = slice((number % 2) * half, (number % 2 + 1) * half)
        for n, piece in enumerate(pieces):
            whole = len(pieces) == 2
            place = core if n < len(pieces) // 2 else 1 - core
            target = kept.at[number, place]
            if not whole:
                at = ((me >> bit) & 1) ^ (n & 1)
                target = kept.at[number, place, :, :, at] if bit == 1 else kept.at[number, place, :, at]
                piece = piece.at[:, :, :, columns]
            else:
                piece = piece.at[:, columns]
            copies.append(pltpu.make_async_copy(piece, target, sems.at[len(pieces) * number + n]))
    return copies


def whole_rows(kept, number, side):
    return kept[number, side].reshape(-1, kept.shape[-1])


def times(left, kept, number):
    return jnp.concatenate([contract(left, whole_rows(kept, number, side), 1, 0) for side in range(2)], axis=1)


def times_back(left, kept, number):
    half = kept.shape[-1]
    return contract(left[:, :half], whole_rows(kept, number, 0), 1, 1) + contract(
        left[:, half:], whole_rows(kept, number, 1), 1, 1
    )


def grad_into(left, right, held, number):
    half = held.shape[-1]
    for side in range(2):
        held[number, side] = low(contract(left, right[:, side * half : (side + 1) * half], 0, 0))


def grad_copies(core, targets, held, number, sems, place_of=None):
    half = held.shape[-1]
    at = number if place_of is None else place_of[number]
    copies = []
    for side, target in enumerate(targets):
        place = core if side == 0 else 1 - core
        copies.append(
            pltpu.make_async_copy(
                held.at[number, place],
                target.at[:, at * half : (at + 1) * half],
                sems.at[2 * number + side],
            )
        )
    return copies


def spread_kernel(matrices, core_ref, keep, theirs, *targets):
    core = core_ref[0]
    half = targets[0].shape[1] // 2
    for number, target in enumerate(targets[:matrices]):
        columns = slice(number * half, (number + 1) * half)
        for side in range(2):
            target[:, side * half : (side + 1) * half] = jnp.where(core == side, keep[:, columns], theirs[:, columns])
    for target in targets[matrices:]:
        target[...] = keep[:, matrices * half :]


def pack_kernel(core_ref, *refs):
    shards, gains, wide_shard, (send, keep) = refs[:-4], refs[-4], refs[-3], refs[-2:]
    core = core_ref[0]
    half = shards[0].shape[1] // 2
    wide = wide_shard.shape[1] // 2
    at = len(shards) * half
    for target, place in ((send, 1 - core), (keep, core)):
        for number, shard in enumerate(shards):
            target[:, number * half : (number + 1) * half] = shard[:, pl.ds(pl.multiple_of(place * half, PAIR), half)]
        target[:, at : at + PAIR] = gains[...]
        target[:, at + PAIR :] = wide_shard[:, pl.ds(pl.multiple_of(place * wide, PAIR), wide)]


def self_mask(ids_row):
    tokens = ids_row.shape[1]
    wide = jnp.broadcast_to(ids_row.astype(jnp.float32), (tokens, tokens))
    query = lax.broadcasted_iota(jnp.int32, (tokens, tokens), 0)
    key = lax.broadcasted_iota(jnp.int32, (tokens, tokens), 1)
    allowed = jnp.where((wide == wide.T) & (key <= query), 1.0, 0.0)
    return jnp.concatenate([allowed, allowed], axis=0) > 0.5


def self_probs(queries, keys, allowed):
    scores = jnp.where(allowed, contract(pair_rows(queries), keys, 1, 1) * 0.125, masked_score)
    weights = jnp.exp(scores - jnp.max(scores, axis=-1, keepdims=True))
    return weights / jnp.sum(weights, axis=-1, keepdims=True)


def self_forward_kernel(
    core_ref, ids, tokens, gains, first_mine, first_sibling, second_mine, second_sibling,
    projected, context, after, kept, sems,
):
    core = core_ref[0]
    copies = weight_copies(
        core, ((first_mine, first_sibling), (second_mine, second_sibling)), kept, sems
    )
    for copy in copies:
        copy.start()
    model = tokens.shape[1]
    hidden = tokens[...].astype(jnp.float32)
    normed = low(normalize(hidden, gains[0:1, :]))
    for number in range(3):
        copies[2 * number].wait()
        copies[2 * number + 1].wait()
        projected[number] = low(times(normed, kept, number))
    allowed = self_mask(ids[...])
    for j in range(model // PAIR):
        columns = slice(j * PAIR, (j + 1) * PAIR)
        probs = self_probs(projected[0, :, columns], projected[1, :, columns], allowed)
        context[:, columns] = low(pair_lanes(contract(low(probs), projected[2, :, columns], 1, 0)))
    copies[6].wait()
    copies[7].wait()
    after[...] = hidden + times(context[...], kept, 3)


def self_backward_kernel(
    core_ref, ids, tokens, gains, grad_after, gain_grads, projected, context,
    first_mine, first_sibling, second_mine, second_sibling,
    tokens_grad, grad_mine, grad_other,
    kept, held, gain_held, sems, out_sems,
):
    core = core_ref[0]
    copies = weight_copies(
        core, ((first_mine, first_sibling), (second_mine, second_sibling)), kept, sems
    )
    for copy in copies:
        copy.start()
    model = tokens.shape[1]
    count = tokens.shape[0]
    hidden = tokens[...].astype(jnp.float32)
    normed = low(normalize(hidden, gains[0:1, :]))
    branch = low(grad_after[...])
    started = []

    def send(number):
        for copy in grad_copies(core, (grad_mine, grad_other), held, number, out_sems):
            copy.start()
            started.append(copy)

    grad_into(context[...], branch, held, 3)
    send(3)
    for copy in copies:
        copy.wait()
    grad_context = low(times_back(branch, kept, 3))
    allowed = self_mask(ids[...])
    found = ([], [], [])
    for j in range(model // PAIR):
        columns = slice(j * PAIR, (j + 1) * PAIR)
        queries, keys = projected[0, :, columns], projected[1, :, columns]
        probs = self_probs(queries, keys, allowed)
        pulled = pair_rows(grad_context[:, columns])
        prob_grad = contract(pulled, projected[2, :, columns], 1, 1)
        inner = jnp.sum(probs * prob_grad, axis=-1, keepdims=True)
        score_grad = low(probs * (prob_grad - inner))
        found[0].append(low(pair_lanes(contract(score_grad, keys, 1, 0)) * 0.125))
        found[1].append(low(contract(score_grad, pair_rows(queries), 0, 0) * 0.125))
        found[2].append(low(contract(low(probs), pulled, 0, 0)))
    grad_normed = None
    for number in range(3):
        whole = jnp.concatenate(found[number], axis=1)
        grad_into(normed, whole, held, number)
        send(number)
        part = times_back(whole, kept, number)
        grad_normed = part if grad_normed is None else grad_normed + part
    grad_hidden, grad_gain = norm_backward(hidden, gains[0:1, :], grad_normed)
    tokens_grad[...] = grad_after[...] + grad_hidden
    row = lax.broadcasted_iota(jnp.int32, (count, model), 0)
    others = gain_grads[...]
    wide = jnp.where(
        row == 0, grad_gain, jnp.where(row == 1, others[0:1], jnp.where(row == 2, others[1:2], 0.0))
    )
    gain_held[...] = low(wide.T)
    for slot, target in enumerate((grad_mine, grad_other)):
        copy = pltpu.make_async_copy(gain_held, target.at[:, 2 * model :], out_sems.at[8 + slot])
        copy.start()
        started.append(copy)
    for copy in started:
        copy.wait()


def row_copies(encoded, rows_ref, sems, segs):
    size = encoded.shape[0] // segs
    return [
        pltpu.make_async_copy(
            encoded.at[pl.ds(s * size, size)], rows_ref.at[pl.ds(s * size, size)], sems.at[s]
        )
        for s in range(segs)
    ]


def block_copy(encoded, rows_ref, sems, groups, s):
    size = encoded.shape[0] // groups.shape[1]
    at = pl.ds(pl.multiple_of(groups[0, s] * size, size), size)
    return pltpu.make_async_copy(encoded.at[at], rows_ref.at[at], sems.at[s])


def chunk_copies(pairs, sems, c):
    at = (slice(None), pl.ds(pl.multiple_of(c * CHUNK, CHUNK), CHUNK), slice(None))
    return [pltpu.make_async_copy(source.at[at], target.at[at], sems.at[n, c]) for n, (source, target) in enumerate(pairs)]


def list_chunks(starts, table):
    def query(s, count):
        begin, end = starts[0, s], starts[0, s + 1]

        def chunk(c, count):
            table[0, count] = c * CHUNK
            table[1, count] = s
            table[2, count] = (c == begin >> 4).astype(jnp.int32)
            table[3, count] = ((c * CHUNK >= begin) | (begin & (CHUNK - 1) == 0)).astype(jnp.int32)
            return count + 1

        return lax.fori_loop(begin >> 4, (end + CHUNK - 1) >> 4, chunk, count)

    return lax.fori_loop(0, starts.shape[1] - 1, query, 0)


def listed(starts, table, at):
    s = table[1, at]
    return pl.multiple_of(table[0, at], CHUNK), s, starts[0, s], starts[0, s + 1]


def in_segment(token, begin, end, heads):
    row = lax.broadcasted_iota(jnp.int32, (heads, CHUNK, 1), 1) + token
    return (row >= begin) & (row < end)


def pair_weight(kept, number, j):
    per_half = kept.shape[-1] // PAIR
    columns = slice((j % per_half) * PAIR, (j % per_half + 1) * PAIR)
    at = (number, j // per_half) + (slice(None),) * (len(kept.shape) - 3) + (columns,)
    return kept[at].reshape(-1, PAIR)


def cross_forward_kernel(
    pieces, me_ref, starts, groups, after_self, gains, encoded, *refs,
):
    first, second = refs[:pieces], refs[pieces : 2 * pieces]
    queries, context, after_cross, normed_out, probs_hbm, mixed_hbm, spread_hbm = refs[2 * pieces : 2 * pieces + 7]
    probs_out, mixed_out, spread_out, rows_ref, kept, table, sems, weight_sems, out_sems = refs[2 * pieces + 7 :]
    heads, tokens, model = spread_out.shape
    segs = groups.shape[1]
    block_rows = encoded.shape[0] // segs
    copies = piece_copies(me_ref[0], ((1, first), (2, second)), kept, weight_sems)
    early, late = copies[: 2 * pieces], copies[2 * pieces :]
    for copy in early:
        copy.start()
    for s in range(segs):
        block_copy(encoded, rows_ref, sems, groups, s).start()
    leaving = [
        pltpu.make_async_copy(source, target, out_sems.at[n])
        for n, (source, target) in enumerate(
            ((spread_out, spread_hbm), (probs_out, probs_hbm), (mixed_out, mixed_hbm))
        )
    ]
    for copy in late:
        copy.start()
    normed = low(normalize(after_self[...], gains[1:2, :]))
    for copy in early:
        copy.wait()
    queries[...] = low(times(normed, kept, 0))
    for j in range(heads // 2):
        block = queries[:, j * PAIR : (j + 1) * PAIR] * jnp.bfloat16(0.125)
        spread = low(contract(pair_rows(block), pair_weight(kept, 1, j), 1, 1))
        spread_out[2 * j] = spread[:tokens]
        spread_out[2 * j + 1] = spread[tokens:]
    leaving[0].start()

    count = list_chunks(starts, table)

    def two_chunks(i, carry):
        places = [2 * i, jnp.minimum(2 * i + 1, count - 1)]
        for n, place in enumerate(places):

            @pl.when((2 * i + n < count) & (table[2, place] == 1))
            def _():
                block_copy(encoded, rows_ref, sems, groups, table[1, place]).wait()

        found, scores, blocks = [], [], []
        for place in places:
            token, s, begin, end = listed(starts, table, place)
            base = pl.multiple_of(groups[0, s] * block_rows, block_rows)
            found.append((token, begin, end))
            blocks.append(rows_ref[pl.ds(base, block_rows), :])
            left = spread_out[:, pl.ds(token, CHUNK), :].reshape(heads * CHUNK, model)
            scores.append(contract(left, blocks[-1], 1, 1))
        for (token, begin, end), score, rows in zip(found, scores, blocks):
            weights = jnp.exp(score - jnp.max(score, axis=-1, keepdims=True))
            totals = jnp.sum(weights, axis=-1, keepdims=True)
            probs = low(weights * (1.0 / totals))
            mixed = low(contract(probs, rows, 1, 0))
            inside = in_segment(token, begin, end, heads)
            at = (slice(None), pl.ds(token, CHUNK), slice(None))
            probs = probs.reshape(heads, CHUNK, block_rows)
            mixed = mixed.reshape(heads, CHUNK, model)
            probs_out[at] = jnp.where(inside, probs, probs_out[at])
            mixed_out[at] = jnp.where(inside, mixed, mixed_out[at])
        return carry

    lax.fori_loop(0, (count + 1) >> 1, two_chunks, 0)
    for copy in leaving[1:]:
        copy.start()
    for copy in late:
        copy.wait()
    for j in range(heads // 2):
        both = jnp.concatenate([mixed_out[2 * j], mixed_out[2 * j + 1]], axis=0)
        found = contract(both, pair_weight(kept, 2, j), 1, 0)
        context[:, j * PAIR : (j + 1) * PAIR] = low(pair_lanes(found))
    after_cross[...] = after_self[...] + times(context[...], kept, 3)
    normed_out[...] = low(normalize(after_cross[...], gains[2:3, :]))
    for copy in leaving:
        copy.wait()


def cross_backward_first(
    pieces, me_ref, after_cross, gains, cotangent, pull_mine, pull_theirs, context, mixed_hbm, *refs,
):
    second, refs = refs[:pieces], refs[pieces:]
    grad_after, gain_grad, grad_context_out, pulled_hbm, grad_mine, grad_other = refs[:6]
    mixed, pulled_ref, kept, held, weight_sems, out_sems = refs[6:]
    core = me_ref[0] & 1
    heads, tokens, model = pulled_ref.shape
    copies = piece_copies(me_ref[0], ((2, second),), kept, weight_sems)
    copies = copies[pieces:] + copies[:pieces]
    coming = pltpu.make_async_copy(mixed_hbm, mixed, out_sems.at[4])
    for copy in copies + [coming]:
        copy.start()
    grad_normed = pull_mine[...] + pull_theirs[...].astype(jnp.float32)
    grad_values, found_gain = norm_backward(after_cross[...], gains[2:3, :], grad_normed)
    grad_after[...] = cotangent[...].astype(jnp.float32) + grad_values
    gain_grad[0:1, :] = found_gain
    branch = low(grad_after[...])
    grad_into(context[...], branch, held, 1)
    started = []

    def send(number):
        for copy in grad_copies(core, (grad_mine, grad_other), held, number, out_sems, (0, 2)):
            copy.start()
            started.append(copy)

    send(1)
    for copy in copies:
        copy.wait()
    grad_context_out[...] = low(times_back(branch, kept, 1))
    coming.wait()
    per_half = held.shape[-1] // PAIR
    for j in range(heads // 2):
        columns = slice((j % per_half) * PAIR, (j % per_half + 1) * PAIR)
        rows = pair_rows(grad_context_out[:, j * PAIR : (j + 1) * PAIR])
        both = jnp.concatenate([mixed[2 * j], mixed[2 * j + 1]], axis=0)
        held[0, j // per_half, :, columns] = low(contract(both, rows, 0, 0))
        pulled = low(contract(rows, pair_weight(kept, 0, j), 1, 1))
        pulled_ref[2 * j] = pulled[:tokens]
        pulled_ref[2 * j + 1] = pulled[tokens:]
    send(0)
    leaving = pltpu.make_async_copy(pulled_ref, pulled_hbm, out_sems.at[5])
    leaving.start()
    started.append(leaving)
    for copy in started:
        copy.wait()


def cross_backward_second(
    pieces, me_ref, starts, groups, grad_after, after_self, gains, ffn_gain_grad, queries, encoded,
    probs_hbm, pulled_hbm, late_mine, late_other, *refs,
):
    first, refs = refs[:pieces], refs[pieces:]
    grad_self, gain_grads, score_hbm, grad_mine, grad_other = refs[:5]
    probs_ref, pulled_ref, score_out, rows_ref, moved_ref, kept, held, table = refs[5:13]
    sems, weight_sems, out_sems, chunk_sems = refs[13:]
    core = me_ref[0] & 1
    heads, tokens, model = pulled_ref.shape
    segs = groups.shape[1]
    block_rows = encoded.shape[0] // segs
    half = kept.shape[-1]
    chunk_pairs = ((pulled_hbm, pulled_ref), (probs_hbm, probs_ref))
    block_copy(encoded, rows_ref, sems, groups, 0).start()
    for c in range(tokens // CHUNK):
        for copy in chunk_copies(chunk_pairs, chunk_sems, c):
            copy.start()
        if c % 2 and c // 2 + 1 < segs:
            block_copy(encoded, rows_ref, sems, groups, c // 2 + 1).start()
    copies = piece_copies(me_ref[0], ((1, first),), kept, weight_sems)
    for copy in copies:
        copy.start()
    started = []

    def send(number):
        for copy in grad_copies(core, (grad_mine, grad_other), held, number, out_sems, (1, 3)):
            copy.start()
            started.append(copy)


    count = list_chunks(starts, table)

    def two_chunks(i, carry):
        places = [2 * i, jnp.minimum(2 * i + 1, count - 1)]
        for n, place in enumerate(places):

            @pl.when((2 * i + n < count) & (table[2, place] == 1))
            def _():
                block_copy(encoded, rows_ref, sems, groups, table[1, place]).wait()

            @pl.when((2 * i + n < count) & (table[3, place] == 1))
            def _():
                for copy in chunk_copies(chunk_pairs, chunk_sems, table[0, place] >> 4):
                    copy.wait()

        found, prob_grads, blocks = [], [], []
        for place in places:
            token, s, begin, end = listed(starts, table, place)
            base = pl.multiple_of(groups[0, s] * block_rows, block_rows)
            blocks.append(rows_ref[pl.ds(base, block_rows), :])
            at = (slice(None), pl.ds(token, CHUNK), slice(None))
            inside = in_segment(token, begin, end, heads)
            found.append((at, inside))
            pulled = jnp.where(inside, pulled_ref[at], jnp.zeros((), jnp.bfloat16))
            prob_grads.append(contract(pulled.reshape(heads * CHUNK, model), blocks[-1], 1, 1))
        for (at, inside), prob_grad, rows in zip(found, prob_grads, blocks):
            wide = probs_ref[at].reshape(heads * CHUNK, block_rows).astype(jnp.float32)
            inner = jnp.sum(wide * prob_grad, axis=-1, keepdims=True)
            score_grad = low(wide * (prob_grad - inner))
            moved = low(contract(score_grad, rows, 1, 0)).reshape(heads, CHUNK, model)
            moved_ref[at] = jnp.where(inside, moved, moved_ref[at])
            score_grad = score_grad.reshape(heads, CHUNK, block_rows)
            score_out[at] = jnp.where(inside, score_grad, score_out[at])
        return carry

    lax.fori_loop(0, (count + 1) >> 1, two_chunks, 0)
    leaving = pltpu.make_async_copy(score_out, score_hbm, out_sems.at[4])
    leaving.start()
    started.append(leaving)
    for copy in copies:
        copy.wait()
    found = []
    per_half = half // PAIR
    for j in range(heads // 2):
        columns = slice((j % per_half) * PAIR, (j % per_half + 1) * PAIR)
        both = jnp.concatenate([moved_ref[2 * j], moved_ref[2 * j + 1]], axis=0)
        found.append(low(pair_lanes(contract(both, pair_weight(kept, 1, j), 1, 0)) * 0.125))
        block = queries[:, j * PAIR : (j + 1) * PAIR] * jnp.bfloat16(0.125)
        held[1, j // per_half, :, columns] = low(contract(both, pair_rows(block), 0, 0))
    send(1)
    grad_queries = jnp.concatenate(found, axis=1)
    values = after_self[...]
    grad_into(low(normalize(values, gains[1:2, :])), grad_queries, held, 0)
    send(0)
    grad_values, grad_gain = norm_backward(values, gains[1:2, :], times_back(grad_queries, kept, 0))
    grad_self[...] = grad_after[...] + grad_values
    gain_grads[0:1, :] = grad_gain
    gain_grads[1:2, :] = ffn_gain_grad[0:1, :]
    for copy in started:
        copy.wait()


def rows_backward_kernel(
    starts, groups, score_hbm, probs_hbm, spread_hbm, pulled_hbm, grad_rows,
    score_grads, probs_ref, spread, pulled_ref, sum_ref, row_sems, chunk_sems,
):
    heads, tokens, model = spread.shape
    segs = groups.shape[1]
    block_rows = grad_rows.shape[0] // segs

    chunk_pairs = (
        (score_hbm, score_grads), (probs_hbm, probs_ref), (spread_hbm, spread), (pulled_hbm, pulled_ref),
    )
    for c in range(tokens // CHUNK):
        for copy in chunk_copies(chunk_pairs, chunk_sems, c):
            copy.start()

    def write_out(s):
        slot = s & 1
        base = pl.multiple_of(groups[0, s] * block_rows, block_rows)
        return pltpu.make_async_copy(
            sum_ref.at[slot], grad_rows.at[pl.ds(base, block_rows)], row_sems.at[slot]
        )

    def segment(s, begin):
        end = starts[0, s + 1]
        slot = s & 1

        @pl.when(s >= 2)
        def _():
            write_out(s - 2).wait()

        def terms(c):
            @pl.when((c * CHUNK >= begin) | (begin & (CHUNK - 1) == 0))
            def _():
                for copy in chunk_copies(chunk_pairs, chunk_sems, c):
                    copy.wait()

            token = pl.multiple_of(c * CHUNK, CHUNK)
            at = (slice(None), pl.ds(token, CHUNK), slice(None))
            inside = in_segment(token, begin, end, heads)
            zero = jnp.zeros((), jnp.bfloat16)
            scores = jnp.where(inside, score_grads[at], zero).reshape(heads * CHUNK, block_rows)
            left = jnp.concatenate([scores, probs_ref[at].reshape(heads * CHUNK, block_rows)], axis=0)
            right = jnp.concatenate(
                [jnp.where(inside, piece[at], zero).reshape(heads * CHUNK, model) for piece in (spread, pulled_ref)],
                axis=0,
            )
            return contract(left, right, 0, 0)

        def chunk(c, carry):
            sum_ref[slot] += terms(c)
            return carry

        first = begin >> 4
        sum_ref[slot] = terms(first)
        lax.fori_loop(first + 1, (end + CHUNK - 1) >> 4, chunk, 0)
        write_out(s).start()
        return end

    lax.fori_loop(0, segs, segment, 0)
    for s in range(segs - 2, segs):
        write_out(s).wait()


def gelu_both(values):
    scale = 0.7978845608028654
    square = values * values
    bend = jnp.tanh(scale * (values + 0.044715 * (square * values)))
    half = 0.5 * (1.0 + bend)
    slope = half + 0.5 * values * (1.0 - bend * bend) * (scale * (1.0 + 3.0 * 0.044715 * square))
    return values * half, slope


def ffn_kernel(
    direct,
    me_ref, normed, normed_theirs, cotangent, cotangent_theirs, *refs,
):
    sources, refs = (refs[:8], refs[8:]) if direct else (refs[:2], refs[2:])
    out_mine, out_other, pull_mine, pull_other, grad_mine, grad_other = refs[:6]
    kept_in, kept_down, held_in, held_down, sems, out_sems = refs[6:]
    core = me_ref[0] & 1
    x_bit = (me_ref[0] >> 2) & 1
    blocks, groups, unused, width = held_in.shape
    model = held_in.shape[1] * held_in.shape[2]
    count = normed.shape[0]
    if direct:
        copies = []
        for n, source in enumerate(sources):
            place = core if n < 4 else 1 - core
            at = x_bit ^ (n >> 1 & 1)
            lead = (slice(None),) * (len(source.shape) - 2)
            target = kept_in.at[(place,) + lead + (at,)] if n % 2 == 0 else kept_down.at[lead + (at, place)]
            copies.append(pltpu.make_async_copy(source, target, sems.at[n]))
    else:
        copies = [
            pltpu.make_async_copy(source, target, sems.at[n])
            for n, (source, target) in enumerate(zip(sources, (kept_in, kept_down)))
        ]
    for copy in copies:
        copy.start()
    tokens = jnp.concatenate([normed[...], normed_theirs[...]], axis=0)
    pull = jnp.concatenate([cotangent[...], cotangent_theirs[...]], axis=0)
    for copy in copies:
        copy.wait()
    total = grad_tokens = None
    started = []
    for b in range(blocks):
        weight_up = kept_in[b].reshape(model, width)
        part = slice(b * groups // blocks, (b + 1) * groups // blocks) if direct else slice(0, 1)
        if direct:
            weight_down = kept_down[b].reshape(width, model)
        else:
            weight_down = kept_down[0, 0, b * width : (b + 1) * width]
        activated, slope = gelu_both(contract(tokens, weight_up, 1, 0))
        activated = low(activated)
        grad_act = low(contract(pull, weight_down, 1, 1)).astype(jnp.float32)
        grad_pre = low(slope * grad_act)
        added = contract(grad_pre, weight_up, 1, 1)
        grad_tokens = added if b == 0 else grad_tokens + added
        added = contract(activated, weight_down, 1, 0)
        total = added if b == 0 else total + added
        held_in[b] = low(contract(tokens, grad_pre, 0, 0)).reshape(held_in.shape[1:])
        grad_down = low(contract(activated, pull, 0, 0))
        if direct:
            held_down[part] = grad_down.reshape((groups // blocks,) + held_down.shape[1:])
        else:
            held_down[0, 0, b * width : (b + 1) * width] = grad_down
    if direct:
        rows = held_down.shape[2]
        targets = (
            (held_in.at[1 - core], grad_other.at[:, :rows]),
            (held_down.at[:, 1 - core], grad_other.at[:, rows:]),
            (held_in.at[core], grad_mine.at[:, :rows]),
            (held_down.at[:, core], grad_mine.at[:, rows:]),
        )
    else:
        targets = ((held_in, grad_mine), (held_down, grad_other))
    started = [pltpu.make_async_copy(source, target, out_sems.at[n]) for n, (source, target) in enumerate(targets)]
    for copy in started:
        copy.start()
    out_mine[...] = total[:count]
    out_other[...] = low(total[count:])
    pull_mine[...] = grad_tokens[:count]
    pull_other[...] = low(grad_tokens[count:])
    for copy in started:
        copy.wait()

VMEM = pl.BlockSpec(memory_space=pltpu.VMEM)
SMEM = pl.BlockSpec(memory_space=pltpu.SMEM)
HBM = pl.BlockSpec(memory_space=pltpu.HBM)
ANY = pl.BlockSpec(memory_space=pl.ANY)


def shaped(shape, dtype):
    return jax.ShapeDtypeStruct(shape, dtype)


def call(kernel, name, flops, in_specs, out_specs, out_shape, scratch, aliases={}, room=VMEM_BYTES):
    return pl.pallas_call(
        kernel,
        out_shape=out_shape,
        in_specs=in_specs,
        out_specs=out_specs,
        scratch_shapes=scratch,
        compiler_params=pltpu.CompilerParams(vmem_limit_bytes=room),
        cost_estimate=pl.CostEstimate(flops=flops, bytes_accessed=1_000_000, transcendentals=0),
        name=name,
        input_output_aliases=aliases,
    )


AXES = ("dp", "fsdp")


def swap_with(piece, mask, devices):
    pairs = [(index, index ^ mask) for index in range(devices)]
    return lax.ppermute(piece, AXES, pairs)


def bit_of(me, bit):
    return (me >> bit) & 1


def pair_up(mine, theirs, my_bit, axis):
    first = jnp.where(my_bit == 0, mine, theirs)
    second = jnp.where(my_bit == 0, theirs, mine)
    return jnp.stack([first, second], axis=axis)


def arranged(found, bits, me):
    found = {mask: [block] for mask, block in found.items()}
    for n, bit in enumerate(sorted(bits)):
        low_side = bit_of(me, bit) == 0
        merged = {}
        for mask in found:
            if not mask >> n & 1:
                both = list(zip(found[mask], found[mask | 1 << n]))
                merged[mask] = [jnp.where(low_side, x, y) for x, y in both] + [
                    jnp.where(low_side, y, x) for x, y in both
                ]
        found = merged
    return jnp.stack(found[0])


def wide_mask(mask, bits):
    return sum(1 << bit for n, bit in enumerate(sorted(bits)) if mask >> n & 1)


def exchange(send, bits, me, devices):
    found = {0: send(0)}
    for mask in range(1, 1 << len(bits)):
        found[mask] = swap_with(send(mask), wide_mask(mask, bits), devices)
    return arranged(found, bits, me)


def gather_line(block, bits, me, devices):
    if len(bits) > 2:
        held = block[None]
        for bit in sorted(bits):
            theirs = swap_with(held, 1 << bit, devices)
            held = pair_up(held, theirs, bit_of(me, bit), 0).reshape((-1,) + block.shape)
        return held
    return exchange(lambda mask: block, bits, me, devices)


def taken(source, places, columns):
    array, bits, offset = source
    begin = [places[bit] if bit in places else 0 for bit in bits] + [0, offset + columns[0]]
    size = [1 if bit in places else 2 for bit in bits] + [array.shape[-2], columns[1] - columns[0]]
    part = lax.dynamic_slice(array, begin, size)
    return part.reshape([2 for bit in bits if bit not in places] + size[-2:])


def summed(entry, places):
    sources, columns = entry
    total = None
    for source in sources:
        part = taken(source, places, columns).astype(jnp.float32)
        total = part if total is None else total + part
    return total


def with_brought(entry, theirs, bit, done):
    sources, columns = entry
    bits = [other for other in sources[0][1] if other not in done and other != bit]
    return (sources + [(theirs, bits, -columns[0])], columns)


def sends_of(entries, bit, done, me):
    places = {other: bit_of(me, other) for other in done}
    send = [low(summed(entry, {**places, bit: 1 - bit_of(me, bit)})) for entry in entries]
    send = jnp.concatenate(send, axis=-1)
    return with_layout_constraint(send, Layout(tuple(range(send.ndim))))


def sum_over(entries, bit, done, me, devices, send=None):
    theirs = swap_with(sends_of(entries, bit, done, me) if send is None else send, 1 << bit, devices)
    found, at = [], 0
    for sources, columns in entries:
        bits = [other for other in sources[0][1] if other not in done and other != bit]
        found.append((sources + [(theirs, bits, at - columns[0])], columns))
        at += columns[1] - columns[0]
    return found


def combine(me_word, outputs):
    arrays, buffers, plan, shapes = [], {}, [], []
    for pieces, dtype in outputs:
        at, steps = 0, []
        for (sources, columns), flips, late in pieces:
            keys = []
            for array, bits, offset in sources:
                number = next((n for n, other in enumerate(arrays) if other is array), len(arrays))
                if number == len(arrays):
                    arrays.append(array)
                picked = tuple(flips.get(bit) for bit in bits)
                key = (number, tuple(bits), picked, offset + columns[0], columns[1] - columns[0])
                buffers.setdefault(key, len(buffers))
                keys.append(key)
            steps.append((at, keys, late))
            at += columns[1] - columns[0]
        sources = pieces[0][0][0]
        left = [bit for bit in sources[0][1] if bit not in pieces[0][1] and bit not in pieces[0][2]]
        plan.append(steps)
        shapes.append(shaped((2,) * len(left) + (sources[0][0].shape[-2], at), dtype))

    def kernel(me_ref, *refs):
        inputs, targets = refs[: len(arrays)], refs[len(arrays) : len(arrays) + len(outputs)]
        held, sems = refs[len(arrays) + len(outputs) : -1], refs[-1]
        me = me_ref[0]
        copies = {}
        for key, n in buffers.items():
            number, bits, picked, begin, width = key
            index = tuple(
                slice(None) if flip is None else ((me >> bit) & 1) ^ flip for bit, flip in zip(bits, picked)
            )
            copies[key] = pltpu.make_async_copy(
                inputs[number].at[index + (slice(None), slice(begin, begin + width))], held[n], sems.at[n]
            )
            copies[key].start()
        waited = set()
        for target, steps in zip(targets, plan):
            for at, keys, late in steps:
                total = None
                for key in keys:
                    if key not in waited:
                        copies[key].wait()
                        waited.add(key)
                    left = [bit for bit, flip in zip(key[1], key[2]) if flip is None]
                    index = tuple(((me >> bit) & 1) ^ late[bit] if bit in late else slice(None) for bit in left)
                    part = held[buffers[key]][index].astype(jnp.float32)
                    total = part if total is None else total + part
                target[..., at : at + keys[0][4]] = total.astype(target.dtype)

    scratch = []
    for number, bits, picked, begin, width in buffers:
        lead = tuple(2 for flip in picked if flip is None)
        scratch.append(pltpu.VMEM(lead + (arrays[number].shape[-2], width), arrays[number].dtype))
    scratch.append(pltpu.SemaphoreType.DMA((len(buffers),)))
    found = call(
        kernel, "combine", 1_000_000, [SMEM] + [ANY] * len(arrays), [VMEM] * len(outputs), tuple(shapes), scratch
    )(me_word, *arrays)
    return list(found)


def line_blocks(me_word, entries, bits, done, devices):
    flips = {bit: 0 for bit in done}
    if len(bits) > 2:
        for bit in sorted(bits):
            entries = sum_over(entries, bit, list(flips), me_word[0], devices)
            flips[bit] = 0
        return combine(me_word, [([(entry, flips, {}) for entry in entries], jnp.float32)])
    outputs = []
    for mask in range(1 << len(bits)):
        wide = wide_mask(mask, bits)
        pieces = [(entry, flips, {bit: wide >> bit & 1 for bit in bits}) for entry in entries]
        outputs.append((pieces, jnp.bfloat16 if mask else jnp.float32))
    return combine(me_word, outputs)


def brought_blocks(blocks, bits, devices):
    return blocks[:1] + [
        swap_with(block, wide_mask(mask + 1, bits), devices) for mask, block in enumerate(blocks[1:])
    ]


def core_rows(total, core, devices):
    rows = total.shape[0] // 2
    keep = lax.dynamic_slice_in_dim(total, core * rows, rows, axis=0)
    send = lax.dynamic_slice_in_dim(total, (1 - core) * rows, rows, axis=0)
    theirs = swap_with(send, 1, devices)
    return jnp.where(core == 0, keep, theirs), jnp.where(core == 0, theirs, keep)


def per_device(
    fsdp,
    devices,
    tokens,
    encoded,
    segment_ids,
    passage_group,
    cotangent,
    self_gain,
    cross_gain,
    ffn_gain,
    self_query,
    self_key,
    self_value,
    self_out,
    cross_query,
    cross_key,
    cross_value,
    cross_out,
    ffn_in,
    ffn_out,
):
    me = lax.axis_index("dp") * fsdp + lax.axis_index("fsdp")
    core = bit_of(me, 0)
    core_word = core.reshape(1).astype(jnp.int32)
    me_word = me.reshape(1).astype(jnp.int32)
    bounds = lax.broadcasted_iota(jnp.int32, (1, passage_group.shape[1] + 1), 1)
    starts = jnp.sum((segment_ids[0, :, None] < bounds).astype(jnp.int32), axis=0, keepdims=True)
    chip_bits = list(range(1, devices.bit_length() - 1))
    line_bits = [bit for bit in reversed(chip_bits) if bit > 2]
    pair_orders = ([2, 1], [1, 2])
    count, model = tokens.shape
    encoder_count = encoded.shape[0]
    hidden_units = ffn_in.shape[1]
    heads = model // HEAD
    half = model // 2
    segs = passage_group.shape[1]
    low_type, wide_type = jnp.bfloat16, jnp.float32

    def my_columns(matrix, owner):
        width = matrix.shape[-1] // 2
        return lax.dynamic_slice_in_dim(matrix, owner * width, width, axis=matrix.ndim - 1)

    barrier = lax.optimization_barrier
    gains = jnp.stack([self_gain, cross_gain, ffn_gain], axis=1)
    gains = jnp.pad(gains, ((0, 0), (0, PAIR - 3)))
    shards = [self_query, self_key, self_value, self_out, cross_query, cross_key, cross_value, cross_out]
    rows_in = ffn_in.shape[0]
    rows_down = ffn_out.shape[0]
    direct = rows_down % 16 == 0
    chip_groups = devices // 4
    group_bits = [0, 1]
    packed = shaped((rows_in, len(shards) * half + PAIR + 2 * model), low_type)
    send, keep = call(
        pack_kernel, "pack", 0, [SMEM] + [VMEM] * 10, [VMEM] * 2, (packed, packed), []
    )(core_word, *shards, gains, ffn_in)
    theirs = swap_with(send, 1, devices)
    chip_block = pair_up(keep, theirs, core, 0).reshape(-1, keep.shape[1])
    self_block = jnp.concatenate([chip_block[:, : 2 * model], chip_block[:, 4 * model : 4 * model + PAIR]], axis=1)
    in_halves = chip_block[:, 4 * model + PAIR :].reshape(2 * rows_in, chip_groups // 2, 2, 2 * rows_down)
    in_halves = in_halves.swapaxes(1, 2).reshape(2 * rows_in, 2 * model)
    cross_block = chip_block[:, 2 * model : 4 * model]

    def double(held, bit, first_bit, me):
        place = 1 if first_bit is None or bit > first_bit else 2
        return pair_up(held, swap_with(held, 1 << bit, devices), bit_of(me, bit), place)

    def first_step(line, width):
        return [double(part, order[0], None, me) for part, order in zip((line[:, :, :width], line[:, :, width:]), pair_orders)]

    def second_step(parts):
        return [
            double(part, order[1], order[0], me).reshape(-1, part.shape[-1])
            for part, order in zip(parts, pair_orders)
        ]

    cotangent_theirs = swap_with(cotangent, 2, devices)

    def block_for(array, mask):
        first = [bit_of(me, 1) ^ (mask >> 1 & 1), core ^ (mask & 1)]
        return lax.dynamic_slice(array, first + [0, 0], (1, 1) + array.shape[2:]).reshape(array.shape[2:])

    ffn_steps = line_bits + [2]

    def merged(held, theirs, steps, number):
        bit = steps[number]
        place = sum(1 for other in steps[:number] if other > bit)
        return pair_up(held, theirs, bit_of(me, bit), place)

    def brought(held, steps, number):
        return swap_with(held, 1 << steps[number], devices)

    def half_at(array, place):
        return lax.dynamic_slice_in_dim(array, place * model, model, axis=1)

    self_line = gather_line(self_block, line_bits, me, devices)
    self_line, cross_held, in_halves, cotangent_theirs, down_held = barrier(
        (self_line, cross_block, in_halves, cotangent_theirs, ffn_out)
    )
    y_bit = bit_of(me, 1)
    in_theirs = swap_with(half_at(in_halves, 1 - y_bit), 2, devices)
    last = len(line_bits) - 1
    self_parts = first_step(self_line, model)
    for number in range(last):
        cross_held = merged(cross_held, brought(cross_held, line_bits, number), line_bits, number)
        down_held = merged(down_held, brought(down_held, ffn_steps, number), ffn_steps, number)
    self_parts, cross_held, in_theirs, down_held = barrier((self_parts, cross_held, in_theirs, down_held))
    in_held = pair_up(half_at(in_halves, y_bit), in_theirs, y_bit, 0).reshape(4 * rows_in, model)
    self_theirs = [brought(part, [2, 1, 2], n + 1) for n, part in enumerate(self_parts)]
    cross_line = merged(cross_held, brought(cross_held, line_bits, last), line_bits, last)
    cross_line = cross_line.reshape((-1,) + cross_block.shape)
    for number in range(last):
        in_held = merged(in_held, brought(in_held, ffn_steps, number), ffn_steps, number)
    down_theirs = brought(down_held, ffn_steps, last)
    cross_line, in_held, down_theirs, self_theirs = barrier((cross_line, in_held, down_theirs, self_theirs))
    cross_parts = first_step(cross_line, model)
    in_theirs = brought(in_held, ffn_steps, last)
    cross_parts, in_theirs = barrier((cross_parts, in_theirs))
    in_held = merged(in_held, in_theirs, ffn_steps, last)
    down_held = merged(down_held, down_theirs, ffn_steps, last)

    def second_merge(parts, theirs):
        return [
            pair_up(part, other, bit_of(me, order[1]), 1 if order[1] > order[0] else 2).reshape(-1, part.shape[-1])
            for part, other, order in zip(parts, theirs, pair_orders)
        ]

    self_mine = second_merge(self_parts, self_theirs)
    cross_theirs = [brought(part, [2, 1, 2], n + 1) for n, part in enumerate(cross_parts)]
    self_weights = [(mine, swap_with(mine[:, :model], 1, devices)) for mine in self_mine]

    gain_rows = self_weights[1][0][:, model : model + 8].T.astype(wide_type)
    self_flat = self_weights[0] + self_weights[1]

    dma = pltpu.SemaphoreType.DMA
    weights_kept = pltpu.VMEM((4, 2, model, half), low_type)
    projected, context_one, after_self = call(
        self_forward_kernel,
        "self_forward",
        2 * count * model * model * 5,
        [SMEM, VMEM, VMEM, VMEM] + [ANY] * 4,
        [VMEM] * 3,
        (
            shaped((3, count, model), low_type),
            shaped((count, model), low_type),
            shaped((count, model), wide_type),
        ),
        [weights_kept, dma((8,))],
        room=MIDDLE_BYTES,
    )(core_word, segment_ids, tokens, gain_rows, *self_flat)

    cross_direct = 2 * rows_in % 16 == 0
    cross_sibling = [swap_with(part, 1, devices) for part in cross_parts]
    cross_theirs, cross_sibling, in_held, down_held, after_self = barrier(
        (cross_theirs, cross_sibling, in_held, down_held, after_self)
    )
    in_theirs, down_theirs = swap_with(in_held, 4, devices), swap_with(down_held, 4, devices)
    in_sibling, down_sibling = swap_with(in_held, 1, devices), swap_with(down_held, 1, devices)
    sibling_theirs = [swap_with(theirs, 1, devices) for theirs in cross_theirs]
    if cross_direct:
        cross_weights = list(zip(cross_parts, cross_theirs, cross_sibling, sibling_theirs))
        cross_rows = cross_parts[0].shape[:1] + (2, 2, 2 * rows_in, half)
    else:
        cross_weights = list(
            zip(second_merge(cross_parts, cross_theirs), second_merge(cross_sibling, sibling_theirs))
        )
        cross_rows = (model, half)
    pieces = len(cross_weights[0])
    cross_flat = list(cross_weights[0]) + list(cross_weights[1])
    cross_kept = pltpu.VMEM((4, 2) + cross_rows, low_type)
    pair_kept = pltpu.VMEM((2, 2) + cross_rows, low_type)

    per_token = (heads, count, model)
    probs_shape = (heads, count, encoder_count // segs)
    probs_kept, tokens_kept = pltpu.VMEM(probs_shape, low_type), pltpu.VMEM(per_token, low_type)
    chunk_count = count // CHUNK
    chunk_table = pltpu.SMEM((4, chunk_count + segs), jnp.int32)
    queries_two, context_two, after_cross, normed_three, probs, mixed, spread = call(
        functools.partial(cross_forward_kernel, pieces),
        "cross_forward",
        12_000_000_000,
        [SMEM, SMEM, SMEM, VMEM, VMEM] + [HBM] * (1 + 2 * pieces),
        [VMEM] * 4 + [HBM] * 3,
        (
            shaped((count, model), low_type),
            shaped((count, model), low_type),
            shaped((count, model), wide_type),
            shaped((count, model), low_type),
            shaped(probs_shape, low_type),
            shaped(per_token, low_type),
            shaped(per_token, low_type),
        ),
        [
            probs_kept, tokens_kept, tokens_kept, pltpu.VMEM(encoded.shape, low_type), cross_kept,
            chunk_table, dma((segs,)), dma((4 * pieces,)), dma((3,)),
        ],
    )(me_word, starts, passage_group, after_self, gain_rows, encoded, *cross_flat)

    normed_theirs = swap_with(normed_three, 2, devices)
    in_theirs, down_theirs, in_sibling, down_sibling, normed_theirs = barrier(
        (in_theirs, down_theirs, in_sibling, down_sibling, normed_theirs)
    )
    in_fourth, down_fourth = swap_with(in_theirs, 1, devices), swap_with(down_theirs, 1, devices)
    ffn_pieces = [in_held, down_held, in_theirs, down_theirs, in_sibling, down_sibling, in_fourth, down_fourth]
    half_units = hidden_units // 2
    high = (2,) * (len(chip_bits) - 1)
    if direct:
        in_shape = (2, chip_groups, rows_down, model)
        down_shape = (chip_groups, 2, rows_down, model)
        ffn_weights = ffn_pieces
        grad_shapes = (shaped((chip_groups, 2 * rows_down, model), low_type),) * 2
    else:
        in_shape, down_shape = (2, 1, model, model), (1, 1, half_units, model)
        ffn_mine = [
            pair_up(held, theirs, bit_of(me, 2), len(line_bits)).reshape((chip_groups,) + held.shape[-2:])
            for held, theirs in ((in_held, in_theirs), (down_held, down_theirs))
        ]
        ffn_sibling = [
            pair_up(held, theirs, bit_of(me, 2), len(line_bits)).reshape((chip_groups,) + held.shape[-2:])
            for held, theirs in ((in_sibling, in_fourth), (down_sibling, down_fourth))
        ]
        ffn_weights = (
            pair_up(ffn_mine[0], ffn_sibling[0], core, 0).reshape(in_shape),
            pair_up(ffn_mine[1], ffn_sibling[1], core, 1).reshape(down_shape),
        )
        grad_shapes = (shaped(in_shape, low_type), shaped(down_shape, low_type))
    token_shapes = (shaped((count, model), wide_type), shaped((count, model), low_type))
    out_mine, out_other, pull_mine, pull_other, ffn_grad, ffn_other = call(
        functools.partial(ffn_kernel, direct),
        "ffn",
        4_000_000_000,
        [SMEM] + [VMEM] * 4 + [ANY] * len(ffn_weights),
        [VMEM] * 4 + [HBM] * 2,
        token_shapes + token_shapes + grad_shapes,
        [
            pltpu.VMEM((2,) + high + in_shape[2:] if direct else in_shape, low_type),
            pltpu.VMEM(high + down_shape[1:] if direct else down_shape, low_type),
            pltpu.VMEM(in_shape, low_type),
            pltpu.VMEM(down_shape, low_type),
            dma((8,)),
            dma((4,)),
        ],
        room=MIDDLE_BYTES,
    )(me_word, normed_three, normed_theirs, cotangent, cotangent_theirs, *ffn_weights)
    pull_theirs = swap_with(pull_other, 2, devices)
    if not direct:
        in_parts = ffn_grad.reshape(2, chip_groups, 4 * rows_in, model)
        down_parts = ffn_other.reshape(chip_groups, 2, rows_down, model).swapaxes(0, 1)
        both = jnp.concatenate([in_parts, down_parts], axis=2)
        ffn_grad, ffn_other = (
            lax.dynamic_index_in_dim(both, place, 0, keepdims=False) for place in (core, 1 - core)
        )
    ffn_theirs = swap_with(ffn_other, 1, devices)
    high_bits = [bit for bit in sorted(chip_bits, reverse=True) if bit > 1]

    def group_source(array):
        return (array.reshape((2,) * len(high_bits) + array.shape[-2:]), high_bits, 0)

    ffn_entry = ([group_source(ffn_grad), group_source(ffn_theirs)], (0, model))
    ffn_send = low(summed(ffn_entry, {2: 1 - bit_of(me, 2)}))
    pull_theirs, ffn_send = barrier((pull_theirs, ffn_send))
    ffn_sum = [with_brought(ffn_entry, swap_with(ffn_send, 4, devices), 2, [])]

    all_bits = sorted(chip_bits, reverse=True)

    def chips_of(array):
        return array.reshape((2,) * len(all_bits) + (array.shape[0] >> len(all_bits), array.shape[-1]))

    def entry_of(mine, theirs, begin, end):
        return ([(chips_of(mine), all_bits, 0), (chips_of(theirs), all_bits, 0)], (begin, end))

    def first_sum(sides):
        return [sum_over(entries, order[0], [], me, devices) for entries, order in zip(sides, pair_orders)]

    def second_sum(sides):
        return [sum_over(entries, order[1], order[:1], me, devices) for entries, order in zip(sides, pair_orders)]

    def received(sides):
        return [entries[0][0][-1][0] for entries in sides]

    def with_received(sides, arrays):
        return [
            [(sources[:-1] + [(array,) + sources[-1][1:]], columns) for sources, columns in entries]
            for entries, array in zip(sides, arrays)
        ]

    grads_shape = shaped((model, 2 * model), low_type)
    rows_kept = pltpu.VMEM(encoded.shape, low_type)
    two_kept = pltpu.VMEM((2, 2, model, half), low_type)
    grad_after_cross, ffn_gain_grad, grad_context, pulled, late_mine, late_other = call(
        functools.partial(cross_backward_first, pieces),
        "cross_backward_first",
        1_000_000_000,
        [SMEM] + [VMEM] * 6 + [HBM] * (1 + pieces),
        [VMEM] * 3 + [HBM] * 3,
        (
            shaped((count, model), wide_type),
            shaped((8, model), wide_type),
            shaped((count, model), low_type),
            shaped(per_token, low_type),
            grads_shape,
            grads_shape,
        ),
        [tokens_kept, tokens_kept, pair_kept, two_kept, dma((2 * pieces,)), dma((6,))],
    )(
        me_word, after_cross, gain_rows, cotangent, pull_mine, pull_theirs, context_two, mixed, *cross_weights[1]
    )
    grad_after_self, gain_grads, score_grads, cross_mine_grad, cross_other_grad = call(
        functools.partial(cross_backward_second, pieces),
        "cross_backward_second",
        3_000_000_000,
        [SMEM, SMEM, SMEM] + [VMEM] * 5 + [HBM] * (5 + pieces),
        [VMEM] * 2 + [HBM] * 3,
        (
            shaped((count, model), wide_type),
            shaped((8, model), wide_type),
            shaped(probs_shape, low_type),
            grads_shape,
            grads_shape,
        ),
        [
            probs_kept, tokens_kept, probs_kept, rows_kept, tokens_kept, pair_kept, two_kept,
            chunk_table, dma((segs,)), dma((2 * pieces,)), dma((5,)), dma((2, chunk_count)),
        ],
        aliases={11: 3, 12: 4},
    )(
        me_word, starts, passage_group, grad_after_cross, after_self, gain_rows, ffn_gain_grad,
        queries_two, encoded, probs, pulled, late_mine, late_other, *cross_weights[0],
    )
    arrays, grad_after_self, cross_mine_grad, cross_other_grad = barrier(
        (received([ffn_sum]), grad_after_self, cross_mine_grad, cross_other_grad)
    )
    ffn_sum = with_received([ffn_sum], arrays)[0]
    ffn_done = [2]
    for bit in sorted(line_bits)[:-1]:
        ffn_sum = sum_over(ffn_sum, bit, ffn_done, me, devices)
        ffn_done = ffn_done + [bit]
    cross_theirs_grad = swap_with(cross_other_grad, 1, devices)

    with_gains = shaped((model, 2 * model + PAIR), low_type)
    tokens_grad, self_mine, self_other = call(
        self_backward_kernel,
        "self_backward",
        2 * count * model * model * 10,
        [SMEM] + [VMEM] * 7 + [ANY] * 4,
        [VMEM] + [HBM] * 2,
        (shaped((count, model), wide_type), with_gains, with_gains),
        [weights_kept, weights_kept, pltpu.VMEM((model, PAIR), low_type), dma((8,)), dma((10,))],
        room=MIDDLE_BYTES,
    )(
        core_word, segment_ids, tokens, gain_rows, grad_after_self, gain_grads, projected, context_one,
        *self_flat,
    )
    arrays, cross_theirs_grad, self_mine, self_other = barrier(
        (received([ffn_sum]), cross_theirs_grad, self_mine, self_other)
    )
    ffn_sum = with_received([ffn_sum], arrays)[0]
    ffn_sum = sum_over(ffn_sum, max(line_bits), ffn_done, me, devices)
    self_theirs = swap_with(self_other, 1, devices)
    crossed = [
        [entry_of(cross_mine_grad, cross_theirs_grad, *cut)] for cut in ((0, model), (model, 2 * model))
    ]
    crossed = first_sum(crossed)
    self_theirs, score_grads = barrier((self_theirs, score_grads))
    attention = [
        [entry_of(self_mine, self_theirs, *cut)] for cut in ((0, model), (model, 2 * model + PAIR))
    ]
    attention = first_sum(attention)
    encoded_grad = call(
        rows_backward_kernel,
        "rows_backward",
        3_000_000_000,
        [SMEM, SMEM] + [HBM] * 4,
        HBM,
        shaped(encoded.shape, wide_type),
        [
            probs_kept, probs_kept, tokens_kept, tokens_kept,
            pltpu.VMEM((2, encoder_count // segs, model), wide_type), dma((2,)), dma((4, chunk_count)),
        ],
    )(starts, passage_group, score_grads, probs, spread, pulled)
    crossed_arrays, arrays, ffn_arrays, encoded_grad = barrier(
        (received(crossed), received(attention), received([ffn_sum]), encoded_grad)
    )
    ffn_sum = with_received([ffn_sum], ffn_arrays)[0]
    ffn_rows = summed(ffn_sum[0], {bit: bit_of(me, bit) for bit in high_bits})
    summed_down = ffn_rows[4 * rows_in :]
    in_parts = ffn_rows[: 4 * rows_in].reshape(2, 2, rows_in, model)
    in_parts = exchange(lambda mask: block_for(in_parts, mask), group_bits, me, devices)
    in_parts = in_parts.reshape(2, 2, rows_in, chip_groups // 2, 2 * rows_down)
    summed_in = in_parts.transpose(2, 1, 3, 0, 4).reshape(rows_in, hidden_units)
    crossed, attention = with_received(crossed, crossed_arrays), with_received(attention, arrays)
    groups = [(entries, order[1], order[:1]) for entries, order in zip(crossed, pair_orders)]
    sends = [sends_of(*group, me) for group in groups]
    sends, arrays = barrier((sends, received(attention)))
    crossed = [sum_over(*group, me, devices, send) for group, send in zip(groups, sends)]
    attention = second_sum(with_received(attention, arrays))
    cross_blocks = line_blocks(me_word, crossed[0] + crossed[1], line_bits, [2, 1], devices)
    unused_blocks, arrays = barrier((cross_blocks, received(attention)))
    attention = with_received(attention, arrays)
    cross_terms = brought_blocks(cross_blocks, line_bits, devices)
    self_blocks = line_blocks(me_word, attention[0] + attention[1], line_bits, [2, 1], devices)
    self_terms = brought_blocks(self_blocks, line_bits, devices)
    unused_blocks, out_other = barrier((cross_blocks, out_other))
    out_theirs = swap_with(out_other, 2, devices)
    self_terms, summed_in, out_theirs = barrier((self_terms, summed_in, out_theirs))
    block_out = low(after_cross + (out_mine + out_theirs.astype(wide_type)))

    def spread_out(terms, matrices, gains):
        found = terms[0]
        for term in terms[1:]:
            found = found + term.astype(wide_type)
        keep = lax.dynamic_slice_in_dim(found, core * rows_in, rows_in, axis=0)
        send = lax.dynamic_slice_in_dim(found, (1 - core) * rows_in, rows_in, axis=0)
        shapes = (shaped((rows_in, model), wide_type),) * matrices
        if gains:
            shapes += (shaped((rows_in, PAIR), wide_type),)
        return call(
            functools.partial(spread_kernel, matrices),
            "spread",
            1_000_000,
            [SMEM, VMEM, VMEM],
            [VMEM] * len(shapes),
            shapes,
            [],
            room=SMALL_BYTES,
        )(core_word, keep, swap_with(send, 1, devices))

    summed_cv, summed_cq, summed_co, summed_ck = spread_out(cross_terms, 4, False)
    summed_query, summed_key, summed_value, summed_out, own_gains = spread_out(self_terms, 4, True)
    return (
        block_out,
        tokens_grad,
        encoded_grad,
        own_gains[:, 0],
        own_gains[:, 1],
        own_gains[:, 2],
        summed_query,
        summed_key,
        summed_value,
        summed_out,
        summed_cq,
        summed_ck,
        summed_cv,
        summed_co,
        summed_in,
        summed_down,
    )


def solution(mesh):
    return jax.shard_map(
        functools.partial(per_device, mesh.shape["fsdp"], mesh.size),
        mesh=mesh,
        in_specs=(
            P(("dp", "fsdp"), None),
            P(("dp", "fsdp"), None),
            P(("dp", "fsdp"), None),
            P(("dp", "fsdp"), None),
            P(("dp", "fsdp"), None),
            P(("dp", "fsdp")),
            P(("dp", "fsdp")),
            P(("dp", "fsdp")),
            P(("dp", "fsdp"), None),
            P(("dp", "fsdp"), None),
            P(("dp", "fsdp"), None),
            P(("dp", "fsdp"), None),
            P(("dp", "fsdp"), None),
            P(("dp", "fsdp"), None),
            P(("dp", "fsdp"), None),
            P(("dp", "fsdp"), None),
            P(("dp", "fsdp"), None),
            P(("dp", "fsdp"), None),
        ),
        out_specs=(
            P(("dp", "fsdp"), None),
            P(("dp", "fsdp"), None),
            P(("dp", "fsdp"), None),
            P(("dp", "fsdp")),
            P(("dp", "fsdp")),
            P(("dp", "fsdp")),
            P(("dp", "fsdp"), None),
            P(("dp", "fsdp"), None),
            P(("dp", "fsdp"), None),
            P(("dp", "fsdp"), None),
            P(("dp", "fsdp"), None),
            P(("dp", "fsdp"), None),
            P(("dp", "fsdp"), None),
            P(("dp", "fsdp"), None),
            P(("dp", "fsdp"), None),
            P(("dp", "fsdp"), None),
        ),
        check_vma=False,
    )
```

```python
import functools

import jax
import jax.numpy as jnp
from jax import lax
from jax.experimental import pallas as pl
from jax.experimental.layout import Layout, with_layout_constraint
from jax.experimental.pallas import tpu as pltpu
from jax.sharding import PartitionSpec as P

HEAD = 64
CHUNK = 16
PAIR = 2 * HEAD
epsilon = 1e-06
masked_score = -1e30
VMEM_BYTES = 60 << 20
MIDDLE_BYTES = 32 << 20
SMALL_BYTES = 20 << 20


def contract(left, right, left_dim, right_dim):
    return lax.dot_general(
        left, right, (((left_dim,), (right_dim,)), ((), ())), preferred_element_type=jnp.float32
    )


def low(values):
    return values.astype(jnp.bfloat16)


def normalize(values, gain_row):
    return values * lax.rsqrt(jnp.mean(values * values, axis=-1, keepdims=True) + epsilon) * gain_row


def norm_backward(values, gain_row, grad):
    scale = lax.rsqrt(jnp.mean(values * values, axis=-1, keepdims=True) + epsilon)
    grad_gain = jnp.sum(grad * values * scale, axis=0, keepdims=True)
    weighted = gain_row * grad
    inner = jnp.mean(weighted * values, axis=-1, keepdims=True)
    return scale * weighted - values * (scale * scale * scale) * inner, grad_gain


def pair_rows(block):
    lane = lax.broadcasted_iota(jnp.int32, block.shape, 1)
    zero = jnp.zeros_like(block)
    return jnp.concatenate(
        [jnp.where(lane < HEAD, block, zero), jnp.where(lane >= HEAD, block, zero)], axis=0
    )


def pair_lanes(both):
    rows = both.shape[0] // 2
    lane = lax.broadcasted_iota(jnp.int32, (rows, both.shape[1]), 1)
    return jnp.where(lane < HEAD, both[:rows], both[rows:])


def weight_copies(core, sources, kept, sems):
    half = kept.shape[-1]
    copies = []
    for number in range(kept.shape[0]):
        for side, source in enumerate(sources[number // 2]):
            place = core if side == 0 else 1 - core
            copies.append(
                pltpu.make_async_copy(
                    source.at[:, (number % 2) * half : (number % 2 + 1) * half],
                    kept.at[number, place],
                    sems.at[2 * number + side],
                )
            )
    return copies


def piece_copies(me, pairs, kept, sems):
    core = me & 1
    half = kept.shape[-1]
    copies = []
    for number in range(kept.shape[0]):
        bit, pieces = pairs[number // 2]
        columns = slice((number % 2) * half, (number % 2 + 1) * half)
        for n, piece in enumerate(pieces):
            whole = len(pieces) == 2
            place = core if n < len(pieces) // 2 else 1 - core
            target = kept.at[number, place]
            if not whole:
                at = ((me >> bit) & 1) ^ (n & 1)
                target = kept.at[number, place, :, :, at] if bit == 1 else kept.at[number, place, :, at]
                piece = piece.at[:, :, :, columns]
            else:
                piece = piece.at[:, columns]
            copies.append(pltpu.make_async_copy(piece, target, sems.at[len(pieces) * number + n]))
    return copies


def whole_rows(kept, number, side):
    return kept[number, side].reshape(-1, kept.shape[-1])


def times(left, kept, number):
    return jnp.concatenate([contract(left, whole_rows(kept, number, side), 1, 0) for side in range(2)], axis=1)


def times_back(left, kept, number):
    half = kept.shape[-1]
    return contract(left[:, :half], whole_rows(kept, number, 0), 1, 1) + contract(
        left[:, half:], whole_rows(kept, number, 1), 1, 1
    )


def grad_into(left, right, held, number):
    half = held.shape[-1]
    for side in range(2):
        held[number, side] = low(contract(left, right[:, side * half : (side + 1) * half], 0, 0))


def grad_copies(core, targets, held, number, sems, place_of=None):
    half = held.shape[-1]
    at = number if place_of is None else place_of[number]
    copies = []
    for side, target in enumerate(targets):
        place = core if side == 0 else 1 - core
        copies.append(
            pltpu.make_async_copy(
                held.at[number, place],
                target.at[:, at * half : (at + 1) * half],
                sems.at[2 * number + side],
            )
        )
    return copies


def spread_kernel(matrices, core_ref, keep, theirs, *targets):
    core = core_ref[0]
    half = targets[0].shape[1] // 2
    for number, target in enumerate(targets[:matrices]):
        columns = slice(number * half, (number + 1) * half)
        for side in range(2):
            target[:, side * half : (side + 1) * half] = jnp.where(core == side, keep[:, columns], theirs[:, columns])
    for target in targets[matrices:]:
        target[...] = keep[:, matrices * half :]


def pack_kernel(core_ref, *refs):
    shards, gains, wide_shard, (send, keep) = refs[:-4], refs[-4], refs[-3], refs[-2:]
    core = core_ref[0]
    half = shards[0].shape[1] // 2
    wide = wide_shard.shape[1] // 2
    at = len(shards) * half
    for target, place in ((send, 1 - core), (keep, core)):
        for number, shard in enumerate(shards):
            target[:, number * half : (number + 1) * half] = shard[:, pl.ds(pl.multiple_of(place * half, PAIR), half)]
        target[:, at : at + PAIR] = gains[...]
        target[:, at + PAIR :] = wide_shard[:, pl.ds(pl.multiple_of(place * wide, PAIR), wide)]


def self_mask(ids_row):
    tokens = ids_row.shape[1]
    wide = jnp.broadcast_to(ids_row.astype(jnp.float32), (tokens, tokens))
    query = lax.broadcasted_iota(jnp.int32, (tokens, tokens), 0)
    key = lax.broadcasted_iota(jnp.int32, (tokens, tokens), 1)
    allowed = jnp.where((wide == wide.T) & (key <= query), 1.0, 0.0)
    return jnp.concatenate([allowed, allowed], axis=0) > 0.5


def self_probs(queries, keys, allowed):
    scores = jnp.where(allowed, contract(pair_rows(queries), keys, 1, 1) * 0.125, masked_score)
    weights = jnp.exp(scores - jnp.max(scores, axis=-1, keepdims=True))
    return weights / jnp.sum(weights, axis=-1, keepdims=True)


def self_forward_kernel(
    core_ref, ids, tokens, gains, first_mine, first_sibling, second_mine, second_sibling,
    projected, context, after, kept, sems,
):
    core = core_ref[0]
    copies = weight_copies(
        core, ((first_mine, first_sibling), (second_mine, second_sibling)), kept, sems
    )
    for copy in copies:
        copy.start()
    model = tokens.shape[1]
    hidden = tokens[...].astype(jnp.float32)
    normed = low(normalize(hidden, gains[0:1, :]))
    for number in range(3):
        copies[2 * number].wait()
        copies[2 * number + 1].wait()
        projected[number] = low(times(normed, kept, number))
    allowed = self_mask(ids[...])
    for j in range(model // PAIR):
        columns = slice(j * PAIR, (j + 1) * PAIR)
        probs = self_probs(projected[0, :, columns], projected[1, :, columns], allowed)
        context[:, columns] = low(pair_lanes(contract(low(probs), projected[2, :, columns], 1, 0)))
    copies[6].wait()
    copies[7].wait()
    after[...] = hidden + times(context[...], kept, 3)


def self_backward_kernel(
    core_ref, ids, tokens, gains, grad_after, gain_grads, projected, context,
    first_mine, first_sibling, second_mine, second_sibling,
    tokens_grad, grad_mine, grad_other,
    kept, held, gain_held, sems, out_sems,
):
    core = core_ref[0]
    copies = weight_copies(
        core, ((first_mine, first_sibling), (second_mine, second_sibling)), kept, sems
    )
    for copy in copies:
        copy.start()
    model = tokens.shape[1]
    count = tokens.shape[0]
    hidden = tokens[...].astype(jnp.float32)
    normed = low(normalize(hidden, gains[0:1, :]))
    branch = low(grad_after[...])
    started = []

    def send(number):
        for copy in grad_copies(core, (grad_mine, grad_other), held, number, out_sems):
            copy.start()
            started.append(copy)

    grad_into(context[...], branch, held, 3)
    send(3)
    for copy in copies:
        copy.wait()
    grad_context = low(times_back(branch, kept, 3))
    allowed = self_mask(ids[...])
    found = ([], [], [])
    for j in range(model // PAIR):
        columns = slice(j * PAIR, (j + 1) * PAIR)
        queries, keys = projected[0, :, columns], projected[1, :, columns]
        probs = self_probs(queries, keys, allowed)
        pulled = pair_rows(grad_context[:, columns])
        prob_grad = contract(pulled, projected[2, :, columns], 1, 1)
        inner = jnp.sum(probs * prob_grad, axis=-1, keepdims=True)
        score_grad = low(probs * (prob_grad - inner))
        found[0].append(low(pair_lanes(contract(score_grad, keys, 1, 0)) * 0.125))
        found[1].append(low(contract(score_grad, pair_rows(queries), 0, 0) * 0.125))
        found[2].append(low(contract(low(probs), pulled, 0, 0)))
    grad_normed = None
    for number in range(3):
        whole = jnp.concatenate(found[number], axis=1)
        grad_into(normed, whole, held, number)
        send(number)
        part = times_back(whole, kept, number)
        grad_normed = part if grad_normed is None else grad_normed + part
    grad_hidden, grad_gain = norm_backward(hidden, gains[0:1, :], grad_normed)
    tokens_grad[...] = grad_after[...] + grad_hidden
    row = lax.broadcasted_iota(jnp.int32, (count, model), 0)
    others = gain_grads[...]
    wide = jnp.where(
        row == 0, grad_gain, jnp.where(row == 1, others[0:1], jnp.where(row == 2, others[1:2], 0.0))
    )
    gain_held[...] = low(wide.T)
    for slot, target in enumerate((grad_mine, grad_other)):
        copy = pltpu.make_async_copy(gain_held, target.at[:, 2 * model :], out_sems.at[8 + slot])
        copy.start()
        started.append(copy)
    for copy in started:
        copy.wait()


def row_copies(encoded, rows_ref, sems, segs):
    size = encoded.shape[0] // segs
    return [
        pltpu.make_async_copy(
            encoded.at[pl.ds(s * size, size)], rows_ref.at[pl.ds(s * size, size)], sems.at[s]
        )
        for s in range(segs)
    ]


def block_copy(encoded, rows_ref, sems, groups, s):
    size = encoded.shape[0] // groups.shape[1]
    at = pl.ds(pl.multiple_of(groups[0, s] * size, size), size)
    return pltpu.make_async_copy(encoded.at[at], rows_ref.at[at], sems.at[s])


def chunk_copies(pairs, sems, c):
    at = (slice(None), pl.ds(pl.multiple_of(c * CHUNK, CHUNK), CHUNK), slice(None))
    return [pltpu.make_async_copy(source.at[at], target.at[at], sems.at[n, c]) for n, (source, target) in enumerate(pairs)]


def list_chunks(starts, table):
    def query(s, count):
        begin, end = starts[0, s], starts[0, s + 1]

        def chunk(c, count):
            table[0, count] = c * CHUNK
            table[1, count] = s
            table[2, count] = (c == begin >> 4).astype(jnp.int32)
            table[3, count] = ((c * CHUNK >= begin) | (begin & (CHUNK - 1) == 0)).astype(jnp.int32)
            return count + 1

        return lax.fori_loop(begin >> 4, (end + CHUNK - 1) >> 4, chunk, count)

    return lax.fori_loop(0, starts.shape[1] - 1, query, 0)


def listed(starts, table, at):
    s = table[1, at]
    return pl.multiple_of(table[0, at], CHUNK), s, starts[0, s], starts[0, s + 1]


def in_segment(token, begin, end, heads):
    row = lax.broadcasted_iota(jnp.int32, (heads, CHUNK, 1), 1) + token
    return (row >= begin) & (row < end)


def pair_weight(kept, number, j):
    per_half = kept.shape[-1] // PAIR
    columns = slice((j % per_half) * PAIR, (j % per_half + 1) * PAIR)
    at = (number, j // per_half) + (slice(None),) * (len(kept.shape) - 3) + (columns,)
    return kept[at].reshape(-1, PAIR)


def cross_forward_kernel(
    pieces, me_ref, starts, groups, after_self, gains, encoded, *refs,
):
    first, second = refs[:pieces], refs[pieces : 2 * pieces]
    queries, context, after_cross, normed_out, probs_hbm, mixed_hbm, spread_hbm = refs[2 * pieces : 2 * pieces + 7]
    probs_out, mixed_out, spread_out, rows_ref, kept, table, sems, weight_sems, out_sems = refs[2 * pieces + 7 :]
    heads, tokens, model = spread_out.shape
    segs = groups.shape[1]
    block_rows = encoded.shape[0] // segs
    copies = piece_copies(me_ref[0], ((1, first), (2, second)), kept, weight_sems)
    early, late = copies[: 2 * pieces], copies[2 * pieces :]
    for copy in early:
        copy.start()
    for s in range(segs):
        block_copy(encoded, rows_ref, sems, groups, s).start()
    leaving = [
        pltpu.make_async_copy(source, target, out_sems.at[n])
        for n, (source, target) in enumerate(
            ((spread_out, spread_hbm), (probs_out, probs_hbm), (mixed_out, mixed_hbm))
        )
    ]
    for copy in late:
        copy.start()
    normed = low(normalize(after_self[...], gains[1:2, :]))
    for copy in early:
        copy.wait()
    queries[...] = low(times(normed, kept, 0))
    for j in range(heads // 2):
        block = queries[:, j * PAIR : (j + 1) * PAIR] * jnp.bfloat16(0.125)
        spread = low(contract(pair_rows(block), pair_weight(kept, 1, j), 1, 1))
        spread_out[2 * j] = spread[:tokens]
        spread_out[2 * j + 1] = spread[tokens:]
    leaving[0].start()

    count = list_chunks(starts, table)

    def two_chunks(i, carry):
        places = [2 * i, jnp.minimum(2 * i + 1, count - 1)]
        for n, place in enumerate(places):

            @pl.when((2 * i + n < count) & (table[2, place] == 1))
            def _():
                block_copy(encoded, rows_ref, sems, groups, table[1, place]).wait()

        found, scores, blocks = [], [], []
        for place in places:
            token, s, begin, end = listed(starts, table, place)
            base = pl.multiple_of(groups[0, s] * block_rows, block_rows)
            found.append((token, begin, end))
            blocks.append(rows_ref[pl.ds(base, block_rows), :])
            left = spread_out[:, pl.ds(token, CHUNK), :].reshape(heads * CHUNK, model)
            scores.append(contract(left, blocks[-1], 1, 1))
        for (token, begin, end), score, rows in zip(found, scores, blocks):
            weights = jnp.exp(score - jnp.max(score, axis=-1, keepdims=True))
            totals = jnp.sum(weights, axis=-1, keepdims=True)
            probs = low(weights * (1.0 / totals))
            mixed = low(contract(probs, rows, 1, 0))
            inside = in_segment(token, begin, end, heads)
            at = (slice(None), pl.ds(token, CHUNK), slice(None))
            probs = probs.reshape(heads, CHUNK, block_rows)
            mixed = mixed.reshape(heads, CHUNK, model)
            probs_out[at] = jnp.where(inside, probs, probs_out[at])
            mixed_out[at] = jnp.where(inside, mixed, mixed_out[at])
        return carry

    lax.fori_loop(0, (count + 1) >> 1, two_chunks, 0)
    for copy in leaving[1:]:
        copy.start()
    for copy in late:
        copy.wait()
    for j in range(heads // 2):
        both = jnp.concatenate([mixed_out[2 * j], mixed_out[2 * j + 1]], axis=0)
        found = contract(both, pair_weight(kept, 2, j), 1, 0)
        context[:, j * PAIR : (j + 1) * PAIR] = low(pair_lanes(found))
    after_cross[...] = after_self[...] + times(context[...], kept, 3)
    normed_out[...] = low(normalize(after_cross[...], gains[2:3, :]))
    for copy in leaving:
        copy.wait()


def cross_backward_kernel(
    pieces, me_ref, starts, groups, after_cross, after_self, gains, cotangent, pull_mine, pull_theirs, queries, context,
    mixed_hbm, encoded, probs_hbm, *refs,
):
    first, second, refs = refs[:pieces], refs[pieces : 2 * pieces], refs[2 * pieces :]
    grad_self, gain_grads, score_hbm, pulled_hbm, grad_mine, grad_other = refs[:6]
    grad_after, grad_context, mixed, probs_ref, pulled_ref, score_out, rows_ref, moved_ref, kept, held, table = refs[6:17]
    sems, weight_sems, out_sems, chunk_sems = refs[17:]
    core = me_ref[0] & 1
    heads, tokens, model = pulled_ref.shape
    segs = groups.shape[1]
    block_rows = encoded.shape[0] // segs
    half = held.shape[-1]
    copies = piece_copies(me_ref[0], ((1, first), (2, second)), kept, weight_sems)
    query_part, key_part, value_part, out_part = (copies[n * pieces : (n + 1) * pieces] for n in range(4))
    coming = pltpu.make_async_copy(mixed_hbm, mixed, out_sems.at[8])
    for copy in out_part + value_part + [coming]:
        copy.start()
    chunk_pairs = ((probs_hbm, probs_ref),)
    started = []

    def send(number):
        for copy in grad_copies(core, (grad_mine, grad_other), held, number, out_sems, (1, 3, 0, 2)):
            copy.start()
            started.append(copy)

    grad_normed = pull_mine[...] + pull_theirs[...].astype(jnp.float32)
    grad_values, found_gain = norm_backward(after_cross[...], gains[2:3, :], grad_normed)
    grad_after[...] = cotangent[...].astype(jnp.float32) + grad_values
    gain_grads[1:2, :] = found_gain
    branch = low(grad_after[...])
    grad_into(context[...], branch, held, 3)
    send(3)
    for copy in out_part + value_part:
        copy.wait()
    block_copy(encoded, rows_ref, sems, groups, 0).start()
    for c in range(tokens // CHUNK):
        for copy in chunk_copies(chunk_pairs, chunk_sems, c):
            copy.start()
        if c % 2 and c // 2 + 1 < segs:
            block_copy(encoded, rows_ref, sems, groups, c // 2 + 1).start()
    for copy in key_part + query_part:
        copy.start()
    grad_context[...] = low(times_back(branch, kept, 3))
    coming.wait()
    per_half = half // PAIR
    for j in range(heads // 2):
        columns = slice((j % per_half) * PAIR, (j % per_half + 1) * PAIR)
        rows = pair_rows(grad_context[:, j * PAIR : (j + 1) * PAIR])
        both = jnp.concatenate([mixed[2 * j], mixed[2 * j + 1]], axis=0)
        held[2, j // per_half, :, columns] = low(contract(both, rows, 0, 0))
        pulled = low(contract(rows, pair_weight(kept, 2, j), 1, 1))
        pulled_ref[2 * j] = pulled[:tokens]
        pulled_ref[2 * j + 1] = pulled[tokens:]
    send(2)
    leaving = pltpu.make_async_copy(pulled_ref, pulled_hbm, out_sems.at[9])
    leaving.start()
    started.append(leaving)
    count = list_chunks(starts, table)

    def two_chunks(i, carry):
        places = [2 * i, jnp.minimum(2 * i + 1, count - 1)]
        for n, place in enumerate(places):

            @pl.when((2 * i + n < count) & (table[2, place] == 1))
            def _():
                block_copy(encoded, rows_ref, sems, groups, table[1, place]).wait()

            @pl.when((2 * i + n < count) & (table[3, place] == 1))
            def _():
                for copy in chunk_copies(chunk_pairs, chunk_sems, table[0, place] >> 4):
                    copy.wait()

        found, prob_grads, blocks = [], [], []
        for place in places:
            token, s, begin, end = listed(starts, table, place)
            base = pl.multiple_of(groups[0, s] * block_rows, block_rows)
            blocks.append(rows_ref[pl.ds(base, block_rows), :])
            at = (slice(None), pl.ds(token, CHUNK), slice(None))
            inside = in_segment(token, begin, end, heads)
            found.append((at, inside))
            pulled = jnp.where(inside, pulled_ref[at], jnp.zeros((), jnp.bfloat16))
            prob_grads.append(contract(pulled.reshape(heads * CHUNK, model), blocks[-1], 1, 1))
        for (at, inside), prob_grad, rows in zip(found, prob_grads, blocks):
            wide = probs_ref[at].reshape(heads * CHUNK, block_rows).astype(jnp.float32)
            inner = jnp.sum(wide * prob_grad, axis=-1, keepdims=True)
            score_grad = low(wide * (prob_grad - inner))
            moved = low(contract(score_grad, rows, 1, 0)).reshape(heads, CHUNK, model)
            moved_ref[at] = jnp.where(inside, moved, moved_ref[at])
            score_grad = score_grad.reshape(heads, CHUNK, block_rows)
            score_out[at] = jnp.where(inside, score_grad, score_out[at])
        return carry

    lax.fori_loop(0, (count + 1) >> 1, two_chunks, 0)
    leaving = pltpu.make_async_copy(score_out, score_hbm, out_sems.at[10])
    leaving.start()
    started.append(leaving)
    for copy in key_part + query_part:
        copy.wait()
    found = []
    for j in range(heads // 2):
        columns = slice((j % per_half) * PAIR, (j % per_half + 1) * PAIR)
        both = jnp.concatenate([moved_ref[2 * j], moved_ref[2 * j + 1]], axis=0)
        found.append(low(pair_lanes(contract(both, pair_weight(kept, 1, j), 1, 0)) * 0.125))
        block = queries[:, j * PAIR : (j + 1) * PAIR] * jnp.bfloat16(0.125)
        held[1, j // per_half, :, columns] = low(contract(both, pair_rows(block), 0, 0))
    send(1)
    grad_queries = jnp.concatenate(found, axis=1)
    values = after_self[...]
    grad_into(low(normalize(values, gains[1:2, :])), grad_queries, held, 0)
    send(0)
    grad_values, grad_gain = norm_backward(values, gains[1:2, :], times_back(grad_queries, kept, 0))
    grad_self[...] = grad_after[...] + grad_values
    gain_grads[0:1, :] = grad_gain
    for copy in started:
        copy.wait()


def rows_backward_kernel(
    starts, groups, score_hbm, probs_hbm, spread_hbm, pulled_hbm, grad_rows,
    score_grads, probs_ref, spread, pulled_ref, sum_ref, row_sems, chunk_sems,
):
    heads, tokens, model = spread.shape
    segs = groups.shape[1]
    block_rows = grad_rows.shape[0] // segs

    chunk_pairs = (
        (score_hbm, score_grads), (probs_hbm, probs_ref), (spread_hbm, spread), (pulled_hbm, pulled_ref),
    )
    for c in range(tokens // CHUNK):
        for copy in chunk_copies(chunk_pairs, chunk_sems, c):
            copy.start()

    def write_out(s):
        slot = s & 1
        base = pl.multiple_of(groups[0, s] * block_rows, block_rows)
        return pltpu.make_async_copy(
            sum_ref.at[slot], grad_rows.at[pl.ds(base, block_rows)], row_sems.at[slot]
        )

    def segment(s, begin):
        end = starts[0, s + 1]
        slot = s & 1

        @pl.when(s >= 2)
        def _():
            write_out(s - 2).wait()

        def terms(c):
            @pl.when((c * CHUNK >= begin) | (begin & (CHUNK - 1) == 0))
            def _():
                for copy in chunk_copies(chunk_pairs, chunk_sems, c):
                    copy.wait()

            token = pl.multiple_of(c * CHUNK, CHUNK)
            at = (slice(None), pl.ds(token, CHUNK), slice(None))
            inside = in_segment(token, begin, end, heads)
            zero = jnp.zeros((), jnp.bfloat16)
            scores = jnp.where(inside, score_grads[at], zero).reshape(heads * CHUNK, block_rows)
            left = jnp.concatenate([scores, probs_ref[at].reshape(heads * CHUNK, block_rows)], axis=0)
            right = jnp.concatenate(
                [jnp.where(inside, piece[at], zero).reshape(heads * CHUNK, model) for piece in (spread, pulled_ref)],
                axis=0,
            )
            return contract(left, right, 0, 0)

        def chunk(c, carry):
            sum_ref[slot] += terms(c)
            return carry

        first = begin >> 4
        sum_ref[slot] = terms(first)
        lax.fori_loop(first + 1, (end + CHUNK - 1) >> 4, chunk, 0)
        write_out(s).start()
        return end

    lax.fori_loop(0, segs, segment, 0)
    for s in range(segs - 2, segs):
        write_out(s).wait()


def gelu_both(values):
    scale = 0.7978845608028654
    square = values * values
    bend = jnp.tanh(scale * (values + 0.044715 * (square * values)))
    half = 0.5 * (1.0 + bend)
    slope = half + 0.5 * values * (1.0 - bend * bend) * (scale * (1.0 + 3.0 * 0.044715 * square))
    return values * half, slope


def ffn_kernel(
    direct,
    me_ref, normed, normed_theirs, cotangent, cotangent_theirs, *refs,
):
    sources, refs = (refs[:8], refs[8:]) if direct else (refs[:2], refs[2:])
    out_mine, out_other, pull_mine, pull_other, grad_mine, grad_other = refs[:6]
    kept_in, kept_down, held_in, held_down, sems, out_sems = refs[6:]
    core = me_ref[0] & 1
    x_bit = (me_ref[0] >> 2) & 1
    blocks, groups, unused, width = held_in.shape
    model = held_in.shape[1] * held_in.shape[2]
    count = normed.shape[0]
    if direct:
        copies = []
        for n, source in enumerate(sources):
            place = core if n < 4 else 1 - core
            at = x_bit ^ (n >> 1 & 1)
            lead = (slice(None),) * (len(source.shape) - 2)
            target = kept_in.at[(place,) + lead + (at,)] if n % 2 == 0 else kept_down.at[lead + (at, place)]
            copies.append(pltpu.make_async_copy(source, target, sems.at[n]))
    else:
        copies = [
            pltpu.make_async_copy(source, target, sems.at[n])
            for n, (source, target) in enumerate(zip(sources, (kept_in, kept_down)))
        ]
    for copy in copies:
        copy.start()
    tokens = jnp.concatenate([normed[...], normed_theirs[...]], axis=0)
    pull = jnp.concatenate([cotangent[...], cotangent_theirs[...]], axis=0)
    for copy in copies:
        copy.wait()
    total = grad_tokens = None
    started = []
    for b in range(blocks):
        weight_up = kept_in[b].reshape(model, width)
        part = slice(b * groups // blocks, (b + 1) * groups // blocks) if direct else slice(0, 1)
        if direct:
            weight_down = kept_down[b].reshape(width, model)
        else:
            weight_down = kept_down[0, 0, b * width : (b + 1) * width]
        activated, slope = gelu_both(contract(tokens, weight_up, 1, 0))
        activated = low(activated)
        grad_act = low(contract(pull, weight_down, 1, 1)).astype(jnp.float32)
        grad_pre = low(slope * grad_act)
        added = contract(grad_pre, weight_up, 1, 1)
        grad_tokens = added if b == 0 else grad_tokens + added
        added = contract(activated, weight_down, 1, 0)
        total = added if b == 0 else total + added
        held_in[b] = low(contract(tokens, grad_pre, 0, 0)).reshape(held_in.shape[1:])
        grad_down = low(contract(activated, pull, 0, 0))
        if direct:
            held_down[part] = grad_down.reshape((groups // blocks,) + held_down.shape[1:])
        else:
            held_down[0, 0, b * width : (b + 1) * width] = grad_down
    if direct:
        rows = held_down.shape[2]
        targets = (
            (held_in.at[1 - core], grad_other.at[:, :rows]),
            (held_down.at[:, 1 - core], grad_other.at[:, rows:]),
            (held_in.at[core], grad_mine.at[:, :rows]),
            (held_down.at[:, core], grad_mine.at[:, rows:]),
        )
    else:
        targets = ((held_in, grad_mine), (held_down, grad_other))
    started = [pltpu.make_async_copy(source, target, out_sems.at[n]) for n, (source, target) in enumerate(targets)]
    for copy in started:
        copy.start()
    out_mine[...] = total[:count]
    out_other[...] = low(total[count:])
    pull_mine[...] = grad_tokens[:count]
    pull_other[...] = low(grad_tokens[count:])
    for copy in started:
        copy.wait()

VMEM = pl.BlockSpec(memory_space=pltpu.VMEM)
SMEM = pl.BlockSpec(memory_space=pltpu.SMEM)
HBM = pl.BlockSpec(memory_space=pltpu.HBM)
ANY = pl.BlockSpec(memory_space=pl.ANY)


def shaped(shape, dtype):
    return jax.ShapeDtypeStruct(shape, dtype)


def call(kernel, name, flops, in_specs, out_specs, out_shape, scratch, aliases={}, room=VMEM_BYTES):
    return pl.pallas_call(
        kernel,
        out_shape=out_shape,
        in_specs=in_specs,
        out_specs=out_specs,
        scratch_shapes=scratch,
        compiler_params=pltpu.CompilerParams(vmem_limit_bytes=room),
        cost_estimate=pl.CostEstimate(flops=flops, bytes_accessed=1_000_000, transcendentals=0),
        name=name,
        input_output_aliases=aliases,
    )


AXES = ("dp", "fsdp")


def swap_with(piece, mask, devices):
    pairs = [(index, index ^ mask) for index in range(devices)]
    return lax.ppermute(piece, AXES, pairs)


def bit_of(me, bit):
    return (me >> bit) & 1


def pair_up(mine, theirs, my_bit, axis):
    first = jnp.where(my_bit == 0, mine, theirs)
    second = jnp.where(my_bit == 0, theirs, mine)
    return jnp.stack([first, second], axis=axis)


def arranged(found, bits, me):
    found = {mask: [block] for mask, block in found.items()}
    for n, bit in enumerate(sorted(bits)):
        low_side = bit_of(me, bit) == 0
        merged = {}
        for mask in found:
            if not mask >> n & 1:
                both = list(zip(found[mask], found[mask | 1 << n]))
                merged[mask] = [jnp.where(low_side, x, y) for x, y in both] + [
                    jnp.where(low_side, y, x) for x, y in both
                ]
        found = merged
    return jnp.stack(found[0])


def wide_mask(mask, bits):
    return sum(1 << bit for n, bit in enumerate(sorted(bits)) if mask >> n & 1)


def exchange(send, bits, me, devices):
    found = {0: send(0)}
    for mask in range(1, 1 << len(bits)):
        found[mask] = swap_with(send(mask), wide_mask(mask, bits), devices)
    return arranged(found, bits, me)


def gather_line(block, bits, me, devices):
    if len(bits) > 2:
        held = block[None]
        for bit in sorted(bits):
            theirs = swap_with(held, 1 << bit, devices)
            held = pair_up(held, theirs, bit_of(me, bit), 0).reshape((-1,) + block.shape)
        return held
    return exchange(lambda mask: block, bits, me, devices)


def taken(source, places, columns):
    array, bits, offset = source
    begin = [places[bit] if bit in places else 0 for bit in bits] + [0, offset + columns[0]]
    size = [1 if bit in places else 2 for bit in bits] + [array.shape[-2], columns[1] - columns[0]]
    part = lax.dynamic_slice(array, begin, size)
    return part.reshape([2 for bit in bits if bit not in places] + size[-2:])


def summed(entry, places):
    sources, columns = entry
    total = None
    for source in sources:
        part = taken(source, places, columns).astype(jnp.float32)
        total = part if total is None else total + part
    return total


def with_brought(entry, theirs, bit, done):
    sources, columns = entry
    bits = [other for other in sources[0][1] if other not in done and other != bit]
    return (sources + [(theirs, bits, -columns[0])], columns)


def sends_of(entries, bit, done, me):
    places = {other: bit_of(me, other) for other in done}
    send = [low(summed(entry, {**places, bit: 1 - bit_of(me, bit)})) for entry in entries]
    send = jnp.concatenate(send, axis=-1)
    return with_layout_constraint(send, Layout(tuple(range(send.ndim))))


def sum_over(entries, bit, done, me, devices, send=None):
    theirs = swap_with(sends_of(entries, bit, done, me) if send is None else send, 1 << bit, devices)
    found, at = [], 0
    for sources, columns in entries:
        bits = [other for other in sources[0][1] if other not in done and other != bit]
        found.append((sources + [(theirs, bits, at - columns[0])], columns))
        at += columns[1] - columns[0]
    return found


def combine(me_word, outputs):
    arrays, buffers, plan, shapes = [], {}, [], []
    for pieces, dtype in outputs:
        at, steps = 0, []
        for (sources, columns), flips, late in pieces:
            keys = []
            for array, bits, offset in sources:
                number = next((n for n, other in enumerate(arrays) if other is array), len(arrays))
                if number == len(arrays):
                    arrays.append(array)
                picked = tuple(flips.get(bit) for bit in bits)
                key = (number, tuple(bits), picked, offset + columns[0], columns[1] - columns[0])
                buffers.setdefault(key, len(buffers))
                keys.append(key)
            steps.append((at, keys, late))
            at += columns[1] - columns[0]
        sources = pieces[0][0][0]
        left = [bit for bit in sources[0][1] if bit not in pieces[0][1] and bit not in pieces[0][2]]
        plan.append(steps)
        shapes.append(shaped((2,) * len(left) + (sources[0][0].shape[-2], at), dtype))

    def kernel(me_ref, *refs):
        inputs, targets = refs[: len(arrays)], refs[len(arrays) : len(arrays) + len(outputs)]
        held, sems = refs[len(arrays) + len(outputs) : -1], refs[-1]
        me = me_ref[0]
        copies = {}
        for key, n in buffers.items():
            number, bits, picked, begin, width = key
            index = tuple(
                slice(None) if flip is None else ((me >> bit) & 1) ^ flip for bit, flip in zip(bits, picked)
            )
            copies[key] = pltpu.make_async_copy(
                inputs[number].at[index + (slice(None), slice(begin, begin + width))], held[n], sems.at[n]
            )
            copies[key].start()
        waited = set()
        for target, steps in zip(targets, plan):
            for at, keys, late in steps:
                total = None
                for key in keys:
                    if key not in waited:
                        copies[key].wait()
                        waited.add(key)
                    left = [bit for bit, flip in zip(key[1], key[2]) if flip is None]
                    index = tuple(((me >> bit) & 1) ^ late[bit] if bit in late else slice(None) for bit in left)
                    part = held[buffers[key]][index].astype(jnp.float32)
                    total = part if total is None else total + part
                target[..., at : at + keys[0][4]] = total.astype(target.dtype)

    scratch = []
    for number, bits, picked, begin, width in buffers:
        lead = tuple(2 for flip in picked if flip is None)
        scratch.append(pltpu.VMEM(lead + (arrays[number].shape[-2], width), arrays[number].dtype))
    scratch.append(pltpu.SemaphoreType.DMA((len(buffers),)))
    found = call(
        kernel, "combine", 1_000_000, [SMEM] + [ANY] * len(arrays), [VMEM] * len(outputs), tuple(shapes), scratch
    )(me_word, *arrays)
    return list(found)


def line_blocks(me_word, entries, bits, done, devices):
    flips = {bit: 0 for bit in done}
    if len(bits) > 2:
        for bit in sorted(bits):
            entries = sum_over(entries, bit, list(flips), me_word[0], devices)
            flips[bit] = 0
        return combine(me_word, [([(entry, flips, {}) for entry in entries], jnp.float32)])
    outputs = []
    for mask in range(1 << len(bits)):
        wide = wide_mask(mask, bits)
        pieces = [(entry, flips, {bit: wide >> bit & 1 for bit in bits}) for entry in entries]
        outputs.append((pieces, jnp.bfloat16 if mask else jnp.float32))
    return combine(me_word, outputs)


def brought_blocks(blocks, bits, devices):
    return blocks[:1] + [
        swap_with(block, wide_mask(mask + 1, bits), devices) for mask, block in enumerate(blocks[1:])
    ]


def core_rows(total, core, devices):
    rows = total.shape[0] // 2
    keep = lax.dynamic_slice_in_dim(total, core * rows, rows, axis=0)
    send = lax.dynamic_slice_in_dim(total, (1 - core) * rows, rows, axis=0)
    theirs = swap_with(send, 1, devices)
    return jnp.where(core == 0, keep, theirs), jnp.where(core == 0, theirs, keep)


def per_device(
    fsdp,
    devices,
    tokens,
    encoded,
    segment_ids,
    passage_group,
    cotangent,
    self_gain,
    cross_gain,
    ffn_gain,
    self_query,
    self_key,
    self_value,
    self_out,
    cross_query,
    cross_key,
    cross_value,
    cross_out,
    ffn_in,
    ffn_out,
):
    me = lax.axis_index("dp") * fsdp + lax.axis_index("fsdp")
    core = bit_of(me, 0)
    core_word = core.reshape(1).astype(jnp.int32)
    me_word = me.reshape(1).astype(jnp.int32)
    bounds = lax.broadcasted_iota(jnp.int32, (1, passage_group.shape[1] + 1), 1)
    starts = jnp.sum((segment_ids[0, :, None] < bounds).astype(jnp.int32), axis=0, keepdims=True)
    chip_bits = list(range(1, devices.bit_length() - 1))
    line_bits = [bit for bit in reversed(chip_bits) if bit > 2]
    pair_orders = ([2, 1], [1, 2])
    count, model = tokens.shape
    encoder_count = encoded.shape[0]
    hidden_units = ffn_in.shape[1]
    heads = model // HEAD
    half = model // 2
    segs = passage_group.shape[1]
    low_type, wide_type = jnp.bfloat16, jnp.float32

    def my_columns(matrix, owner):
        width = matrix.shape[-1] // 2
        return lax.dynamic_slice_in_dim(matrix, owner * width, width, axis=matrix.ndim - 1)

    barrier = lax.optimization_barrier
    gains = jnp.stack([self_gain, cross_gain, ffn_gain], axis=1)
    gains = jnp.pad(gains, ((0, 0), (0, PAIR - 3)))
    shards = [self_query, self_key, self_value, self_out, cross_query, cross_key, cross_value, cross_out]
    rows_in = ffn_in.shape[0]
    rows_down = ffn_out.shape[0]
    direct = rows_down % 16 == 0
    chip_groups = devices // 4
    group_bits = [0, 1]
    packed = shaped((rows_in, len(shards) * half + PAIR + 2 * model), low_type)
    send, keep = call(
        pack_kernel, "pack", 0, [SMEM] + [VMEM] * 10, [VMEM] * 2, (packed, packed), []
    )(core_word, *shards, gains, ffn_in)
    theirs = swap_with(send, 1, devices)
    chip_block = pair_up(keep, theirs, core, 0).reshape(-1, keep.shape[1])
    self_block = jnp.concatenate([chip_block[:, : 2 * model], chip_block[:, 4 * model : 4 * model + PAIR]], axis=1)
    in_halves = chip_block[:, 4 * model + PAIR :].reshape(2 * rows_in, chip_groups // 2, 2, 2 * rows_down)
    in_halves = in_halves.swapaxes(1, 2).reshape(2 * rows_in, 2 * model)
    cross_block = chip_block[:, 2 * model : 4 * model]

    def double(held, bit, first_bit, me):
        place = 1 if first_bit is None or bit > first_bit else 2
        return pair_up(held, swap_with(held, 1 << bit, devices), bit_of(me, bit), place)

    def first_step(line, width):
        return [double(part, order[0], None, me) for part, order in zip((line[:, :, :width], line[:, :, width:]), pair_orders)]

    def second_step(parts):
        return [
            double(part, order[1], order[0], me).reshape(-1, part.shape[-1])
            for part, order in zip(parts, pair_orders)
        ]

    cotangent_theirs = swap_with(cotangent, 2, devices)

    def block_for(array, mask):
        first = [bit_of(me, 1) ^ (mask >> 1 & 1), core ^ (mask & 1)]
        return lax.dynamic_slice(array, first + [0, 0], (1, 1) + array.shape[2:]).reshape(array.shape[2:])

    ffn_steps = line_bits + [2]

    def merged(held, theirs, steps, number):
        bit = steps[number]
        place = sum(1 for other in steps[:number] if other > bit)
        return pair_up(held, theirs, bit_of(me, bit), place)

    def brought(held, steps, number):
        return swap_with(held, 1 << steps[number], devices)

    def half_at(array, place):
        return lax.dynamic_slice_in_dim(array, place * model, model, axis=1)

    self_line = gather_line(self_block, line_bits, me, devices)
    self_line, cross_held, in_halves, cotangent_theirs, down_held = barrier(
        (self_line, cross_block, in_halves, cotangent_theirs, ffn_out)
    )
    y_bit = bit_of(me, 1)
    in_theirs = swap_with(half_at(in_halves, 1 - y_bit), 2, devices)
    last = len(line_bits) - 1
    self_parts = first_step(self_line, model)
    for number in range(last):
        cross_held = merged(cross_held, brought(cross_held, line_bits, number), line_bits, number)
        down_held = merged(down_held, brought(down_held, ffn_steps, number), ffn_steps, number)
    self_parts, cross_held, in_theirs, down_held = barrier((self_parts, cross_held, in_theirs, down_held))
    in_held = pair_up(half_at(in_halves, y_bit), in_theirs, y_bit, 0).reshape(4 * rows_in, model)
    self_theirs = [brought(part, [2, 1, 2], n + 1) for n, part in enumerate(self_parts)]
    cross_line = merged(cross_held, brought(cross_held, line_bits, last), line_bits, last)
    cross_line = cross_line.reshape((-1,) + cross_block.shape)
    for number in range(last):
        in_held = merged(in_held, brought(in_held, ffn_steps, number), ffn_steps, number)
    down_theirs = brought(down_held, ffn_steps, last)
    cross_line, in_held, down_theirs, self_theirs = barrier((cross_line, in_held, down_theirs, self_theirs))
    cross_parts = first_step(cross_line, model)
    cross_parts = [with_layout_constraint(part, Layout(tuple(range(part.ndim)))) for part in cross_parts]
    in_theirs = brought(in_held, ffn_steps, last)
    cross_parts, in_theirs = barrier((cross_parts, in_theirs))
    in_held = merged(in_held, in_theirs, ffn_steps, last)
    down_held = merged(down_held, down_theirs, ffn_steps, last)
    in_held, down_held = (
        with_layout_constraint(held, Layout(tuple(range(held.ndim)))) for held in (in_held, down_held)
    )

    def second_merge(parts, theirs):
        return [
            pair_up(part, other, bit_of(me, order[1]), 1 if order[1] > order[0] else 2).reshape(-1, part.shape[-1])
            for part, other, order in zip(parts, theirs, pair_orders)
        ]

    self_mine = second_merge(self_parts, self_theirs)
    cross_theirs = [brought(part, [2, 1, 2], n + 1) for n, part in enumerate(cross_parts)]
    self_weights = [(mine, swap_with(mine[:, :model], 1, devices)) for mine in self_mine]

    gain_rows = self_weights[1][0][:, model : model + 8].T.astype(wide_type)
    self_flat = self_weights[0] + self_weights[1]

    dma = pltpu.SemaphoreType.DMA
    weights_kept = pltpu.VMEM((4, 2, model, half), low_type)
    projected, context_one, after_self = call(
        self_forward_kernel,
        "self_forward",
        2 * count * model * model * 5,
        [SMEM, VMEM, VMEM, VMEM] + [ANY] * 4,
        [VMEM] * 3,
        (
            shaped((3, count, model), low_type),
            shaped((count, model), low_type),
            shaped((count, model), wide_type),
        ),
        [weights_kept, dma((8,))],
        room=MIDDLE_BYTES,
    )(core_word, segment_ids, tokens, gain_rows, *self_flat)

    cross_direct = 2 * rows_in % 16 == 0
    cross_sibling = [swap_with(part, 1, devices) for part in cross_parts]
    cross_theirs, cross_sibling, in_held, down_held, after_self = barrier(
        (cross_theirs, cross_sibling, in_held, down_held, after_self)
    )
    in_theirs, down_theirs = swap_with(in_held, 4, devices), swap_with(down_held, 4, devices)
    in_sibling, down_sibling = swap_with(in_held, 1, devices), swap_with(down_held, 1, devices)
    sibling_theirs = [swap_with(theirs, 1, devices) for theirs in cross_theirs]
    if cross_direct:
        cross_weights = list(zip(cross_parts, cross_theirs, cross_sibling, sibling_theirs))
        cross_rows = cross_parts[0].shape[:1] + (2, 2, 2 * rows_in, half)
    else:
        cross_weights = list(
            zip(second_merge(cross_parts, cross_theirs), second_merge(cross_sibling, sibling_theirs))
        )
        cross_rows = (model, half)
    pieces = len(cross_weights[0])
    cross_flat = list(cross_weights[0]) + list(cross_weights[1])
    cross_kept = pltpu.VMEM((4, 2) + cross_rows, low_type)

    per_token = (heads, count, model)
    probs_shape = (heads, count, encoder_count // segs)
    probs_kept, tokens_kept = pltpu.VMEM(probs_shape, low_type), pltpu.VMEM(per_token, low_type)
    chunk_count = count // CHUNK
    chunk_table = pltpu.SMEM((4, chunk_count + segs), jnp.int32)
    queries_two, context_two, after_cross, normed_three, probs, mixed, spread = call(
        functools.partial(cross_forward_kernel, pieces),
        "cross_forward",
        12_000_000_000,
        [SMEM, SMEM, SMEM, VMEM, VMEM] + [HBM] * (1 + 2 * pieces),
        [VMEM] * 4 + [HBM] * 3,
        (
            shaped((count, model), low_type),
            shaped((count, model), low_type),
            shaped((count, model), wide_type),
            shaped((count, model), low_type),
            shaped(probs_shape, low_type),
            shaped(per_token, low_type),
            shaped(per_token, low_type),
        ),
        [
            probs_kept, tokens_kept, tokens_kept, pltpu.VMEM(encoded.shape, low_type), cross_kept,
            chunk_table, dma((segs,)), dma((4 * pieces,)), dma((3,)),
        ],
    )(me_word, starts, passage_group, after_self, gain_rows, encoded, *cross_flat)

    normed_theirs = swap_with(normed_three, 2, devices)
    in_theirs, down_theirs, in_sibling, down_sibling, normed_theirs = barrier(
        (in_theirs, down_theirs, in_sibling, down_sibling, normed_theirs)
    )
    in_fourth, down_fourth = swap_with(in_theirs, 1, devices), swap_with(down_theirs, 1, devices)
    ffn_pieces = [in_held, down_held, in_theirs, down_theirs, in_sibling, down_sibling, in_fourth, down_fourth]
    half_units = hidden_units // 2
    high = (2,) * (len(chip_bits) - 1)
    if direct:
        in_shape = (2, chip_groups, rows_down, model)
        down_shape = (chip_groups, 2, rows_down, model)
        ffn_weights = ffn_pieces
        grad_shapes = (shaped((chip_groups, 2 * rows_down, model), low_type),) * 2
    else:
        in_shape, down_shape = (2, 1, model, model), (1, 1, half_units, model)
        ffn_mine = [
            pair_up(held, theirs, bit_of(me, 2), len(line_bits)).reshape((chip_groups,) + held.shape[-2:])
            for held, theirs in ((in_held, in_theirs), (down_held, down_theirs))
        ]
        ffn_sibling = [
            pair_up(held, theirs, bit_of(me, 2), len(line_bits)).reshape((chip_groups,) + held.shape[-2:])
            for held, theirs in ((in_sibling, in_fourth), (down_sibling, down_fourth))
        ]
        ffn_weights = (
            pair_up(ffn_mine[0], ffn_sibling[0], core, 0).reshape(in_shape),
            pair_up(ffn_mine[1], ffn_sibling[1], core, 1).reshape(down_shape),
        )
        grad_shapes = (shaped(in_shape, low_type), shaped(down_shape, low_type))
    token_shapes = (shaped((count, model), wide_type), shaped((count, model), low_type))
    out_mine, out_other, pull_mine, pull_other, ffn_grad, ffn_other = call(
        functools.partial(ffn_kernel, direct),
        "ffn",
        4_000_000_000,
        [SMEM] + [VMEM] * 4 + [ANY] * len(ffn_weights),
        [VMEM] * 4 + [HBM] * 2,
        token_shapes + token_shapes + grad_shapes,
        [
            pltpu.VMEM((2,) + high + in_shape[2:] if direct else in_shape, low_type),
            pltpu.VMEM(high + down_shape[1:] if direct else down_shape, low_type),
            pltpu.VMEM(in_shape, low_type),
            pltpu.VMEM(down_shape, low_type),
            dma((8,)),
            dma((4,)),
        ],
        room=MIDDLE_BYTES,
    )(me_word, normed_three, normed_theirs, cotangent, cotangent_theirs, *ffn_weights)
    pull_theirs = swap_with(pull_other, 2, devices)
    if not direct:
        in_parts = ffn_grad.reshape(2, chip_groups, 4 * rows_in, model)
        down_parts = ffn_other.reshape(chip_groups, 2, rows_down, model).swapaxes(0, 1)
        both = jnp.concatenate([in_parts, down_parts], axis=2)
        ffn_grad, ffn_other = (
            lax.dynamic_index_in_dim(both, place, 0, keepdims=False) for place in (core, 1 - core)
        )
    ffn_theirs = swap_with(ffn_other, 1, devices)
    high_bits = [bit for bit in sorted(chip_bits, reverse=True) if bit > 1]

    def group_source(array):
        return (array.reshape((2,) * len(high_bits) + array.shape[-2:]), high_bits, 0)

    ffn_entry = ([group_source(ffn_grad), group_source(ffn_theirs)], (0, model))
    ffn_send = low(summed(ffn_entry, {2: 1 - bit_of(me, 2)}))
    pull_theirs, ffn_send = barrier((pull_theirs, ffn_send))
    ffn_sum = [with_brought(ffn_entry, swap_with(ffn_send, 4, devices), 2, [])]

    all_bits = sorted(chip_bits, reverse=True)

    def chips_of(array):
        return array.reshape((2,) * len(all_bits) + (array.shape[0] >> len(all_bits), array.shape[-1]))

    def entry_of(mine, theirs, begin, end):
        return ([(chips_of(mine), all_bits, 0), (chips_of(theirs), all_bits, 0)], (begin, end))

    def first_sum(sides):
        return [sum_over(entries, order[0], [], me, devices) for entries, order in zip(sides, pair_orders)]

    def second_sum(sides):
        return [sum_over(entries, order[1], order[:1], me, devices) for entries, order in zip(sides, pair_orders)]

    def received(sides):
        return [entries[0][0][-1][0] for entries in sides]

    def with_received(sides, arrays):
        return [
            [(sources[:-1] + [(array,) + sources[-1][1:]], columns) for sources, columns in entries]
            for entries, array in zip(sides, arrays)
        ]

    grads_shape = shaped((model, 2 * model), low_type)
    rows_kept = pltpu.VMEM(encoded.shape, low_type)
    grad_after_self, gain_grads, score_grads, pulled, cross_mine_grad, cross_other_grad = call(
        functools.partial(cross_backward_kernel, pieces),
        "cross_backward",
        4_000_000_000,
        [SMEM, SMEM, SMEM] + [VMEM] * 8 + [HBM] * (3 + 2 * pieces),
        [VMEM] * 2 + [HBM] * 4,
        (
            shaped((count, model), wide_type),
            shaped((8, model), wide_type),
            shaped(probs_shape, low_type),
            shaped(per_token, low_type),
            grads_shape,
            grads_shape,
        ),
        [
            pltpu.VMEM((count, model), wide_type), pltpu.VMEM((count, model), low_type), tokens_kept, probs_kept,
            tokens_kept, probs_kept, rows_kept, tokens_kept, cross_kept, weights_kept,
            chunk_table, dma((segs,)), dma((4 * pieces,)), dma((11,)), dma((1, chunk_count)),
        ],
    )(
        me_word, starts, passage_group, after_cross, after_self, gain_rows, cotangent, pull_mine, pull_theirs,
        queries_two, context_two, mixed, encoded, probs, *cross_flat,
    )
    arrays, grad_after_self, cross_mine_grad, cross_other_grad = barrier(
        (received([ffn_sum]), grad_after_self, cross_mine_grad, cross_other_grad)
    )
    ffn_sum = with_received([ffn_sum], arrays)[0]
    ffn_done = [2]
    for bit in sorted(line_bits)[:-1]:
        ffn_sum = sum_over(ffn_sum, bit, ffn_done, me, devices)
        ffn_done = ffn_done + [bit]
    cross_theirs_grad = swap_with(cross_other_grad, 1, devices)

    with_gains = shaped((model, 2 * model + PAIR), low_type)
    tokens_grad, self_mine, self_other = call(
        self_backward_kernel,
        "self_backward",
        2 * count * model * model * 10,
        [SMEM] + [VMEM] * 7 + [ANY] * 4,
        [VMEM] + [HBM] * 2,
        (shaped((count, model), wide_type), with_gains, with_gains),
        [weights_kept, weights_kept, pltpu.VMEM((model, PAIR), low_type), dma((8,)), dma((10,))],
        room=MIDDLE_BYTES,
    )(
        core_word, segment_ids, tokens, gain_rows, grad_after_self, gain_grads, projected, context_one,
        *self_flat,
    )
    arrays, cross_theirs_grad, self_mine, self_other = barrier(
        (received([ffn_sum]), cross_theirs_grad, self_mine, self_other)
    )
    ffn_sum = with_received([ffn_sum], arrays)[0]
    ffn_sum = sum_over(ffn_sum, max(line_bits), ffn_done, me, devices)
    self_theirs = swap_with(self_other, 1, devices)
    crossed = [
        [entry_of(cross_mine_grad, cross_theirs_grad, *cut)] for cut in ((0, model), (model, 2 * model))
    ]
    crossed = first_sum(crossed)
    self_theirs, score_grads = barrier((self_theirs, score_grads))
    attention = [
        [entry_of(self_mine, self_theirs, *cut)] for cut in ((0, model), (model, 2 * model + PAIR))
    ]
    attention = first_sum(attention)
    encoded_grad = call(
        rows_backward_kernel,
        "rows_backward",
        3_000_000_000,
        [SMEM, SMEM] + [HBM] * 4,
        HBM,
        shaped(encoded.shape, wide_type),
        [
            probs_kept, probs_kept, tokens_kept, tokens_kept,
            pltpu.VMEM((2, encoder_count // segs, model), wide_type), dma((2,)), dma((4, chunk_count)),
        ],
    )(starts, passage_group, score_grads, probs, spread, pulled)
    crossed_arrays, arrays, ffn_arrays, encoded_grad = barrier(
        (received(crossed), received(attention), received([ffn_sum]), encoded_grad)
    )
    ffn_sum = with_received([ffn_sum], ffn_arrays)[0]
    ffn_rows = summed(ffn_sum[0], {bit: bit_of(me, bit) for bit in high_bits})
    summed_down = ffn_rows[4 * rows_in :]
    in_parts = ffn_rows[: 4 * rows_in].reshape(2, 2, rows_in, model)
    in_parts = exchange(lambda mask: block_for(in_parts, mask), group_bits, me, devices)
    in_parts = in_parts.reshape(2, 2, rows_in, chip_groups // 2, 2 * rows_down)
    summed_in = in_parts.transpose(2, 1, 3, 0, 4).reshape(rows_in, hidden_units)
    crossed, attention = with_received(crossed, crossed_arrays), with_received(attention, arrays)
    groups = [(entries, order[1], order[:1]) for entries, order in zip(crossed, pair_orders)]
    sends = [sends_of(*group, me) for group in groups]
    sends, arrays = barrier((sends, received(attention)))
    crossed = [sum_over(*group, me, devices, send) for group, send in zip(groups, sends)]
    attention = second_sum(with_received(attention, arrays))
    cross_blocks = line_blocks(me_word, crossed[0] + crossed[1], line_bits, [2, 1], devices)
    unused_blocks, arrays = barrier((cross_blocks, received(attention)))
    attention = with_received(attention, arrays)
    cross_terms = brought_blocks(cross_blocks, line_bits, devices)
    self_blocks = line_blocks(me_word, attention[0] + attention[1], line_bits, [2, 1], devices)
    self_terms = brought_blocks(self_blocks, line_bits, devices)
    unused_blocks, out_other = barrier((cross_blocks, out_other))
    out_theirs = swap_with(out_other, 2, devices)
    self_terms, summed_in, out_theirs = barrier((self_terms, summed_in, out_theirs))
    block_out = low(after_cross + (out_mine + out_theirs.astype(wide_type)))

    def spread_out(terms, matrices, gains):
        found = terms[0]
        for term in terms[1:]:
            found = found + term.astype(wide_type)
        keep = lax.dynamic_slice_in_dim(found, core * rows_in, rows_in, axis=0)
        send = lax.dynamic_slice_in_dim(found, (1 - core) * rows_in, rows_in, axis=0)
        shapes = (shaped((rows_in, model), wide_type),) * matrices
        if gains:
            shapes += (shaped((rows_in, PAIR), wide_type),)
        return call(
            functools.partial(spread_kernel, matrices),
            "spread",
            1_000_000,
            [SMEM, VMEM, VMEM],
            [VMEM] * len(shapes),
            shapes,
            [],
            room=SMALL_BYTES,
        )(core_word, keep, swap_with(send, 1, devices))

    summed_cv, summed_cq, summed_co, summed_ck = spread_out(cross_terms, 4, False)
    summed_query, summed_key, summed_value, summed_out, own_gains = spread_out(self_terms, 4, True)
    return (
        block_out,
        tokens_grad,
        encoded_grad,
        own_gains[:, 0],
        own_gains[:, 1],
        own_gains[:, 2],
        summed_query,
        summed_key,
        summed_value,
        summed_out,
        summed_cq,
        summed_ck,
        summed_cv,
        summed_co,
        summed_in,
        summed_down,
    )


def solution(mesh):
    return jax.shard_map(
        functools.partial(per_device, mesh.shape["fsdp"], mesh.size),
        mesh=mesh,
        in_specs=(
            P(("dp", "fsdp"), None),
            P(("dp", "fsdp"), None),
            P(("dp", "fsdp"), None),
            P(("dp", "fsdp"), None),
            P(("dp", "fsdp"), None),
            P(("dp", "fsdp")),
            P(("dp", "fsdp")),
            P(("dp", "fsdp")),
            P(("dp", "fsdp"), None),
            P(("dp", "fsdp"), None),
            P(("dp", "fsdp"), None),
            P(("dp", "fsdp"), None),
            P(("dp", "fsdp"), None),
            P(("dp", "fsdp"), None),
            P(("dp", "fsdp"), None),
            P(("dp", "fsdp"), None),
            P(("dp", "fsdp"), None),
            P(("dp", "fsdp"), None),
        ),
        out_specs=(
            P(("dp", "fsdp"), None),
            P(("dp", "fsdp"), None),
            P(("dp", "fsdp"), None),
            P(("dp", "fsdp")),
            P(("dp", "fsdp")),
            P(("dp", "fsdp")),
            P(("dp", "fsdp"), None),
            P(("dp", "fsdp"), None),
            P(("dp", "fsdp"), None),
            P(("dp", "fsdp"), None),
            P(("dp", "fsdp"), None),
            P(("dp", "fsdp"), None),
            P(("dp", "fsdp"), None),
            P(("dp", "fsdp"), None),
            P(("dp", "fsdp"), None),
            P(("dp", "fsdp"), None),
        ),
        check_vma=False,
    )
```

```python
import functools

import jax
import jax.numpy as jnp
from jax import lax
from jax.experimental import pallas as pl
from jax.experimental.layout import Layout, with_layout_constraint
from jax.experimental.pallas import tpu as pltpu
from jax.sharding import PartitionSpec as P

HEAD = 64
CHUNK = 16
PAIR = 2 * HEAD
epsilon = 1e-06
masked_score = -1e30
VMEM_BYTES = 60 << 20
MIDDLE_BYTES = 32 << 20
SMALL_BYTES = 20 << 20


def contract(left, right, left_dim, right_dim):
    return lax.dot_general(
        left, right, (((left_dim,), (right_dim,)), ((), ())), preferred_element_type=jnp.float32
    )


def low(values):
    return values.astype(jnp.bfloat16)


def normalize(values, gain_row):
    return values * lax.rsqrt(jnp.mean(values * values, axis=-1, keepdims=True) + epsilon) * gain_row


def norm_backward(values, gain_row, grad):
    scale = lax.rsqrt(jnp.mean(values * values, axis=-1, keepdims=True) + epsilon)
    grad_gain = jnp.sum(grad * values * scale, axis=0, keepdims=True)
    weighted = gain_row * grad
    inner = jnp.mean(weighted * values, axis=-1, keepdims=True)
    return scale * weighted - values * (scale * scale * scale) * inner, grad_gain


def pair_rows(block):
    lane = lax.broadcasted_iota(jnp.int32, block.shape, 1)
    zero = jnp.zeros_like(block)
    return jnp.concatenate(
        [jnp.where(lane < HEAD, block, zero), jnp.where(lane >= HEAD, block, zero)], axis=0
    )


def pair_lanes(both):
    rows = both.shape[0] // 2
    lane = lax.broadcasted_iota(jnp.int32, (rows, both.shape[1]), 1)
    return jnp.where(lane < HEAD, both[:rows], both[rows:])


def weight_copies(core, sources, kept, sems):
    half = kept.shape[-1]
    copies = []
    for number in range(kept.shape[0]):
        for side, source in enumerate(sources[number // 2]):
            place = core if side == 0 else 1 - core
            copies.append(
                pltpu.make_async_copy(
                    source.at[:, (number % 2) * half : (number % 2 + 1) * half],
                    kept.at[number, place],
                    sems.at[2 * number + side],
                )
            )
    return copies


def piece_copies(me, pairs, kept, sems):
    core = me & 1
    half = kept.shape[-1]
    copies = []
    for number in range(kept.shape[0]):
        bit, pieces = pairs[number // 2]
        columns = slice((number % 2) * half, (number % 2 + 1) * half)
        for n, piece in enumerate(pieces):
            whole = len(pieces) == 2
            place = core if n < len(pieces) // 2 else 1 - core
            target = kept.at[number, place]
            if not whole:
                at = ((me >> bit) & 1) ^ (n & 1)
                target = kept.at[number, place, :, :, at] if bit == 1 else kept.at[number, place, :, at]
                piece = piece.at[:, :, :, columns]
            else:
                piece = piece.at[:, columns]
            copies.append(pltpu.make_async_copy(piece, target, sems.at[len(pieces) * number + n]))
    return copies


def whole_rows(kept, number, side):
    return kept[number, side].reshape(-1, kept.shape[-1])


def times(left, kept, number):
    return jnp.concatenate([contract(left, whole_rows(kept, number, side), 1, 0) for side in range(2)], axis=1)


def times_back(left, kept, number):
    half = kept.shape[-1]
    return contract(left[:, :half], whole_rows(kept, number, 0), 1, 1) + contract(
        left[:, half:], whole_rows(kept, number, 1), 1, 1
    )


def grad_into(left, right, held, number):
    half = held.shape[-1]
    for side in range(2):
        held[number, side] = low(contract(left, right[:, side * half : (side + 1) * half], 0, 0))


def grad_copies(core, targets, held, number, sems, place_of=None):
    half = held.shape[-1]
    at = number if place_of is None else place_of[number]
    copies = []
    for side, target in enumerate(targets):
        place = core if side == 0 else 1 - core
        copies.append(
            pltpu.make_async_copy(
                held.at[number, place],
                target.at[:, at * half : (at + 1) * half],
                sems.at[2 * number + side],
            )
        )
    return copies


def spread_kernel(matrices, core_ref, keep, theirs, *targets):
    core = core_ref[0]
    half = targets[0].shape[1] // 2
    for number, target in enumerate(targets[:matrices]):
        columns = slice(number * half, (number + 1) * half)
        for side in range(2):
            target[:, side * half : (side + 1) * half] = jnp.where(core == side, keep[:, columns], theirs[:, columns])
    for target in targets[matrices:]:
        target[...] = keep[:, matrices * half :]


def pack_kernel(core_ref, *refs):
    shards, gains, wide_shard, (send, keep) = refs[:-4], refs[-4], refs[-3], refs[-2:]
    core = core_ref[0]
    half = shards[0].shape[1] // 2
    wide = wide_shard.shape[1] // 2
    at = len(shards) * half
    for target, place in ((send, 1 - core), (keep, core)):
        for number, shard in enumerate(shards):
            target[:, number * half : (number + 1) * half] = shard[:, pl.ds(pl.multiple_of(place * half, PAIR), half)]
        target[:, at : at + PAIR] = gains[...]
        target[:, at + PAIR :] = wide_shard[:, pl.ds(pl.multiple_of(place * wide, PAIR), wide)]


def self_mask(ids_row):
    tokens = ids_row.shape[1]
    wide = jnp.broadcast_to(ids_row.astype(jnp.float32), (tokens, tokens))
    query = lax.broadcasted_iota(jnp.int32, (tokens, tokens), 0)
    key = lax.broadcasted_iota(jnp.int32, (tokens, tokens), 1)
    allowed = jnp.where((wide == wide.T) & (key <= query), 1.0, 0.0)
    return jnp.concatenate([allowed, allowed], axis=0) > 0.5


def self_probs(queries, keys, allowed):
    scores = jnp.where(allowed, contract(pair_rows(queries), keys, 1, 1) * 0.125, masked_score)
    weights = jnp.exp(scores - jnp.max(scores, axis=-1, keepdims=True))
    return weights / jnp.sum(weights, axis=-1, keepdims=True)


def self_forward_kernel(
    core_ref, ids, tokens, gains, first_mine, first_sibling, second_mine, second_sibling,
    projected, context, after, kept, sems,
):
    core = core_ref[0]
    copies = weight_copies(
        core, ((first_mine, first_sibling), (second_mine, second_sibling)), kept, sems
    )
    for copy in copies:
        copy.start()
    model = tokens.shape[1]
    hidden = tokens[...].astype(jnp.float32)
    normed = low(normalize(hidden, gains[0:1, :]))
    for number in range(3):
        copies[2 * number].wait()
        copies[2 * number + 1].wait()
        projected[number] = low(times(normed, kept, number))
    allowed = self_mask(ids[...])
    for j in range(model // PAIR):
        columns = slice(j * PAIR, (j + 1) * PAIR)
        probs = self_probs(projected[0, :, columns], projected[1, :, columns], allowed)
        context[:, columns] = low(pair_lanes(contract(low(probs), projected[2, :, columns], 1, 0)))
    copies[6].wait()
    copies[7].wait()
    after[...] = hidden + times(context[...], kept, 3)


def self_backward_kernel(
    core_ref, ids, tokens, gains, grad_after, gain_grads, projected, context,
    first_mine, first_sibling, second_mine, second_sibling,
    tokens_grad, grad_mine, grad_other,
    kept, held, gain_held, sems, out_sems,
):
    core = core_ref[0]
    copies = weight_copies(
        core, ((first_mine, first_sibling), (second_mine, second_sibling)), kept, sems
    )
    for copy in copies:
        copy.start()
    model = tokens.shape[1]
    count = tokens.shape[0]
    hidden = tokens[...].astype(jnp.float32)
    normed = low(normalize(hidden, gains[0:1, :]))
    branch = low(grad_after[...])
    started = []

    def send(number):
        for copy in grad_copies(core, (grad_mine, grad_other), held, number, out_sems):
            copy.start()
            started.append(copy)

    grad_into(context[...], branch, held, 3)
    send(3)
    for copy in copies:
        copy.wait()
    grad_context = low(times_back(branch, kept, 3))
    allowed = self_mask(ids[...])
    found = ([], [], [])
    for j in range(model // PAIR):
        columns = slice(j * PAIR, (j + 1) * PAIR)
        queries, keys = projected[0, :, columns], projected[1, :, columns]
        probs = self_probs(queries, keys, allowed)
        pulled = pair_rows(grad_context[:, columns])
        prob_grad = contract(pulled, projected[2, :, columns], 1, 1)
        inner = jnp.sum(probs * prob_grad, axis=-1, keepdims=True)
        score_grad = low(probs * (prob_grad - inner))
        found[0].append(low(pair_lanes(contract(score_grad, keys, 1, 0)) * 0.125))
        found[1].append(low(contract(score_grad, pair_rows(queries), 0, 0) * 0.125))
        found[2].append(low(contract(low(probs), pulled, 0, 0)))
    grad_normed = None
    for number in range(3):
        whole = jnp.concatenate(found[number], axis=1)
        grad_into(normed, whole, held, number)
        send(number)
        part = times_back(whole, kept, number)
        grad_normed = part if grad_normed is None else grad_normed + part
    grad_hidden, grad_gain = norm_backward(hidden, gains[0:1, :], grad_normed)
    tokens_grad[...] = grad_after[...] + grad_hidden
    row = lax.broadcasted_iota(jnp.int32, (count, model), 0)
    others = gain_grads[...]
    wide = jnp.where(
        row == 0, grad_gain, jnp.where(row == 1, others[0:1], jnp.where(row == 2, others[1:2], 0.0))
    )
    gain_held[...] = low(wide.T)
    for slot, target in enumerate((grad_mine, grad_other)):
        copy = pltpu.make_async_copy(gain_held, target.at[:, 2 * model :], out_sems.at[8 + slot])
        copy.start()
        started.append(copy)
    for copy in started:
        copy.wait()


def row_copies(encoded, rows_ref, sems, segs):
    size = encoded.shape[0] // segs
    return [
        pltpu.make_async_copy(
            encoded.at[pl.ds(s * size, size)], rows_ref.at[pl.ds(s * size, size)], sems.at[s]
        )
        for s in range(segs)
    ]


def block_copy(encoded, rows_ref, sems, groups, s):
    size = encoded.shape[0] // groups.shape[1]
    at = pl.ds(pl.multiple_of(groups[0, s] * size, size), size)
    return pltpu.make_async_copy(encoded.at[at], rows_ref.at[at], sems.at[s])


def chunk_copies(pairs, sems, c):
    at = (slice(None), pl.ds(pl.multiple_of(c * CHUNK, CHUNK), CHUNK), slice(None))
    return [pltpu.make_async_copy(source.at[at], target.at[at], sems.at[n, c]) for n, (source, target) in enumerate(pairs)]


def list_chunks(starts, table):
    def query(s, count):
        begin, end = starts[0, s], starts[0, s + 1]

        def chunk(c, count):
            table[0, count] = c * CHUNK
            table[1, count] = s
            table[2, count] = (c == begin >> 4).astype(jnp.int32)
            table[3, count] = ((c * CHUNK >= begin) | (begin & (CHUNK - 1) == 0)).astype(jnp.int32)
            return count + 1

        return lax.fori_loop(begin >> 4, (end + CHUNK - 1) >> 4, chunk, count)

    return lax.fori_loop(0, starts.shape[1] - 1, query, 0)


def listed(starts, table, at):
    s = table[1, at]
    return pl.multiple_of(table[0, at], CHUNK), s, starts[0, s], starts[0, s + 1]


def in_segment(token, begin, end, heads):
    row = lax.broadcasted_iota(jnp.int32, (heads, CHUNK, 1), 1) + token
    return (row >= begin) & (row < end)


def pair_weight(kept, number, j):
    per_half = kept.shape[-1] // PAIR
    columns = slice((j % per_half) * PAIR, (j % per_half + 1) * PAIR)
    at = (number, j // per_half) + (slice(None),) * (len(kept.shape) - 3) + (columns,)
    return kept[at].reshape(-1, PAIR)


def cross_forward_kernel(
    pieces, me_ref, starts, groups, after_self, gains, encoded, *refs,
):
    first, second = refs[:pieces], refs[pieces : 2 * pieces]
    queries, context, after_cross, normed_out, probs_hbm, mixed_hbm, spread_hbm = refs[2 * pieces : 2 * pieces + 7]
    probs_out, mixed_out, spread_out, rows_ref, kept, table, sems, weight_sems, out_sems = refs[2 * pieces + 7 :]
    heads, tokens, model = spread_out.shape
    segs = groups.shape[1]
    block_rows = encoded.shape[0] // segs
    copies = piece_copies(me_ref[0], ((1, first), (2, second)), kept, weight_sems)
    early, late = copies[: 2 * pieces], copies[2 * pieces :]
    for copy in early:
        copy.start()
    for s in range(segs):
        block_copy(encoded, rows_ref, sems, groups, s).start()
    leaving = [
        pltpu.make_async_copy(source, target, out_sems.at[n])
        for n, (source, target) in enumerate(
            ((spread_out, spread_hbm), (probs_out, probs_hbm), (mixed_out, mixed_hbm))
        )
    ]
    for copy in late:
        copy.start()
    normed = low(normalize(after_self[...], gains[1:2, :]))
    for copy in early:
        copy.wait()
    queries[...] = low(times(normed, kept, 0))
    for j in range(heads // 2):
        block = queries[:, j * PAIR : (j + 1) * PAIR] * jnp.bfloat16(0.125)
        spread = low(contract(pair_rows(block), pair_weight(kept, 1, j), 1, 1))
        spread_out[2 * j] = spread[:tokens]
        spread_out[2 * j + 1] = spread[tokens:]
    leaving[0].start()

    count = list_chunks(starts, table)

    def two_chunks(i, carry):
        places = [2 * i, jnp.minimum(2 * i + 1, count - 1)]
        for n, place in enumerate(places):

            @pl.when((2 * i + n < count) & (table[2, place] == 1))
            def _():
                block_copy(encoded, rows_ref, sems, groups, table[1, place]).wait()

        found, scores, blocks = [], [], []
        for place in places:
            token, s, begin, end = listed(starts, table, place)
            base = pl.multiple_of(groups[0, s] * block_rows, block_rows)
            found.append((token, begin, end))
            blocks.append(rows_ref[pl.ds(base, block_rows), :])
            left = spread_out[:, pl.ds(token, CHUNK), :].reshape(heads * CHUNK, model)
            scores.append(contract(left, blocks[-1], 1, 1))
        for (token, begin, end), score, rows in zip(found, scores, blocks):
            weights = jnp.exp(score - jnp.max(score, axis=-1, keepdims=True))
            totals = jnp.sum(weights, axis=-1, keepdims=True)
            probs = low(weights * (1.0 / totals))
            mixed = low(contract(probs, rows, 1, 0))
            inside = in_segment(token, begin, end, heads)
            at = (slice(None), pl.ds(token, CHUNK), slice(None))
            probs = probs.reshape(heads, CHUNK, block_rows)
            mixed = mixed.reshape(heads, CHUNK, model)
            probs_out[at] = jnp.where(inside, probs, probs_out[at])
            mixed_out[at] = jnp.where(inside, mixed, mixed_out[at])
        return carry

    lax.fori_loop(0, (count + 1) >> 1, two_chunks, 0)
    for copy in leaving[1:]:
        copy.start()
    for copy in late:
        copy.wait()
    for j in range(heads // 2):
        both = jnp.concatenate([mixed_out[2 * j], mixed_out[2 * j + 1]], axis=0)
        found = contract(both, pair_weight(kept, 2, j), 1, 0)
        context[:, j * PAIR : (j + 1) * PAIR] = low(pair_lanes(found))
    after_cross[...] = after_self[...] + times(context[...], kept, 3)
    normed_out[...] = low(normalize(after_cross[...], gains[2:3, :]))
    for copy in leaving:
        copy.wait()


def cross_backward_kernel(
    pieces, me_ref, starts, groups, after_cross, after_self, gains, cotangent, pull_mine, pull_theirs, queries, context,
    mixed_hbm, encoded, probs_hbm, *refs,
):
    first, second, refs = refs[:pieces], refs[pieces : 2 * pieces], refs[2 * pieces :]
    grad_self, gain_grads, score_hbm, pulled_hbm, grad_mine, grad_other = refs[:6]
    grad_after, grad_context, mixed, probs_ref, pulled_ref, score_out, rows_ref, moved_ref, kept, held, table = refs[6:17]
    sems, weight_sems, out_sems, chunk_sems = refs[17:]
    core = me_ref[0] & 1
    heads, tokens, model = pulled_ref.shape
    segs = groups.shape[1]
    block_rows = encoded.shape[0] // segs
    half = held.shape[-1]
    copies = piece_copies(me_ref[0], ((1, first), (2, second)), kept, weight_sems)
    query_part, key_part, value_part, out_part = (copies[n * pieces : (n + 1) * pieces] for n in range(4))
    coming = pltpu.make_async_copy(mixed_hbm, mixed, out_sems.at[8])
    for copy in out_part + value_part + [coming]:
        copy.start()
    chunk_pairs = ((probs_hbm, probs_ref),)
    started = []

    def send(number):
        for copy in grad_copies(core, (grad_mine, grad_other), held, number, out_sems, (1, 3, 0, 2)):
            copy.start()
            started.append(copy)

    grad_normed = pull_mine[...] + pull_theirs[...].astype(jnp.float32)
    grad_values, found_gain = norm_backward(after_cross[...], gains[2:3, :], grad_normed)
    grad_after[...] = cotangent[...].astype(jnp.float32) + grad_values
    gain_grads[1:2, :] = found_gain
    branch = low(grad_after[...])
    grad_into(context[...], branch, held, 3)
    send(3)
    for copy in out_part + value_part:
        copy.wait()
    block_copy(encoded, rows_ref, sems, groups, 0).start()
    for c in range(tokens // CHUNK):
        for copy in chunk_copies(chunk_pairs, chunk_sems, c):
            copy.start()
        if c % 2 and c // 2 + 1 < segs:
            block_copy(encoded, rows_ref, sems, groups, c // 2 + 1).start()
    for copy in key_part + query_part:
        copy.start()
    grad_context[...] = low(times_back(branch, kept, 3))
    coming.wait()
    per_half = half // PAIR
    for j in range(heads // 2):
        columns = slice((j % per_half) * PAIR, (j % per_half + 1) * PAIR)
        rows = pair_rows(grad_context[:, j * PAIR : (j + 1) * PAIR])
        both = jnp.concatenate([mixed[2 * j], mixed[2 * j + 1]], axis=0)
        held[2, j // per_half, :, columns] = low(contract(both, rows, 0, 0))
        pulled = low(contract(rows, pair_weight(kept, 2, j), 1, 1))
        pulled_ref[2 * j] = pulled[:tokens]
        pulled_ref[2 * j + 1] = pulled[tokens:]
    send(2)
    leaving = pltpu.make_async_copy(pulled_ref, pulled_hbm, out_sems.at[9])
    leaving.start()
    started.append(leaving)
    count = list_chunks(starts, table)

    def two_chunks(i, carry):
        places = [2 * i, jnp.minimum(2 * i + 1, count - 1)]
        for n, place in enumerate(places):

            @pl.when((2 * i + n < count) & (table[2, place] == 1))
            def _():
                block_copy(encoded, rows_ref, sems, groups, table[1, place]).wait()

            @pl.when((2 * i + n < count) & (table[3, place] == 1))
            def _():
                for copy in chunk_copies(chunk_pairs, chunk_sems, table[0, place] >> 4):
                    copy.wait()

        found, prob_grads, blocks = [], [], []
        for place in places:
            token, s, begin, end = listed(starts, table, place)
            base = pl.multiple_of(groups[0, s] * block_rows, block_rows)
            blocks.append(rows_ref[pl.ds(base, block_rows), :])
            at = (slice(None), pl.ds(token, CHUNK), slice(None))
            inside = in_segment(token, begin, end, heads)
            found.append((at, inside))
            pulled = jnp.where(inside, pulled_ref[at], jnp.zeros((), jnp.bfloat16))
            prob_grads.append(contract(pulled.reshape(heads * CHUNK, model), blocks[-1], 1, 1))
        for (at, inside), prob_grad, rows in zip(found, prob_grads, blocks):
            wide = probs_ref[at].reshape(heads * CHUNK, block_rows).astype(jnp.float32)
            inner = jnp.sum(wide * prob_grad, axis=-1, keepdims=True)
            score_grad = low(wide * (prob_grad - inner))
            moved = low(contract(score_grad, rows, 1, 0)).reshape(heads, CHUNK, model)
            moved_ref[at] = jnp.where(inside, moved, moved_ref[at])
            score_grad = score_grad.reshape(heads, CHUNK, block_rows)
            score_out[at] = jnp.where(inside, score_grad, score_out[at])
        return carry

    lax.fori_loop(0, (count + 1) >> 1, two_chunks, 0)
    leaving = pltpu.make_async_copy(score_out, score_hbm, out_sems.at[10])
    leaving.start()
    started.append(leaving)
    for copy in key_part + query_part:
        copy.wait()
    found = []
    for j in range(heads // 2):
        columns = slice((j % per_half) * PAIR, (j % per_half + 1) * PAIR)
        both = jnp.concatenate([moved_ref[2 * j], moved_ref[2 * j + 1]], axis=0)
        found.append(low(pair_lanes(contract(both, pair_weight(kept, 1, j), 1, 0)) * 0.125))
        block = queries[:, j * PAIR : (j + 1) * PAIR] * jnp.bfloat16(0.125)
        held[1, j // per_half, :, columns] = low(contract(both, pair_rows(block), 0, 0))
    send(1)
    grad_queries = jnp.concatenate(found, axis=1)
    values = after_self[...]
    grad_into(low(normalize(values, gains[1:2, :])), grad_queries, held, 0)
    send(0)
    grad_values, grad_gain = norm_backward(values, gains[1:2, :], times_back(grad_queries, kept, 0))
    grad_self[...] = grad_after[...] + grad_values
    gain_grads[0:1, :] = grad_gain
    for copy in started:
        copy.wait()


def rows_backward_kernel(
    starts, groups, score_hbm, probs_hbm, spread_hbm, pulled_hbm, grad_rows,
    score_grads, probs_ref, spread, pulled_ref, sum_ref, row_sems, chunk_sems,
):
    heads, tokens, model = spread.shape
    segs = groups.shape[1]
    block_rows = grad_rows.shape[0] // segs

    chunk_pairs = (
        (score_hbm, score_grads), (probs_hbm, probs_ref), (spread_hbm, spread), (pulled_hbm, pulled_ref),
    )
    for c in range(tokens // CHUNK):
        for copy in chunk_copies(chunk_pairs, chunk_sems, c):
            copy.start()

    def write_out(s):
        slot = s & 1
        base = pl.multiple_of(groups[0, s] * block_rows, block_rows)
        return pltpu.make_async_copy(
            sum_ref.at[slot], grad_rows.at[pl.ds(base, block_rows)], row_sems.at[slot]
        )

    def segment(s, begin):
        end = starts[0, s + 1]
        slot = s & 1

        @pl.when(s >= 2)
        def _():
            write_out(s - 2).wait()

        def terms(c):
            @pl.when((c * CHUNK >= begin) | (begin & (CHUNK - 1) == 0))
            def _():
                for copy in chunk_copies(chunk_pairs, chunk_sems, c):
                    copy.wait()

            token = pl.multiple_of(c * CHUNK, CHUNK)
            at = (slice(None), pl.ds(token, CHUNK), slice(None))
            inside = in_segment(token, begin, end, heads)
            zero = jnp.zeros((), jnp.bfloat16)
            scores = jnp.where(inside, score_grads[at], zero).reshape(heads * CHUNK, block_rows)
            left = jnp.concatenate([scores, probs_ref[at].reshape(heads * CHUNK, block_rows)], axis=0)
            right = jnp.concatenate(
                [jnp.where(inside, piece[at], zero).reshape(heads * CHUNK, model) for piece in (spread, pulled_ref)],
                axis=0,
            )
            return contract(left, right, 0, 0)

        def chunk(c, carry):
            sum_ref[slot] += terms(c)
            return carry

        first = begin >> 4
        sum_ref[slot] = terms(first)
        lax.fori_loop(first + 1, (end + CHUNK - 1) >> 4, chunk, 0)
        write_out(s).start()
        return end

    lax.fori_loop(0, segs, segment, 0)
    for s in range(segs - 2, segs):
        write_out(s).wait()


def gelu_both(values):
    scale = 0.7978845608028654
    square = values * values
    bend = jnp.tanh(scale * (values + 0.044715 * (square * values)))
    half = 0.5 * (1.0 + bend)
    slope = half + 0.5 * values * (1.0 - bend * bend) * (scale * (1.0 + 3.0 * 0.044715 * square))
    return values * half, slope


def ffn_kernel(
    direct,
    me_ref, normed, normed_theirs, cotangent, cotangent_theirs, *refs,
):
    sources, refs = (refs[:8], refs[8:]) if direct else (refs[:2], refs[2:])
    out_mine, out_other, pull_mine, pull_other, grad_mine, grad_other = refs[:6]
    kept_in, kept_down, held_in, held_down, sems, out_sems = refs[6:]
    core = me_ref[0] & 1
    x_bit = (me_ref[0] >> 2) & 1
    blocks, groups, unused, width = held_in.shape
    model = held_in.shape[1] * held_in.shape[2]
    count = normed.shape[0]
    if direct:
        copies = []
        for n, source in enumerate(sources):
            place = core if n < 4 else 1 - core
            at = x_bit ^ (n >> 1 & 1)
            lead = (slice(None),) * (len(source.shape) - 2)
            target = kept_in.at[(place,) + lead + (at,)] if n % 2 == 0 else kept_down.at[lead + (at, place)]
            copies.append(pltpu.make_async_copy(source, target, sems.at[n]))
    else:
        copies = [
            pltpu.make_async_copy(source, target, sems.at[n])
            for n, (source, target) in enumerate(zip(sources, (kept_in, kept_down)))
        ]
    for copy in copies:
        copy.start()
    tokens = jnp.concatenate([normed[...], normed_theirs[...]], axis=0)
    pull = jnp.concatenate([cotangent[...], cotangent_theirs[...]], axis=0)
    for copy in copies:
        copy.wait()
    total = grad_tokens = None
    started = []
    for b in range(blocks):
        weight_up = kept_in[b].reshape(model, width)
        part = slice(b * groups // blocks, (b + 1) * groups // blocks) if direct else slice(0, 1)
        if direct:
            weight_down = kept_down[b].reshape(width, model)
        else:
            weight_down = kept_down[0, 0, b * width : (b + 1) * width]
        activated, slope = gelu_both(contract(tokens, weight_up, 1, 0))
        activated = low(activated)
        grad_act = low(contract(pull, weight_down, 1, 1)).astype(jnp.float32)
        grad_pre = low(slope * grad_act)
        added = contract(grad_pre, weight_up, 1, 1)
        grad_tokens = added if b == 0 else grad_tokens + added
        added = contract(activated, weight_down, 1, 0)
        total = added if b == 0 else total + added
        held_in[b] = low(contract(tokens, grad_pre, 0, 0)).reshape(held_in.shape[1:])
        grad_down = low(contract(activated, pull, 0, 0))
        if direct:
            held_down[part] = grad_down.reshape((groups // blocks,) + held_down.shape[1:])
        else:
            held_down[0, 0, b * width : (b + 1) * width] = grad_down
    if direct:
        rows = held_down.shape[2]
        targets = (
            (held_in.at[1 - core], grad_other.at[:, :rows]),
            (held_down.at[:, 1 - core], grad_other.at[:, rows:]),
            (held_in.at[core], grad_mine.at[:, :rows]),
            (held_down.at[:, core], grad_mine.at[:, rows:]),
        )
    else:
        targets = ((held_in, grad_mine), (held_down, grad_other))
    started = [pltpu.make_async_copy(source, target, out_sems.at[n]) for n, (source, target) in enumerate(targets)]
    for copy in started:
        copy.start()
    out_mine[...] = total[:count]
    out_other[...] = low(total[count:])
    pull_mine[...] = grad_tokens[:count]
    pull_other[...] = low(grad_tokens[count:])
    for copy in started:
        copy.wait()

VMEM = pl.BlockSpec(memory_space=pltpu.VMEM)
SMEM = pl.BlockSpec(memory_space=pltpu.SMEM)
HBM = pl.BlockSpec(memory_space=pltpu.HBM)
ANY = pl.BlockSpec(memory_space=pl.ANY)


def shaped(shape, dtype):
    return jax.ShapeDtypeStruct(shape, dtype)


def call(kernel, name, flops, in_specs, out_specs, out_shape, scratch, aliases={}, room=VMEM_BYTES):
    return pl.pallas_call(
        kernel,
        out_shape=out_shape,
        in_specs=in_specs,
        out_specs=out_specs,
        scratch_shapes=scratch,
        compiler_params=pltpu.CompilerParams(vmem_limit_bytes=room),
        cost_estimate=pl.CostEstimate(flops=flops, bytes_accessed=1_000_000, transcendentals=0),
        name=name,
        input_output_aliases=aliases,
    )


AXES = ("dp", "fsdp")


def swap_with(piece, mask, devices):
    pairs = [(index, index ^ mask) for index in range(devices)]
    return lax.ppermute(piece, AXES, pairs)


def bit_of(me, bit):
    return (me >> bit) & 1


def pair_up(mine, theirs, my_bit, axis):
    first = jnp.where(my_bit == 0, mine, theirs)
    second = jnp.where(my_bit == 0, theirs, mine)
    return jnp.stack([first, second], axis=axis)


def arranged(found, bits, me):
    found = {mask: [block] for mask, block in found.items()}
    for n, bit in enumerate(sorted(bits)):
        low_side = bit_of(me, bit) == 0
        merged = {}
        for mask in found:
            if not mask >> n & 1:
                both = list(zip(found[mask], found[mask | 1 << n]))
                merged[mask] = [jnp.where(low_side, x, y) for x, y in both] + [
                    jnp.where(low_side, y, x) for x, y in both
                ]
        found = merged
    return jnp.stack(found[0])


def wide_mask(mask, bits):
    return sum(1 << bit for n, bit in enumerate(sorted(bits)) if mask >> n & 1)


def exchange(send, bits, me, devices):
    found = {0: send(0)}
    for mask in range(1, 1 << len(bits)):
        found[mask] = swap_with(send(mask), wide_mask(mask, bits), devices)
    return arranged(found, bits, me)


def gather_line(block, bits, me, devices):
    if len(bits) > 2:
        held = block[None]
        for bit in sorted(bits):
            theirs = swap_with(held, 1 << bit, devices)
            held = pair_up(held, theirs, bit_of(me, bit), 0).reshape((-1,) + block.shape)
        return held
    return exchange(lambda mask: block, bits, me, devices)


def taken(source, places, columns):
    array, bits, offset = source
    begin = [places[bit] if bit in places else 0 for bit in bits] + [0, offset + columns[0]]
    size = [1 if bit in places else 2 for bit in bits] + [array.shape[-2], columns[1] - columns[0]]
    part = lax.dynamic_slice(array, begin, size)
    return part.reshape([2 for bit in bits if bit not in places] + size[-2:])


def summed(entry, places):
    sources, columns = entry
    total = None
    for source in sources:
        part = taken(source, places, columns).astype(jnp.float32)
        total = part if total is None else total + part
    return total


def with_brought(entry, theirs, bit, done):
    sources, columns = entry
    bits = [other for other in sources[0][1] if other not in done and other != bit]
    return (sources + [(theirs, bits, -columns[0])], columns)


def sends_of(entries, bit, done, me):
    places = {other: bit_of(me, other) for other in done}
    send = [low(summed(entry, {**places, bit: 1 - bit_of(me, bit)})) for entry in entries]
    send = jnp.concatenate(send, axis=-1)
    return with_layout_constraint(send, Layout(tuple(range(send.ndim))))


def sum_over(entries, bit, done, me, devices, send=None):
    theirs = swap_with(sends_of(entries, bit, done, me) if send is None else send, 1 << bit, devices)
    found, at = [], 0
    for sources, columns in entries:
        bits = [other for other in sources[0][1] if other not in done and other != bit]
        found.append((sources + [(theirs, bits, at - columns[0])], columns))
        at += columns[1] - columns[0]
    return found


def combine(me_word, outputs):
    arrays, buffers, plan, shapes = [], {}, [], []
    for pieces, dtype in outputs:
        at, steps = 0, []
        for (sources, columns), flips, late in pieces:
            keys = []
            for array, bits, offset in sources:
                number = next((n for n, other in enumerate(arrays) if other is array), len(arrays))
                if number == len(arrays):
                    arrays.append(array)
                picked = tuple(flips.get(bit) for bit in bits)
                key = (number, tuple(bits), picked, offset + columns[0], columns[1] - columns[0])
                buffers.setdefault(key, len(buffers))
                keys.append(key)
            steps.append((at, keys, late))
            at += columns[1] - columns[0]
        sources = pieces[0][0][0]
        left = [bit for bit in sources[0][1] if bit not in pieces[0][1] and bit not in pieces[0][2]]
        plan.append(steps)
        shapes.append(shaped((2,) * len(left) + (sources[0][0].shape[-2], at), dtype))

    def kernel(me_ref, *refs):
        inputs, targets = refs[: len(arrays)], refs[len(arrays) : len(arrays) + len(outputs)]
        held, sems = refs[len(arrays) + len(outputs) : -1], refs[-1]
        me = me_ref[0]
        copies = {}
        for key, n in buffers.items():
            number, bits, picked, begin, width = key
            index = tuple(
                slice(None) if flip is None else ((me >> bit) & 1) ^ flip for bit, flip in zip(bits, picked)
            )
            copies[key] = pltpu.make_async_copy(
                inputs[number].at[index + (slice(None), slice(begin, begin + width))], held[n], sems.at[n]
            )
            copies[key].start()
        waited = set()
        for target, steps in zip(targets, plan):
            for at, keys, late in steps:
                total = None
                for key in keys:
                    if key not in waited:
                        copies[key].wait()
                        waited.add(key)
                    left = [bit for bit, flip in zip(key[1], key[2]) if flip is None]
                    index = tuple(((me >> bit) & 1) ^ late[bit] if bit in late else slice(None) for bit in left)
                    part = held[buffers[key]][index].astype(jnp.float32)
                    total = part if total is None else total + part
                target[..., at : at + keys[0][4]] = total.astype(target.dtype)

    scratch = []
    for number, bits, picked, begin, width in buffers:
        lead = tuple(2 for flip in picked if flip is None)
        scratch.append(pltpu.VMEM(lead + (arrays[number].shape[-2], width), arrays[number].dtype))
    scratch.append(pltpu.SemaphoreType.DMA((len(buffers),)))
    found = call(
        kernel, "combine", 1_000_000, [SMEM] + [ANY] * len(arrays), [VMEM] * len(outputs), tuple(shapes), scratch
    )(me_word, *arrays)
    return list(found)


def line_blocks(me_word, entries, bits, done, devices):
    flips = {bit: 0 for bit in done}
    if len(bits) > 2:
        for bit in sorted(bits):
            entries = sum_over(entries, bit, list(flips), me_word[0], devices)
            flips[bit] = 0
        return combine(me_word, [([(entry, flips, {}) for entry in entries], jnp.float32)])
    outputs = []
    for mask in range(1 << len(bits)):
        wide = wide_mask(mask, bits)
        pieces = [(entry, flips, {bit: wide >> bit & 1 for bit in bits}) for entry in entries]
        outputs.append((pieces, jnp.bfloat16 if mask else jnp.float32))
    return combine(me_word, outputs)


def brought_blocks(blocks, bits, devices):
    return blocks[:1] + [
        swap_with(block, wide_mask(mask + 1, bits), devices) for mask, block in enumerate(blocks[1:])
    ]


def core_rows(total, core, devices):
    rows = total.shape[0] // 2
    keep = lax.dynamic_slice_in_dim(total, core * rows, rows, axis=0)
    send = lax.dynamic_slice_in_dim(total, (1 - core) * rows, rows, axis=0)
    theirs = swap_with(send, 1, devices)
    return jnp.where(core == 0, keep, theirs), jnp.where(core == 0, theirs, keep)


def per_device(
    fsdp,
    devices,
    tokens,
    encoded,
    segment_ids,
    passage_group,
    cotangent,
    self_gain,
    cross_gain,
    ffn_gain,
    self_query,
    self_key,
    self_value,
    self_out,
    cross_query,
    cross_key,
    cross_value,
    cross_out,
    ffn_in,
    ffn_out,
):
    me = lax.axis_index("dp") * fsdp + lax.axis_index("fsdp")
    core = bit_of(me, 0)
    core_word = core.reshape(1).astype(jnp.int32)
    me_word = me.reshape(1).astype(jnp.int32)
    bounds = lax.broadcasted_iota(jnp.int32, (1, passage_group.shape[1] + 1), 1)
    starts = jnp.sum((segment_ids[0, :, None] < bounds).astype(jnp.int32), axis=0, keepdims=True)
    chip_bits = list(range(1, devices.bit_length() - 1))
    line_bits = [bit for bit in reversed(chip_bits) if bit > 2]
    pair_orders = ([2, 1], [1, 2])
    count, model = tokens.shape
    encoder_count = encoded.shape[0]
    hidden_units = ffn_in.shape[1]
    heads = model // HEAD
    half = model // 2
    segs = passage_group.shape[1]
    low_type, wide_type = jnp.bfloat16, jnp.float32

    def my_columns(matrix, owner):
        width = matrix.shape[-1] // 2
        return lax.dynamic_slice_in_dim(matrix, owner * width, width, axis=matrix.ndim - 1)

    barrier = lax.optimization_barrier
    gains = jnp.stack([self_gain, cross_gain, ffn_gain], axis=1)
    gains = jnp.pad(gains, ((0, 0), (0, PAIR - 3)))
    shards = [self_query, self_key, self_value, self_out, cross_query, cross_key, cross_value, cross_out]
    rows_in = ffn_in.shape[0]
    rows_down = ffn_out.shape[0]
    direct = rows_down % 16 == 0
    chip_groups = devices // 4
    group_bits = [0, 1]
    packed = shaped((rows_in, len(shards) * half + PAIR + 2 * model), low_type)
    send, keep = call(
        pack_kernel, "pack", 0, [SMEM] + [VMEM] * 10, [VMEM] * 2, (packed, packed), []
    )(core_word, *shards, gains, ffn_in)
    theirs = swap_with(send, 1, devices)
    chip_block = pair_up(keep, theirs, core, 0).reshape(-1, keep.shape[1])
    self_block = jnp.concatenate([chip_block[:, : 2 * model], chip_block[:, 4 * model : 4 * model + PAIR]], axis=1)
    in_halves = chip_block[:, 4 * model + PAIR :].reshape(2 * rows_in, chip_groups // 2, 2, 2 * rows_down)
    in_halves = in_halves.swapaxes(1, 2).reshape(2 * rows_in, 2 * model)
    cross_block = chip_block[:, 2 * model : 4 * model]

    def double(held, bit, first_bit, me):
        place = 1 if first_bit is None or bit > first_bit else 2
        return pair_up(held, swap_with(held, 1 << bit, devices), bit_of(me, bit), place)

    def first_step(line, width):
        return [double(part, order[0], None, me) for part, order in zip((line[:, :, :width], line[:, :, width:]), pair_orders)]

    def second_step(parts):
        return [
            double(part, order[1], order[0], me).reshape(-1, part.shape[-1])
            for part, order in zip(parts, pair_orders)
        ]

    cotangent_theirs = swap_with(cotangent, 2, devices)

    def block_for(array, mask):
        first = [bit_of(me, 1) ^ (mask >> 1 & 1), core ^ (mask & 1)]
        return lax.dynamic_slice(array, first + [0, 0], (1, 1) + array.shape[2:]).reshape(array.shape[2:])

    ffn_steps = line_bits + [2]

    def merged(held, theirs, steps, number):
        bit = steps[number]
        place = sum(1 for other in steps[:number] if other > bit)
        return pair_up(held, theirs, bit_of(me, bit), place)

    def brought(held, steps, number):
        return swap_with(held, 1 << steps[number], devices)

    def half_at(array, place):
        return lax.dynamic_slice_in_dim(array, place * model, model, axis=1)

    self_line = gather_line(self_block, line_bits, me, devices)
    self_line, cross_held, in_halves, cotangent_theirs, down_held = barrier(
        (self_line, cross_block, in_halves, cotangent_theirs, ffn_out)
    )
    y_bit = bit_of(me, 1)
    in_theirs = swap_with(half_at(in_halves, 1 - y_bit), 2, devices)
    last = len(line_bits) - 1
    self_parts = first_step(self_line, model)
    for number in range(last):
        cross_held = merged(cross_held, brought(cross_held, line_bits, number), line_bits, number)
        down_held = merged(down_held, brought(down_held, ffn_steps, number), ffn_steps, number)
    self_parts, cross_held, in_theirs, down_held = barrier((self_parts, cross_held, in_theirs, down_held))
    in_held = pair_up(half_at(in_halves, y_bit), in_theirs, y_bit, 0).reshape(4 * rows_in, model)
    self_theirs = [brought(part, [2, 1, 2], n + 1) for n, part in enumerate(self_parts)]
    cross_line = merged(cross_held, brought(cross_held, line_bits, last), line_bits, last)
    cross_line = cross_line.reshape((-1,) + cross_block.shape)
    for number in range(last):
        in_held = merged(in_held, brought(in_held, ffn_steps, number), ffn_steps, number)
    down_theirs = brought(down_held, ffn_steps, last)
    cross_line, in_held, down_theirs, self_theirs = barrier((cross_line, in_held, down_theirs, self_theirs))
    cross_parts = first_step(cross_line, model)
    cross_parts = [with_layout_constraint(part, Layout(tuple(range(part.ndim)))) for part in cross_parts]
    in_theirs = brought(in_held, ffn_steps, last)
    cross_parts, in_theirs = barrier((cross_parts, in_theirs))
    in_held = merged(in_held, in_theirs, ffn_steps, last)
    down_held = merged(down_held, down_theirs, ffn_steps, last)
    in_held, down_held = (
        with_layout_constraint(held, Layout(tuple(range(held.ndim)))) for held in (in_held, down_held)
    )

    def second_merge(parts, theirs):
        return [
            pair_up(part, other, bit_of(me, order[1]), 1 if order[1] > order[0] else 2).reshape(-1, part.shape[-1])
            for part, other, order in zip(parts, theirs, pair_orders)
        ]

    self_mine = second_merge(self_parts, self_theirs)
    cross_theirs = [brought(part, [2, 1, 2], n + 1) for n, part in enumerate(cross_parts)]
    self_weights = [(mine, swap_with(mine[:, :model], 1, devices)) for mine in self_mine]

    gain_rows = self_weights[1][0][:, model : model + 8].T.astype(wide_type)
    self_flat = self_weights[0] + self_weights[1]

    dma = pltpu.SemaphoreType.DMA
    weights_kept = pltpu.VMEM((4, 2, model, half), low_type)
    projected, context_one, after_self = call(
        self_forward_kernel,
        "self_forward",
        2 * count * model * model * 5,
        [SMEM, VMEM, VMEM, VMEM] + [ANY] * 4,
        [VMEM] * 3,
        (
            shaped((3, count, model), low_type),
            shaped((count, model), low_type),
            shaped((count, model), wide_type),
        ),
        [weights_kept, dma((8,))],
        room=MIDDLE_BYTES,
    )(core_word, segment_ids, tokens, gain_rows, *self_flat)

    cross_direct = 2 * rows_in % 16 == 0
    cross_sibling = [swap_with(part, 1, devices) for part in cross_parts]
    cross_theirs, cross_sibling, in_held, down_held, after_self = barrier(
        (cross_theirs, cross_sibling, in_held, down_held, after_self)
    )
    in_theirs, down_theirs = swap_with(in_held, 4, devices), swap_with(down_held, 4, devices)
    in_sibling, down_sibling = swap_with(in_held, 1, devices), swap_with(down_held, 1, devices)
    sibling_theirs = [swap_with(theirs, 1, devices) for theirs in cross_theirs]
    if cross_direct:
        cross_weights = list(zip(cross_parts, cross_theirs, cross_sibling, sibling_theirs))
        cross_rows = cross_parts[0].shape[:1] + (2, 2, 2 * rows_in, half)
    else:
        cross_weights = list(
            zip(second_merge(cross_parts, cross_theirs), second_merge(cross_sibling, sibling_theirs))
        )
        cross_rows = (model, half)
    pieces = len(cross_weights[0])
    cross_flat = list(cross_weights[0]) + list(cross_weights[1])
    cross_kept = pltpu.VMEM((4, 2) + cross_rows, low_type)

    per_token = (heads, count, model)
    probs_shape = (heads, count, encoder_count // segs)
    probs_kept, tokens_kept = pltpu.VMEM(probs_shape, low_type), pltpu.VMEM(per_token, low_type)
    chunk_count = count // CHUNK
    chunk_table = pltpu.SMEM((4, chunk_count + segs), jnp.int32)
    queries_two, context_two, after_cross, normed_three, probs, mixed, spread = call(
        functools.partial(cross_forward_kernel, pieces),
        "cross_forward",
        12_000_000_000,
        [SMEM, SMEM, SMEM, VMEM, VMEM] + [HBM] * (1 + 2 * pieces),
        [VMEM] * 4 + [HBM] * 3,
        (
            shaped((count, model), low_type),
            shaped((count, model), low_type),
            shaped((count, model), wide_type),
            shaped((count, model), low_type),
            shaped(probs_shape, low_type),
            shaped(per_token, low_type),
            shaped(per_token, low_type),
        ),
        [
            probs_kept, tokens_kept, tokens_kept, pltpu.VMEM(encoded.shape, low_type), cross_kept,
            chunk_table, dma((segs,)), dma((4 * pieces,)), dma((3,)),
        ],
    )(me_word, starts, passage_group, after_self, gain_rows, encoded, *cross_flat)

    normed_theirs = swap_with(normed_three, 2, devices)
    in_theirs, down_theirs, in_sibling, down_sibling, normed_theirs = barrier(
        (in_theirs, down_theirs, in_sibling, down_sibling, normed_theirs)
    )
    in_fourth, down_fourth = swap_with(in_theirs, 1, devices), swap_with(down_theirs, 1, devices)
    ffn_pieces = [in_held, down_held, in_theirs, down_theirs, in_sibling, down_sibling, in_fourth, down_fourth]
    half_units = hidden_units // 2
    high = (2,) * (len(chip_bits) - 1)
    if direct:
        in_shape = (2, chip_groups, rows_down, model)
        down_shape = (chip_groups, 2, rows_down, model)
        ffn_weights = ffn_pieces
        grad_shapes = (shaped((chip_groups, 2 * rows_down, model), low_type),) * 2
    else:
        in_shape, down_shape = (2, 1, model, model), (1, 1, half_units, model)
        ffn_mine = [
            pair_up(held, theirs, bit_of(me, 2), len(line_bits)).reshape((chip_groups,) + held.shape[-2:])
            for held, theirs in ((in_held, in_theirs), (down_held, down_theirs))
        ]
        ffn_sibling = [
            pair_up(held, theirs, bit_of(me, 2), len(line_bits)).reshape((chip_groups,) + held.shape[-2:])
            for held, theirs in ((in_sibling, in_fourth), (down_sibling, down_fourth))
        ]
        ffn_weights = (
            pair_up(ffn_mine[0], ffn_sibling[0], core, 0).reshape(in_shape),
            pair_up(ffn_mine[1], ffn_sibling[1], core, 1).reshape(down_shape),
        )
        grad_shapes = (shaped(in_shape, low_type), shaped(down_shape, low_type))
    token_shapes = (shaped((count, model), wide_type), shaped((count, model), low_type))
    out_mine, out_other, pull_mine, pull_other, ffn_grad, ffn_other = call(
        functools.partial(ffn_kernel, direct),
        "ffn",
        4_000_000_000,
        [SMEM] + [VMEM] * 4 + [HBM] * len(ffn_weights),
        [VMEM] * 4 + [HBM] * 2,
        token_shapes + token_shapes + grad_shapes,
        [
            pltpu.VMEM((2,) + high + in_shape[2:] if direct else in_shape, low_type),
            pltpu.VMEM(high + down_shape[1:] if direct else down_shape, low_type),
            pltpu.VMEM(in_shape, low_type),
            pltpu.VMEM(down_shape, low_type),
            dma((8,)),
            dma((4,)),
        ],
    )(me_word, normed_three, normed_theirs, cotangent, cotangent_theirs, *ffn_weights)
    pull_theirs = swap_with(pull_other, 2, devices)
    if not direct:
        in_parts = ffn_grad.reshape(2, chip_groups, 4 * rows_in, model)
        down_parts = ffn_other.reshape(chip_groups, 2, rows_down, model).swapaxes(0, 1)
        both = jnp.concatenate([in_parts, down_parts], axis=2)
        ffn_grad, ffn_other = (
            lax.dynamic_index_in_dim(both, place, 0, keepdims=False) for place in (core, 1 - core)
        )
    ffn_theirs = swap_with(ffn_other, 1, devices)
    high_bits = [bit for bit in sorted(chip_bits, reverse=True) if bit > 1]

    def group_source(array):
        return (array.reshape((2,) * len(high_bits) + array.shape[-2:]), high_bits, 0)

    ffn_entry = ([group_source(ffn_grad), group_source(ffn_theirs)], (0, model))
    ffn_send = low(summed(ffn_entry, {2: 1 - bit_of(me, 2)}))
    pull_theirs, ffn_send = barrier((pull_theirs, ffn_send))
    ffn_sum = [with_brought(ffn_entry, swap_with(ffn_send, 4, devices), 2, [])]

    all_bits = sorted(chip_bits, reverse=True)

    def chips_of(array):
        return array.reshape((2,) * len(all_bits) + (array.shape[0] >> len(all_bits), array.shape[-1]))

    def entry_of(mine, theirs, begin, end):
        return ([(chips_of(mine), all_bits, 0), (chips_of(theirs), all_bits, 0)], (begin, end))

    def first_sum(sides):
        return [sum_over(entries, order[0], [], me, devices) for entries, order in zip(sides, pair_orders)]

    def second_sum(sides):
        return [sum_over(entries, order[1], order[:1], me, devices) for entries, order in zip(sides, pair_orders)]

    def received(sides):
        return [entries[0][0][-1][0] for entries in sides]

    def with_received(sides, arrays):
        return [
            [(sources[:-1] + [(array,) + sources[-1][1:]], columns) for sources, columns in entries]
            for entries, array in zip(sides, arrays)
        ]

    grads_shape = shaped((model, 2 * model), low_type)
    rows_kept = pltpu.VMEM(encoded.shape, low_type)
    grad_after_self, gain_grads, score_grads, pulled, cross_mine_grad, cross_other_grad = call(
        functools.partial(cross_backward_kernel, pieces),
        "cross_backward",
        4_000_000_000,
        [SMEM, SMEM, SMEM] + [VMEM] * 8 + [HBM] * (3 + 2 * pieces),
        [VMEM] * 2 + [HBM] * 4,
        (
            shaped((count, model), wide_type),
            shaped((8, model), wide_type),
            shaped(probs_shape, low_type),
            shaped(per_token, low_type),
            grads_shape,
            grads_shape,
        ),
        [
            pltpu.VMEM((count, model), wide_type), pltpu.VMEM((count, model), low_type), tokens_kept, probs_kept,
            tokens_kept, probs_kept, rows_kept, tokens_kept, cross_kept, weights_kept,
            chunk_table, dma((segs,)), dma((4 * pieces,)), dma((11,)), dma((1, chunk_count)),
        ],
    )(
        me_word, starts, passage_group, after_cross, after_self, gain_rows, cotangent, pull_mine, pull_theirs,
        queries_two, context_two, mixed, encoded, probs, *cross_flat,
    )
    arrays, grad_after_self, cross_mine_grad, cross_other_grad = barrier(
        (received([ffn_sum]), grad_after_self, cross_mine_grad, cross_other_grad)
    )
    ffn_sum = with_received([ffn_sum], arrays)[0]
    ffn_done = [2]
    for bit in sorted(line_bits)[:-1]:
        ffn_sum = sum_over(ffn_sum, bit, ffn_done, me, devices)
        ffn_done = ffn_done + [bit]
    cross_theirs_grad = swap_with(cross_other_grad, 1, devices)

    with_gains = shaped((model, 2 * model + PAIR), low_type)
    tokens_grad, self_mine, self_other = call(
        self_backward_kernel,
        "self_backward",
        2 * count * model * model * 10,
        [SMEM] + [VMEM] * 7 + [ANY] * 4,
        [VMEM] + [HBM] * 2,
        (shaped((count, model), wide_type), with_gains, with_gains),
        [weights_kept, weights_kept, pltpu.VMEM((model, PAIR), low_type), dma((8,)), dma((10,))],
        room=MIDDLE_BYTES,
    )(
        core_word, segment_ids, tokens, gain_rows, grad_after_self, gain_grads, projected, context_one,
        *self_flat,
    )
    arrays, cross_theirs_grad, self_mine, self_other = barrier(
        (received([ffn_sum]), cross_theirs_grad, self_mine, self_other)
    )
    ffn_sum = with_received([ffn_sum], arrays)[0]
    ffn_sum = sum_over(ffn_sum, max(line_bits), ffn_done, me, devices)
    self_theirs = swap_with(self_other, 1, devices)
    crossed = [
        [entry_of(cross_mine_grad, cross_theirs_grad, *cut)] for cut in ((0, model), (model, 2 * model))
    ]
    crossed = first_sum(crossed)
    self_theirs, score_grads = barrier((self_theirs, score_grads))
    attention = [
        [entry_of(self_mine, self_theirs, *cut)] for cut in ((0, model), (model, 2 * model + PAIR))
    ]
    attention = first_sum(attention)
    encoded_grad = call(
        rows_backward_kernel,
        "rows_backward",
        3_000_000_000,
        [SMEM, SMEM] + [HBM] * 4,
        HBM,
        shaped(encoded.shape, wide_type),
        [
            probs_kept, probs_kept, tokens_kept, tokens_kept,
            pltpu.VMEM((2, encoder_count // segs, model), wide_type), dma((2,)), dma((4, chunk_count)),
        ],
    )(starts, passage_group, score_grads, probs, spread, pulled)
    crossed_arrays, arrays, ffn_arrays, encoded_grad = barrier(
        (received(crossed), received(attention), received([ffn_sum]), encoded_grad)
    )
    ffn_sum = with_received([ffn_sum], ffn_arrays)[0]
    ffn_rows = summed(ffn_sum[0], {bit: bit_of(me, bit) for bit in high_bits})
    summed_down = ffn_rows[4 * rows_in :]
    in_parts = ffn_rows[: 4 * rows_in].reshape(2, 2, rows_in, model)
    in_parts = exchange(lambda mask: block_for(in_parts, mask), group_bits, me, devices)
    in_parts = in_parts.reshape(2, 2, rows_in, chip_groups // 2, 2 * rows_down)
    summed_in = in_parts.transpose(2, 1, 3, 0, 4).reshape(rows_in, hidden_units)
    crossed, attention = with_received(crossed, crossed_arrays), with_received(attention, arrays)
    groups = [(entries, order[1], order[:1]) for entries, order in zip(crossed, pair_orders)]
    sends = [sends_of(*group, me) for group in groups]
    sends, arrays = barrier((sends, received(attention)))
    crossed = [sum_over(*group, me, devices, send) for group, send in zip(groups, sends)]
    attention = second_sum(with_received(attention, arrays))
    cross_blocks = line_blocks(me_word, crossed[0] + crossed[1], line_bits, [2, 1], devices)
    unused_blocks, arrays = barrier((cross_blocks, received(attention)))
    attention = with_received(attention, arrays)
    cross_terms = brought_blocks(cross_blocks, line_bits, devices)
    self_blocks = line_blocks(me_word, attention[0] + attention[1], line_bits, [2, 1], devices)
    self_terms = brought_blocks(self_blocks, line_bits, devices)
    unused_blocks, out_other = barrier((cross_blocks, out_other))
    out_theirs = swap_with(out_other, 2, devices)
    self_terms, summed_in, out_theirs = barrier((self_terms, summed_in, out_theirs))
    block_out = low(after_cross + (out_mine + out_theirs.astype(wide_type)))

    def spread_out(terms, matrices, gains):
        found = terms[0]
        for term in terms[1:]:
            found = found + term.astype(wide_type)
        keep = lax.dynamic_slice_in_dim(found, core * rows_in, rows_in, axis=0)
        send = lax.dynamic_slice_in_dim(found, (1 - core) * rows_in, rows_in, axis=0)
        shapes = (shaped((rows_in, model), wide_type),) * matrices
        if gains:
            shapes += (shaped((rows_in, PAIR), wide_type),)
        return call(
            functools.partial(spread_kernel, matrices),
            "spread",
            1_000_000,
            [SMEM, VMEM, VMEM],
            [VMEM] * len(shapes),
            shapes,
            [],
            room=SMALL_BYTES,
        )(core_word, keep, swap_with(send, 1, devices))

    summed_cv, summed_cq, summed_co, summed_ck = spread_out(cross_terms, 4, False)
    summed_query, summed_key, summed_value, summed_out, own_gains = spread_out(self_terms, 4, True)
    return (
        block_out,
        tokens_grad,
        encoded_grad,
        own_gains[:, 0],
        own_gains[:, 1],
        own_gains[:, 2],
        summed_query,
        summed_key,
        summed_value,
        summed_out,
        summed_cq,
        summed_ck,
        summed_cv,
        summed_co,
        summed_in,
        summed_down,
    )


def solution(mesh):
    return jax.shard_map(
        functools.partial(per_device, mesh.shape["fsdp"], mesh.size),
        mesh=mesh,
        in_specs=(
            P(("dp", "fsdp"), None),
            P(("dp", "fsdp"), None),
            P(("dp", "fsdp"), None),
            P(("dp", "fsdp"), None),
            P(("dp", "fsdp"), None),
            P(("dp", "fsdp")),
            P(("dp", "fsdp")),
            P(("dp", "fsdp")),
            P(("dp", "fsdp"), None),
            P(("dp", "fsdp"), None),
            P(("dp", "fsdp"), None),
            P(("dp", "fsdp"), None),
            P(("dp", "fsdp"), None),
            P(("dp", "fsdp"), None),
            P(("dp", "fsdp"), None),
            P(("dp", "fsdp"), None),
            P(("dp", "fsdp"), None),
            P(("dp", "fsdp"), None),
        ),
        out_specs=(
            P(("dp", "fsdp"), None),
            P(("dp", "fsdp"), None),
            P(("dp", "fsdp"), None),
            P(("dp", "fsdp")),
            P(("dp", "fsdp")),
            P(("dp", "fsdp")),
            P(("dp", "fsdp"), None),
            P(("dp", "fsdp"), None),
            P(("dp", "fsdp"), None),
            P(("dp", "fsdp"), None),
            P(("dp", "fsdp"), None),
            P(("dp", "fsdp"), None),
            P(("dp", "fsdp"), None),
            P(("dp", "fsdp"), None),
            P(("dp", "fsdp"), None),
            P(("dp", "fsdp"), None),
        ),
        check_vma=False,
    )
```
